256 devices in a mesh: row: 32 (over x, y, z_lo), ma: 8 (over z_hi, core).
Axes of the slice: x: 4, y: 4, z: 8 (z_hi: 4, z_lo: 2; z = z_hi * 2 + z_lo), core: 2. Of those that a mesh axis runs over, the one named last changes fastest.
Arguments:
- coeffs: bfloat16 [64, 12, 136, 4096], P('row', None, 'ma'), may hold values from -6 to 6
- legendre: bfloat16 [136, 64, 2048], P('ma'), may hold values from -0.1875 to 0.1875
- lat_weights: float32 [32], replicated, may hold values from 4 to 16
- m_blocks: int32 [16], replicated, may hold values from 0 to 15, as said below
Outputs:
- nonlinear: bfloat16 [64, 8, 136, 4096], P('row', None, 'ma')
- radial_slope: bfloat16 [64, 8, 136, 4096], P('row', None, 'ma')
The draws below stay inside these ranges and needn't reach their ends.
Inputs may be any that keep to these rules, and one draw needn't show every extreme that they name: `m_blocks`: each of the 16 order blocks appears once; entries 2p and 2p + 1 always sum to 15.
All inputs are finite; a program needn't handle non-finite values.
Results may differ from the reference program's by a relative error of at most 0.017.
Values may be sent and summed in bfloat16 or wider, within the bound.
No kernel may reach another device: no remote copies, remote signals or barrier semaphores. Data moves between devices by JAX's collectives and lax.ppermute only.
A program may use at most 128 MiB of HBM per device.

```python
import math
import jax
import jax.numpy as jnp
from jax import lax

DEGREES = 1024
PHI_POINTS = 3072
BLOCK = 64
LATS = 32
MBLOCKS = 16
SLOTS = 136
SHELLS = 64


def draw_m_blocks(key, part):
    key = jax.random.fold_in(key, 11)
    half_count = MBLOCKS // 2
    pair_order = jax.random.permutation(jax.random.fold_in(key, 1), half_count).astype(jnp.int32)
    flipped = jax.random.randint(jax.random.fold_in(key, 2), (half_count,), 0, 2)
    leading = jnp.where(flipped == 1, pair_order, MBLOCKS - 1 - pair_order)
    second = MBLOCKS - 1 - leading
    return jnp.stack([leading, second], axis=1).reshape(MBLOCKS).astype(jnp.int32)


def levels(rng, shape, shards, least, high):
    loudness, own = 1.0, jax.random.fold_in(rng, 6)
    for dim, blocks in shards:
        heights = jnp.exp(jax.random.uniform(jax.random.fold_in(own, dim), (blocks,), jnp.float32, least / len(shards), high / len(shards)))
        loudness = loudness * jnp.repeat(heights, shape[dim] // blocks).reshape([-1 if axis == dim else 1 for axis in range(len(shape))])
    return loudness


def noise(stream_key, shape, scale, bound, pieces=(), held_as=jnp.bfloat16):
    level = levels(stream_key, shape, pieces, -0.22, 0.18) if pieces else 1.0
    drawn = jax.random.normal(stream_key, shape, jnp.float32) * scale * level
    return jnp.minimum(jnp.maximum(drawn, -bound), bound).astype(held_as)


def setup_inputs(seed: int = 0) -> dict:
    key_list = jax.random.split(jax.random.key(seed), 5)
    coeffs = noise(key_list[0], (SHELLS, 12, SLOTS, BLOCK * BLOCK), 1.0, 6.0, ((0, 32), (2, 8)))
    legendre = noise(key_list[1], (SLOTS, BLOCK, BLOCK * LATS), DEGREES ** -0.5, 0.1875, ((0, 8),))
    lat_weights = jnp.clip(jnp.exp(jax.random.uniform(key_list[2], (LATS,), jnp.float32, math.log(4.0), math.log(16.0))), 4.0, 16.0)
    m_blocks = draw_m_blocks(jax.random.fold_in(key_list[4], 71), 0)
    return dict(coeffs=coeffs, legendre=legendre, lat_weights=lat_weights, m_blocks=m_blocks)


def block_lookup(blocks, wanted):
    indices = jnp.arange(blocks.shape[0], dtype=jnp.int32)
    return lax.optimization_barrier(jnp.sum(jnp.where(indices[None, :] == wanted[:, None], blocks[None, :], 0), axis=1)).astype(jnp.int32)

def slot_positions(listed, slot_total, span):
    slot_ids = jnp.arange(slot_total, dtype=jnp.int32)
    pair_index = slot_ids // span
    offsets = slot_ids % span
    leading = block_lookup(listed, 2 * pair_index)
    return 2 * pair_index + (offsets >= span - 1 - leading).astype(jnp.int32)

def azimuth_basis(blocks, block, points):
    columns = jnp.arange(blocks.shape[0] * block, dtype=jnp.int32)
    block_base = block_lookup(blocks, columns // block)
    orders = block_base * block + columns % block
    phases = orders[:, None] * jnp.arange(points, dtype=jnp.int32)[None, :] % points
    angles = phases.astype(jnp.float32) * (2.0 * math.pi / points)
    return jnp.stack([jnp.cos(angles), -jnp.sin(angles)])

def induction_terms(velocity, magnetic):
    return [velocity[1] * magnetic[2] - velocity[2] * magnetic[1], velocity[2] * magnetic[0] - velocity[0] * magnetic[2], velocity[0] * magnetic[1] - velocity[1] * magnetic[0], 0.5 * (magnetic[0] * magnetic[0] + magnetic[1] * magnetic[1] + magnetic[2] * magnetic[2])]

def reference(coeffs, legendre, lat_weights, m_blocks):
    highest = lax.Precision.HIGHEST
    position = slot_positions(m_blocks, SLOTS, MBLOCKS + 1)
    one_hot = (position[:, None] == jnp.arange(MBLOCKS, dtype=jnp.int32)[None, :]).astype(jnp.float32)
    legendre_table = legendre.astype(jnp.float32).reshape(SLOTS, BLOCK, BLOCK, LATS)
    basis = azimuth_basis(m_blocks, BLOCK, PHI_POINTS)
    inv_width = 1.0 / math.sqrt(DEGREES)
    inv_points = 1.0 / math.sqrt(PHI_POINTS)

    def one_shell(spectra):
        values = spectra.astype(jnp.float32).reshape(12, SLOTS, BLOCK, BLOCK)
        partial_value = jnp.einsum('ksjl,sjlt->sjkt', values, legendre_table, precision=highest)
        grouped = jnp.einsum('sq,sjkt->ktqj', one_hot, partial_value, precision=highest)
        rounded = grouped.reshape(12, LATS, DEGREES).astype(jnp.bfloat16)
        rounded = lax.optimization_barrier(rounded)
        lat_values = rounded.astype(jnp.float32).reshape(6, 2, LATS, DEGREES)
        field_grid = jnp.einsum('fctm,cmp->ftp', lat_values, basis, precision=highest) * inv_width
        products = jnp.stack(induction_terms([field_grid[0], field_grid[1], field_grid[2]], [field_grid[3], field_grid[4], field_grid[5]]))
        spectral_out = jnp.einsum('gtp,cmp->gctm', products, basis, precision=highest) * inv_points
        spectral_out = spectral_out * lat_weights[None, None, :, None]
        return spectral_out.reshape(8, LATS, DEGREES).astype(jnp.bfloat16)
    lat_terms = lax.map(one_shell, coeffs)
    widened = jnp.pad(lat_terms.astype(jnp.float32), ((2, 2), (0, 0), (0, 0), (0, 0)))
    combined = (widened[:-4] - 8.0 * widened[1:-3] + 8.0 * widened[3:-1] - widened[4:]) / 12.0

    def analyse(shell_terms):
        grouped = shell_terms.reshape(8, LATS, MBLOCKS, BLOCK)
        per_slot = jnp.take(grouped, position, axis=2)
        result = jnp.einsum('sjlt,ktsj->ksjl', legendre_table, per_slot, precision=highest)
        return result.reshape(8, SLOTS, BLOCK * BLOCK)

    def finish(paired):
        return (analyse(paired[0]).astype(jnp.bfloat16), analyse(paired[1]).astype(jnp.bfloat16))
    nonlinear, radial_slope = lax.map(finish, (lat_terms.astype(jnp.float32), combined))
    return (nonlinear, radial_slope)
```

```python
import math

import jax
import jax.numpy as jnp
import numpy as np
from jax import lax
from jax.experimental import pallas as pl
from jax.experimental.pallas import tpu as pltpu
from jax.sharding import PartitionSpec as P

F32, BF16 = jnp.float32, jnp.bfloat16
POINTS = 3072
QUARTER = POINTS // 4
SLOTS = 17
GROUPS = 16
SPAN = 16


def lane_permutation():
    natural = np.zeros((256, 256), np.float32)
    for j in range(4):
        for c in range(16):
            for a in range(4):
                natural[j * 64 + c * 4 + a, j * 64 + a * 16 + c] = 1.0
    return natural


def lane_masks():
    lanes = np.arange(128) // 32
    return np.stack([np.broadcast_to(lanes == j, (16, 128)) for j in range(4)])


def quarter_table():
    j = np.arange(4)[:, None, None, None]
    b = np.arange(16)[None, :, None, None]
    g = np.arange(16)[None, None, :, None]
    x = np.arange(QUARTER)[None, None, None, :]
    order = b * 64 + g * 4 + j
    turns = (order * (2 * x + 1)) % (2 * POINTS)
    angles = turns * (math.pi / POINTS)
    table = np.stack([np.cos(angles), np.sin(angles)])
    return table.reshape(2, 4, 256, QUARTER)


def own_block(blocks_ref, s):
    lead = blocks_ref[2 * lax.axis_index("ma")]
    return (s >= SPAN - lead).astype(jnp.int32)


def spread_rows(leg, s, rows_scr):
    for c in range(16):
        rows_scr[pl.ds(c, 64, stride=16), :] = leg[s, :, c * 128 : (c + 1) * 128].astype(F32)


def block_weights(rows, masks):
    rolled = [rows] + [pltpu.roll(rows, 32 * r, 1) for r in (1, 2, 3)]
    return jnp.concatenate(
        [rolled[(j - a) % 4][j * 16 : (j + 1) * 16] * masks[j] for j in range(4) for a in range(4)],
        axis=0,
    )


def swap_lane_groups(parts, lane_group):
    results = []
    for a in range(4):
        value = None
        for s in range(4):
            shift = (s - a) % 4
            moved = pltpu.roll(parts[s], 32 * shift, 1) if shift else parts[s]
            value = moved if value is None else jnp.where(lane_group == s, moved, value)
        results.append(value)
    return results


def synth_kernel(blocks_ref, coef_hbm, leg_hbm, perm_ref, mask_ref, out_ref, coef, leg, sem_c, sem_l, rows_scr, acc, turned):
    def fetch(s):
        return (
            pltpu.make_async_copy(leg_hbm.at[s], leg.at[s], sem_l.at[s]),
            pltpu.make_async_copy(coef_hbm.at[:, s], coef.at[s], sem_c.at[s]),
        )

    def start(s, carry):
        for copy in fetch(s):
            copy.start()
        return carry

    lax.fori_loop(0, SLOTS, start, 0)
    acc[...] = jnp.zeros_like(acc)
    masks = [mask_ref[j] for j in range(4)]

    def slot(s, carry):
        for copy in fetch(s):
            copy.wait()
        spread_rows(leg, s, rows_scr)
        base = own_block(blocks_ref, s) * (GROUPS * 24)
        values = jnp.concatenate(
            [coef[s, :, :, g * 256 : (g + 1) * 256].reshape(24, 256) for g in range(GROUPS)], axis=0
        )
        values = jnp.dot(values, perm_ref[...], preferred_element_type=F32).astype(BF16)
        for g in range(GROUPS):
            weights = block_weights(rows_scr[g * 64 : (g + 1) * 64, :].astype(BF16), masks)
            term = jnp.dot(values[g * 24 : (g + 1) * 24], weights, preferred_element_type=F32)
            where = pl.ds(pl.multiple_of(base + g * 24, 8), 24)
            acc[where, :] = acc[where, :] + term
        return carry

    lax.fori_loop(0, SLOTS, slot, 0)
    for comp in range(3):
        for i in range(2):
            parts = []
            for part in range(2):
                for vm in range(2):
                    row = ((vm * 3 + comp) * 2 + part) * 2 + i
                    parts.append(acc[pl.ds(row, 2 * GROUPS, stride=24), :])
            turned[comp * 2 + i] = jnp.concatenate(parts, axis=0).T
    for d in range(8):
        for j in range(4):
            pieces = [turned[n, pl.ds(j * 32 + d, 4, stride=8), :] for n in range(6)]
            out_ref[d, j] = jnp.concatenate(pieces, axis=0).astype(BF16)


def synthesis(m_blocks, coeffs, legendre, perm, masks):
    return pl.pallas_call(
        synth_kernel,
        in_specs=[
            pl.BlockSpec(memory_space=pltpu.SMEM),
            pl.BlockSpec(memory_space=pltpu.HBM),
            pl.BlockSpec(memory_space=pltpu.HBM),
            pl.BlockSpec(memory_space=pltpu.VMEM),
            pl.BlockSpec(memory_space=pltpu.VMEM),
        ],
        out_specs=pl.BlockSpec(memory_space=pltpu.VMEM),
        out_shape=jax.ShapeDtypeStruct((8, 4, 24, 128), BF16),
        scratch_shapes=[
            pltpu.VMEM((SLOTS, 12, 2, 4096), BF16),
            pltpu.VMEM((SLOTS, 64, 2048), BF16),
            pltpu.SemaphoreType.DMA((SLOTS,)),
            pltpu.SemaphoreType.DMA((SLOTS,)),
            pltpu.VMEM((1024, 128), F32),
            pltpu.VMEM((2 * GROUPS * 24, 128), F32),
            pltpu.VMEM((6, 128, 128), F32),
        ],
        compiler_params=pltpu.CompilerParams(vmem_limit_bytes=32 * 2**20),
        name="synthesis",
    )(m_blocks, coeffs, legendre, perm, masks)


def azimuth_kernel(blocks_ref, weights_ref, in_ref, table_hbm, out_ref, table, sem, even_c, odd_c, even_s, odd_s, folded):
    def copies(p):
        source = pl.ds(pl.multiple_of(blocks_ref[p] * 16, 16), 16)
        target = pl.ds(pl.multiple_of(p * 16, 16), 16)
        return [
            pltpu.make_async_copy(table_hbm.at[part, j, source], table.at[part, j, target], sem.at[part, j, p])
            for part in range(2)
            for j in range(4)
        ]

    def start(p, carry):
        for copy in copies(p):
            copy.start()
        return carry

    def finish(p, carry):
        for copy in copies(p):
            copy.wait()
        return carry

    lax.fori_loop(0, 16, start, 0)
    lane_group = lax.broadcasted_iota(jnp.int32, (24, 128), 1) // 32
    left = []
    for j in range(4):
        halves = []
        for h in range(2):
            parts = [in_ref[h * 4 + s, j].astype(F32) * (1.0 / 32.0) for s in range(4)]
            halves.append(swap_lane_groups(parts, lane_group))
        both = [jnp.concatenate([halves[0][n], halves[1][n]], axis=1) for n in range(4)]
        left.append([jnp.concatenate([both[part * 2], both[part * 2 + 1]], axis=0).astype(BF16) for part in range(2)])
    lax.fori_loop(0, 16, finish, 0)
    for part, refs in ((0, (even_c, odd_c)), (1, (even_s, odd_s))):
        for parity in range(2):
            refs[parity][...] = jnp.dot(
                left[parity][part], table[part, parity], preferred_element_type=F32
            ) + jnp.dot(left[parity + 2][part], table[part, parity + 2], preferred_element_type=F32)
    for x in range(QUARTER // 128):
        cols = slice(x * 128, (x + 1) * 128)
        fields = [[], [], [], []]
        for f in range(6):
            rows = slice(f * 8, (f + 1) * 8)
            ce, co, se, so = even_c[rows, cols], odd_c[rows, cols], even_s[rows, cols], odd_s[rows, cols]
            plus, minus = ce + co, ce - co
            total, other = se + so, se - so
            fields[0].append(plus - total)
            fields[1].append(plus + total)
            fields[2].append(minus + other)
            fields[3].append(minus - other)
        products = []
        for n in range(4):
            u0, u1, u2, b0, b1, b2 = fields[n]
            products.append(
                [
                    u1 * b2 - u2 * b1,
                    u2 * b0 - u0 * b2,
                    u0 * b1 - u1 * b0,
                    0.5 * (b0 * b0 + b1 * b1 + b2 * b2),
                ]
            )
        folds = [[], [], [], []]
        for g in range(4):
            p0, p1, p2, p3 = (products[n][g] for n in range(4))
            front, back = p0 + p1, p2 + p3
            left_odd, right_odd = p1 - p0, p2 - p3
            folds[0].append(front + back)
            folds[1].append(front - back)
            folds[2].append(left_odd + right_odd)
            folds[3].append(left_odd - right_odd)
        for n in range(4):
            folded[n, :, cols] = jnp.concatenate(folds[n], axis=0).astype(BF16)
    row = lax.broadcasted_iota(jnp.int32, (8, 1), 0) % 4
    own = lax.axis_index("ma")
    weight = jnp.zeros((8, 1), F32)
    for t in range(4):
        weight = jnp.where(row == t, weights_ref[t * 8 + own], weight)
    lane_group = lax.broadcasted_iota(jnp.int32, (8, 128), 1) // 32
    for j in range(4):
        terms = [
            lax.dot_general(
                folded[part * 2 + j % 2], table[part, j], (((1,), (1,)), ((), ())), preferred_element_type=F32
            )
            for part in range(2)
        ]
        for gh in range(2):
            for h in range(2):
                parts = []
                for gl in range(2):
                    for part in range(2):
                        g = gh * 2 + gl
                        piece = terms[part][g * 8 : (g + 1) * 8, h * 128 : (h + 1) * 128]
                        parts.append((piece * (1.0 / math.sqrt(POINTS))) * weight)
                swapped = swap_lane_groups(parts, lane_group)
                for s in range(4):
                    where = (j * 2 + gh) * 8
                    out_ref[h * 4 + s, where : where + 8, :] = swapped[s].astype(BF16)


def azimuth(m_blocks, lat_weights, received, table):
    grid_shape = pltpu.VMEM((48, QUARTER), F32)
    return pl.pallas_call(
        azimuth_kernel,
        in_specs=[
            pl.BlockSpec(memory_space=pltpu.SMEM),
            pl.BlockSpec(memory_space=pltpu.SMEM),
            pl.BlockSpec(memory_space=pltpu.VMEM),
            pl.BlockSpec(memory_space=pltpu.HBM),
        ],
        out_specs=pl.BlockSpec(memory_space=pltpu.VMEM),
        out_shape=jax.ShapeDtypeStruct((8, 64, 128), BF16),
        scratch_shapes=[
            pltpu.VMEM((2, 4, 256, QUARTER), BF16),
            pltpu.SemaphoreType.DMA((2, 4, 16)),
            grid_shape,
            grid_shape,
            grid_shape,
            grid_shape,
            pltpu.VMEM((4, 32, QUARTER), BF16),
        ],
        compiler_params=pltpu.CompilerParams(vmem_limit_bytes=32 * 2**20),
        name="azimuth",
    )(m_blocks, lat_weights, received, table)


def analysis_kernel(
    blocks_ref, own_ref, low_ref, high_ref, leg_hbm, perm_ref, mask_ref, plain_hbm, slope_hbm,
    leg, sem_l, rows_scr, placed, turned, terms, out, sem_o,
):
    def fetch(s):
        return pltpu.make_async_copy(leg_hbm.at[s], leg.at[s], sem_l.at[s])

    def start(s, carry):
        fetch(s).start()
        return carry

    lax.fori_loop(0, SLOTS, start, 0)
    for n, ref in enumerate((own_ref, low_ref, high_ref)):
        for d in range(8):
            for j in range(4):
                for gh in range(2):
                    where = (j * 2 + gh) * 8
                    placed[n, pl.ds((gh * 4 + j) * 64 + d, 8, stride=8), :] = ref[d, where : where + 8, :].astype(F32)

    def pick(n, gh, j, i):
        return placed[n, (gh * 4 + j) * 64 + i * 32 : (gh * 4 + j) * 64 + (i + 1) * 32, :]

    for gh in range(2):
        columns = [[], [], [], []]
        for j in range(4):
            o0, o1 = pick(0, gh, j, 0), pick(0, gh, j, 1)
            l0, l1 = pick(1, gh, j, 0), pick(1, gh, j, 1)
            h0, h1 = pick(2, gh, j, 0), pick(2, gh, j, 1)
            columns[0].append(o0)
            columns[1].append(o1)
            columns[2].append((l0 - 8.0 * l1 + 8.0 * o1 - h0) / 12.0)
            columns[3].append((l1 - 8.0 * o0 + 8.0 * h0 - h1) / 12.0)
        for n in range(2):
            for i in range(2):
                block = jnp.concatenate(columns[n * 2 + i], axis=0)
                turned[n, (i * 2 + gh) * 128 : (i * 2 + gh + 1) * 128, :] = block.T
    for qg in range(2 * GROUPS):
        pair = [turned[n, pl.ds(qg, 16, stride=32), :] for n in range(2)]
        terms[qg] = jnp.concatenate(pair, axis=0).astype(BF16)
    masks = [mask_ref[j] for j in range(4)]

    def send(s):
        return [
            pltpu.make_async_copy(out.at[s, n, i], ref.at[i, s], sem_o.at[s, n, i])
            for n, ref in enumerate((plain_hbm, slope_hbm))
            for i in range(2)
        ]

    def slot(s, carry):
        fetch(s).wait()
        spread_rows(leg, s, rows_scr)
        base = own_block(blocks_ref, s) * GROUPS
        values = []
        for g in range(GROUPS):
            weights = block_weights(rows_scr[g * 64 : (g + 1) * 64, :].astype(BF16), masks)
            value = lax.dot_general(
                terms[base + g], weights, (((1,), (1,)), ((), ())), preferred_element_type=F32
            )
            values.append(value.astype(BF16))
        values = jnp.concatenate(values, axis=0)
        values = jnp.dot(values, perm_ref[...], preferred_element_type=F32).astype(BF16)
        for g in range(GROUPS):
            for n in range(2):
                for i in range(2):
                    row = g * 32 + n * 16 + i * 8
                    out[s, n, i, :, g * 256 : (g + 1) * 256] = values[row : row + 8]
        for copy in send(s):
            copy.start()
        return carry

    lax.fori_loop(0, SLOTS, slot, 0)

    def finish(s, carry):
        for copy in send(s):
            copy.wait()
        return carry

    lax.fori_loop(0, SLOTS, finish, 0)


def analysis(m_blocks, own, low, high, legendre, perm_back, masks):
    shape = jax.ShapeDtypeStruct((2, SLOTS, 8, 4096), BF16)
    vmem = pl.BlockSpec(memory_space=pltpu.VMEM)
    hbm = pl.BlockSpec(memory_space=pltpu.HBM)
    return pl.pallas_call(
        analysis_kernel,
        in_specs=[pl.BlockSpec(memory_space=pltpu.SMEM), vmem, vmem, vmem, hbm, vmem, vmem],
        out_specs=[hbm, hbm],
        out_shape=[shape, shape],
        scratch_shapes=[
            pltpu.VMEM((SLOTS, 64, 2048), BF16),
            pltpu.SemaphoreType.DMA((SLOTS,)),
            pltpu.VMEM((1024, 128), F32),
            pltpu.VMEM((3, 512, 128), F32),
            pltpu.VMEM((2, 512, 128), F32),
            pltpu.VMEM((2 * GROUPS, 32, 128), BF16),
            pltpu.VMEM((SLOTS, 2, 2, 8, 4096), BF16),
            pltpu.SemaphoreType.DMA((SLOTS, 2, 2)),
        ],
        compiler_params=pltpu.CompilerParams(vmem_limit_bytes=32 * 2**20),
        name="analysis",
    )(m_blocks, own, low, high, legendre, perm_back, masks)


def constants():
    perm = lane_permutation()
    return (
        jnp.asarray(perm, BF16),
        jnp.asarray(perm.T, BF16),
        jnp.asarray(lane_masks(), BF16),
        jnp.asarray(quarter_table(), BF16),
    )


def local(coeffs, legendre, lat_weights, m_blocks):
    perm, perm_back, masks, table = constants()
    sent = synthesis(m_blocks, coeffs.transpose(1, 2, 0, 3), legendre, perm, masks)
    received = lax.all_to_all(sent, "ma", split_axis=0, concat_axis=0, tiled=True)
    sent_back = azimuth(m_blocks, lat_weights, received, table)
    own = lax.all_to_all(sent_back, "ma", split_axis=0, concat_axis=0, tiled=True)
    count = lax.axis_size("row")
    low = lax.ppermute(own, "row", [(r, r + 1) for r in range(count - 1)])
    high = lax.ppermute(own, "row", [(r + 1, r) for r in range(count - 1)])
    plain, slope = analysis(m_blocks, own, low, high, legendre, perm_back, masks)
    return plain.transpose(0, 2, 1, 3), slope.transpose(0, 2, 1, 3)


def solution(mesh):
    placed = (P("row", None, "ma", None), P("ma", None, None), P(), P())
    return jax.shard_map(
        local,
        mesh=mesh,
        in_specs=placed,
        out_specs=(P("row", None, "ma", None), P("row", None, "ma", None)),
        check_vma=False,
    )
```

```python
import math

import jax
import jax.numpy as jnp
import numpy as np
from jax import lax
from jax.experimental import pallas as pl
from jax.experimental.pallas import tpu as pltpu
from jax.sharding import PartitionSpec as P

F32, BF16 = jnp.float32, jnp.bfloat16
POINTS = 3072
QUARTER = POINTS // 4
SLOTS = 17
GROUPS = 16
SPAN = 16


def lane_permutation(back=False):
    natural = lax.broadcasted_iota(jnp.int32, (256, 256), 1 if back else 0)
    grouped = lax.broadcasted_iota(jnp.int32, (256, 256), 0 if back else 1)
    target = natural // 64 * 64 + natural % 4 * 16 + natural % 64 // 4
    return (target == grouped).astype(F32).astype(BF16)


def lane_masks():
    group = lax.broadcasted_iota(jnp.int32, (16, 128), 1) // 32
    return [(group == j).astype(F32).astype(BF16) for j in range(4)]


def quarter_table():
    j = np.arange(4)[:, None, None, None]
    b = np.arange(16)[None, :, None, None]
    g = np.arange(16)[None, None, :, None]
    x = np.arange(QUARTER)[None, None, None, :]
    order = b * 64 + g * 4 + j
    turns = (order * (2 * x + 1)) % (2 * POINTS)
    angles = turns * (math.pi / POINTS)
    table = np.stack([np.cos(angles), np.sin(angles)])
    return table.reshape(2, 4, 256, QUARTER)


def own_block(blocks_ref, s):
    lead = blocks_ref[2 * lax.axis_index("ma")]
    return (s >= SPAN - lead).astype(jnp.int32)


def spread_rows(leg, s, rows_scr):
    for c in range(16):
        rows_scr[pl.ds(c, 64, stride=16), :] = leg[s, :, c * 128 : (c + 1) * 128].astype(F32)


def block_weights(rows, masks):
    rolled = [rows] + [pltpu.roll(rows, 32 * r, 1) for r in (1, 2, 3)]
    pieces = []
    for j in range(2):
        for a in range(4):
            first, second = j, 2 + j
            pieces.append(
                rolled[(first - a) % 4][first * 16 : (first + 1) * 16] * masks[first]
                + rolled[(second - a) % 4][second * 16 : (second + 1) * 16] * masks[second]
            )
    return jnp.concatenate(pieces, axis=0)


def swap_lane_groups(parts, lane_group):
    results = []
    for a in range(4):
        value = None
        for s in range(4):
            shift = (s - a) % 4
            moved = pltpu.roll(parts[s], 32 * shift, 1) if shift else parts[s]
            value = moved if value is None else jnp.where(lane_group == s, moved, value)
        results.append(value)
    return results


def synth_kernel(blocks_ref, coef_hbm, leg_hbm, out_ref, coef, leg, sem_c, sem_l, rows_scr, acc, turned):
    def fetch(s):
        return (
            pltpu.make_async_copy(leg_hbm.at[s], leg.at[s], sem_l.at[s]),
            pltpu.make_async_copy(coef_hbm.at[:, s], coef.at[s], sem_c.at[s]),
        )

    def start(s, carry):
        for copy in fetch(s):
            copy.start()
        return carry

    lax.fori_loop(0, SLOTS, start, 0)
    acc[...] = jnp.zeros_like(acc)
    masks = lane_masks()
    perm = lane_permutation()
    lower = lax.broadcasted_iota(jnp.int32, (24, 128), 1) < 64

    def slot(s, carry):
        for copy in fetch(s):
            copy.wait()
        spread_rows(leg, s, rows_scr)
        base = own_block(blocks_ref, s) * (GROUPS * 24)
        values = jnp.concatenate(
            [coef[s, :, :, g * 256 : (g + 1) * 256].reshape(24, 256) for g in range(GROUPS)], axis=0
        )
        values = jnp.dot(values, perm, preferred_element_type=F32)
        for g in range(GROUPS):
            weights = block_weights(rows_scr[g * 64 : (g + 1) * 64, :].astype(BF16), masks)
            rows = slice(g * 24, (g + 1) * 24)
            stacked = jnp.concatenate([values[rows, :128], values[rows, 128:]], axis=0).astype(BF16)
            term = jnp.dot(stacked, weights, preferred_element_type=F32)
            where = pl.ds(pl.multiple_of(base + g * 24, 8), 24)
            acc[where, :] = acc[where, :] + jnp.where(lower, term[:24], term[24:])
        return carry

    lax.fori_loop(0, SLOTS, slot, 0)
    for comp in range(3):
        for i in range(2):
            parts = []
            for part in range(2):
                for vm in range(2):
                    row = ((vm * 3 + comp) * 2 + part) * 2 + i
                    parts.append(acc[pl.ds(row, 2 * GROUPS, stride=24), :])
            turned[comp * 2 + i] = jnp.concatenate(parts, axis=0).T
    for d in range(8):
        for j in range(4):
            pieces = [turned[n, pl.ds(j * 32 + d, 4, stride=8), :] for n in range(6)]
            out_ref[d, j] = jnp.concatenate(pieces, axis=0).astype(BF16)


def synthesis(m_blocks, coeffs, legendre):
    return pl.pallas_call(
        synth_kernel,
        in_specs=[
            pl.BlockSpec(memory_space=pltpu.SMEM),
            pl.BlockSpec(memory_space=pltpu.HBM),
            pl.BlockSpec(memory_space=pltpu.HBM),
        ],
        out_specs=pl.BlockSpec(memory_space=pltpu.VMEM),
        out_shape=jax.ShapeDtypeStruct((8, 4, 24, 128), BF16),
        scratch_shapes=[
            pltpu.VMEM((SLOTS, 12, 2, 4096), BF16),
            pltpu.VMEM((SLOTS, 64, 2048), BF16),
            pltpu.SemaphoreType.DMA((SLOTS,)),
            pltpu.SemaphoreType.DMA((SLOTS,)),
            pltpu.VMEM((1024, 128), F32),
            pltpu.VMEM((2 * GROUPS * 24, 128), F32),
            pltpu.VMEM((6, 128, 128), F32),
        ],
        compiler_params=pltpu.CompilerParams(vmem_limit_bytes=60 * 2**20),
        name="synthesis",
    )(m_blocks, coeffs, legendre)


def azimuth_kernel(blocks_ref, weights_ref, in_ref, table, out_ref, even_c, odd_c, even_s, odd_s, folded):
    starts = [pl.multiple_of(blocks_ref[p] * 16, 16) for p in range(16)]

    def basis(part, j):
        return jnp.concatenate([table[part, j, pl.ds(start, 16), :] for start in starts], axis=0)

    lane_group = lax.broadcasted_iota(jnp.int32, (24, 128), 1) // 32
    left = []
    for j in range(4):
        halves = []
        for h in range(2):
            parts = [in_ref[h * 4 + s, j].astype(F32) * (1.0 / 32.0) for s in range(4)]
            halves.append(swap_lane_groups(parts, lane_group))
        both = [jnp.concatenate([halves[0][n], halves[1][n]], axis=1) for n in range(4)]
        left.append([jnp.concatenate([both[part * 2], both[part * 2 + 1]], axis=0).astype(BF16) for part in range(2)])
    for part, refs in ((0, (even_c, odd_c)), (1, (even_s, odd_s))):
        for parity in range(2):
            refs[parity][...] = jnp.dot(
                left[parity][part], basis(part, parity), preferred_element_type=F32
            ) + jnp.dot(left[parity + 2][part], basis(part, parity + 2), preferred_element_type=F32)
    for x in range(QUARTER // 128):
        cols = slice(x * 128, (x + 1) * 128)
        fields = [[], [], [], []]
        for f in range(6):
            rows = slice(f * 8, (f + 1) * 8)
            ce, co, se, so = even_c[rows, cols], odd_c[rows, cols], even_s[rows, cols], odd_s[rows, cols]
            plus, minus = ce + co, ce - co
            total, other = se + so, se - so
            fields[0].append(plus - total)
            fields[1].append(plus + total)
            fields[2].append(minus + other)
            fields[3].append(minus - other)
        products = []
        for n in range(4):
            u0, u1, u2, b0, b1, b2 = fields[n]
            products.append(
                [
                    u1 * b2 - u2 * b1,
                    u2 * b0 - u0 * b2,
                    u0 * b1 - u1 * b0,
                    0.5 * (b0 * b0 + b1 * b1 + b2 * b2),
                ]
            )
        folds = [[], [], [], []]
        for g in range(4):
            p0, p1, p2, p3 = (products[n][g] for n in range(4))
            front, back = p0 + p1, p2 + p3
            left_odd, right_odd = p1 - p0, p2 - p3
            folds[0].append(front + back)
            folds[1].append(front - back)
            folds[2].append(left_odd + right_odd)
            folds[3].append(left_odd - right_odd)
        for n in range(4):
            folded[n, :, cols] = jnp.concatenate(folds[n], axis=0).astype(BF16)
    row = lax.broadcasted_iota(jnp.int32, (8, 1), 0) % 4
    own = lax.axis_index("ma")
    weight = jnp.zeros((8, 1), F32)
    for t in range(4):
        weight = jnp.where(row == t, weights_ref[t * 8 + own], weight)
    lane_group = lax.broadcasted_iota(jnp.int32, (8, 128), 1) // 32
    for j in range(4):
        terms = [
            lax.dot_general(
                folded[part * 2 + j % 2], basis(part, j), (((1,), (1,)), ((), ())), preferred_element_type=F32
            )
            for part in range(2)
        ]
        for gh in range(2):
            for h in range(2):
                parts = []
                for gl in range(2):
                    for part in range(2):
                        g = gh * 2 + gl
                        piece = terms[part][g * 8 : (g + 1) * 8, h * 128 : (h + 1) * 128]
                        parts.append((piece * (1.0 / math.sqrt(POINTS))) * weight)
                swapped = swap_lane_groups(parts, lane_group)
                for s in range(4):
                    where = (j * 2 + gh) * 8
                    out_ref[h * 4 + s, where : where + 8, :] = swapped[s].astype(BF16)


def azimuth(m_blocks, lat_weights, received, table):
    grid_shape = pltpu.VMEM((48, QUARTER), F32)
    return pl.pallas_call(
        azimuth_kernel,
        in_specs=[
            pl.BlockSpec(memory_space=pltpu.SMEM),
            pl.BlockSpec(memory_space=pltpu.SMEM),
            pl.BlockSpec(memory_space=pltpu.VMEM),
            pl.BlockSpec(memory_space=pltpu.VMEM),
        ],
        out_specs=pl.BlockSpec(memory_space=pltpu.VMEM),
        out_shape=jax.ShapeDtypeStruct((8, 64, 128), BF16),
        scratch_shapes=[
            grid_shape,
            grid_shape,
            grid_shape,
            grid_shape,
            pltpu.VMEM((4, 32, QUARTER), BF16),
        ],
        compiler_params=pltpu.CompilerParams(vmem_limit_bytes=32 * 2**20),
        name="azimuth",
    )(m_blocks, lat_weights, received, table)


def analysis_kernel(
    blocks_ref, own_ref, low_ref, high_ref, leg_hbm, plain_hbm, slope_hbm,
    leg, sem_l, rows_scr, placed, turned, terms, out, sem_o,
):
    def fetch(s):
        return pltpu.make_async_copy(leg_hbm.at[s], leg.at[s], sem_l.at[s])

    def start(s, carry):
        fetch(s).start()
        return carry

    lax.fori_loop(0, SLOTS, start, 0)
    for n, ref in enumerate((own_ref, low_ref, high_ref)):
        for d in range(8):
            for j in range(4):
                for gh in range(2):
                    where = (j * 2 + gh) * 8
                    placed[n, pl.ds((gh * 4 + j) * 64 + d, 8, stride=8), :] = ref[d, where : where + 8, :].astype(F32)

    def pick(n, gh, j, i):
        return placed[n, (gh * 4 + j) * 64 + i * 32 : (gh * 4 + j) * 64 + (i + 1) * 32, :]

    for gh in range(2):
        columns = [[], [], [], []]
        for j in range(4):
            o0, o1 = pick(0, gh, j, 0), pick(0, gh, j, 1)
            l0, l1 = pick(1, gh, j, 0), pick(1, gh, j, 1)
            h0, h1 = pick(2, gh, j, 0), pick(2, gh, j, 1)
            columns[0].append(o0)
            columns[1].append(o1)
            columns[2].append((l0 - 8.0 * l1 + 8.0 * o1 - h0) / 12.0)
            columns[3].append((l1 - 8.0 * o0 + 8.0 * h0 - h1) / 12.0)
        for n in range(2):
            for i in range(2):
                block = jnp.concatenate(columns[n * 2 + i], axis=0)
                turned[n, (i * 2 + gh) * 128 : (i * 2 + gh + 1) * 128, :] = block.T
    lower = lax.broadcasted_iota(jnp.int32, (32, 128), 1) < 64
    for qg in range(2 * GROUPS):
        pair = [turned[n, pl.ds(qg, 16, stride=32), :] for n in range(2)]
        both = jnp.concatenate(pair, axis=0)
        halves = [jnp.where(lower, both, 0.0), jnp.where(lower, 0.0, both)]
        terms[qg] = jnp.concatenate(halves, axis=0).astype(BF16)
    masks = lane_masks()
    perm = lane_permutation(back=True)

    def send(s):
        return [
            pltpu.make_async_copy(out.at[s, n, i], ref.at[i, s], sem_o.at[s, n, i])
            for n, ref in enumerate((plain_hbm, slope_hbm))
            for i in range(2)
        ]

    def slot(s, carry):
        fetch(s).wait()
        spread_rows(leg, s, rows_scr)
        base = own_block(blocks_ref, s) * GROUPS
        values = []
        for g in range(GROUPS):
            weights = block_weights(rows_scr[g * 64 : (g + 1) * 64, :].astype(BF16), masks)
            value = lax.dot_general(
                terms[base + g], weights, (((1,), (1,)), ((), ())), preferred_element_type=F32
            )
            values.append(jnp.concatenate([value[:32], value[32:]], axis=1).astype(BF16))
        values = jnp.concatenate(values, axis=0)
        values = jnp.dot(values, perm, preferred_element_type=F32).astype(BF16)
        for g in range(GROUPS):
            for n in range(2):
                for i in range(2):
                    row = g * 32 + n * 16 + i * 8
                    out[s, n, i, :, g * 256 : (g + 1) * 256] = values[row : row + 8]
        for copy in send(s):
            copy.start()
        return carry

    lax.fori_loop(0, SLOTS, slot, 0)

    def finish(s, carry):
        for copy in send(s):
            copy.wait()
        return carry

    lax.fori_loop(0, SLOTS, finish, 0)


def analysis(m_blocks, own, low, high, legendre):
    shape = jax.ShapeDtypeStruct((2, SLOTS, 8, 4096), BF16)
    vmem = pl.BlockSpec(memory_space=pltpu.VMEM)
    hbm = pl.BlockSpec(memory_space=pltpu.HBM)
    return pl.pallas_call(
        analysis_kernel,
        in_specs=[pl.BlockSpec(memory_space=pltpu.SMEM), vmem, vmem, vmem, hbm],
        out_specs=[hbm, hbm],
        out_shape=[shape, shape],
        scratch_shapes=[
            pltpu.VMEM((SLOTS, 64, 2048), BF16),
            pltpu.SemaphoreType.DMA((SLOTS,)),
            pltpu.VMEM((1024, 128), F32),
            pltpu.VMEM((3, 512, 128), F32),
            pltpu.VMEM((2, 512, 128), F32),
            pltpu.VMEM((2 * GROUPS, 64, 128), BF16),
            pltpu.VMEM((SLOTS, 2, 2, 8, 4096), BF16),
            pltpu.SemaphoreType.DMA((SLOTS, 2, 2)),
        ],
        compiler_params=pltpu.CompilerParams(vmem_limit_bytes=32 * 2**20),
        name="analysis",
    )(m_blocks, own, low, high, legendre)


def local(coeffs, legendre, lat_weights, m_blocks):
    table = jnp.asarray(quarter_table(), BF16)
    sent = synthesis(m_blocks, coeffs.transpose(1, 2, 0, 3), legendre)
    received = lax.all_to_all(sent, "ma", split_axis=0, concat_axis=0, tiled=True)
    sent_back = azimuth(m_blocks, lat_weights, received, table)
    own = lax.all_to_all(sent_back, "ma", split_axis=0, concat_axis=0, tiled=True)
    count = lax.axis_size("row")
    low = lax.ppermute(own, "row", [(r, r + 1) for r in range(count - 1)])
    high = lax.ppermute(own, "row", [(r + 1, r) for r in range(count - 1)])
    plain, slope = analysis(m_blocks, own, low, high, legendre)
    return plain.transpose(0, 2, 1, 3), slope.transpose(0, 2, 1, 3)


def solution(mesh):
    placed = (P("row", None, "ma", None), P("ma", None, None), P(), P())
    return jax.shard_map(
        local,
        mesh=mesh,
        in_specs=placed,
        out_specs=(P("row", None, "ma", None), P("row", None, "ma", None)),
        check_vma=False,
    )
```

```python
import math

import jax
import jax.numpy as jnp
import numpy as np
from jax import lax
from jax.experimental import pallas as pl
from jax.experimental.pallas import tpu as pltpu
from jax.sharding import PartitionSpec as P

F32, BF16 = jnp.float32, jnp.bfloat16
POINTS = 3072
QUARTER = POINTS // 4
SLOTS = 17
GROUPS = 16
SPAN = 16


def lane_permutation(back=False):
    natural = lax.broadcasted_iota(jnp.int32, (256, 256), 1 if back else 0)
    grouped = lax.broadcasted_iota(jnp.int32, (256, 256), 0 if back else 1)
    target = natural // 64 * 64 + natural % 4 * 16 + natural % 64 // 4
    return (target == grouped).astype(F32).astype(BF16)


def lane_masks():
    group = lax.broadcasted_iota(jnp.int32, (16, 128), 1) // 32
    return [(group == j).astype(F32).astype(BF16) for j in range(4)]


def quarter_table():
    j = np.arange(4)[:, None, None, None]
    b = np.arange(16)[None, :, None, None]
    g = np.arange(16)[None, None, :, None]
    x = np.arange(QUARTER)[None, None, None, :]
    order = b * 64 + g * 4 + j
    turns = (order * (2 * x + 1)) % (2 * POINTS)
    angles = turns * (math.pi / POINTS)
    table = np.stack([np.cos(angles), np.sin(angles)])
    return table.reshape(2, 4, 256, QUARTER)


def own_block(blocks_ref, s):
    lead = blocks_ref[2 * lax.axis_index("ma")]
    return (s >= SPAN - lead).astype(jnp.int32)


def spread_rows(table, chunks):
    for c in range(16):
        chunks[c * 72 : c * 72 + 64, :] = table[:, c * 128 : (c + 1) * 128].astype(F32)


def group_rows(chunks, g):
    pieces = [chunks[pl.ds(g * 4 + j, 16, stride=72), :] for j in range(4)]
    return jnp.concatenate(pieces, axis=0).astype(BF16)


def block_weights(rows, masks):
    rolled = [rows] + [pltpu.roll(rows, 32 * r, 1) for r in (1, 2, 3)]
    pieces = []
    for j in range(2):
        for a in range(4):
            first, second = j, 2 + j
            pieces.append(
                rolled[(first - a) % 4][first * 16 : (first + 1) * 16] * masks[first]
                + rolled[(second - a) % 4][second * 16 : (second + 1) * 16] * masks[second]
            )
    return jnp.concatenate(pieces, axis=0)


def swap_lane_groups(parts, lane_group):
    results = []
    for a in range(4):
        value = None
        for s in range(4):
            shift = (s - a) % 4
            moved = pltpu.roll(parts[s], 32 * shift, 1) if shift else parts[s]
            value = moved if value is None else jnp.where(lane_group == s, moved, value)
        results.append(value)
    return results


def synth_kernel(
    blocks_ref, coef_hbm, leg_hbm, out_ref, weights_hbm,
    coef, leg, sem_c, sem_l, sem_w, chunks_even, chunks_odd, weights_even, weights_odd, values_even, values_odd, acc, turned,
):
    def fetch(s):
        return (
            pltpu.make_async_copy(leg_hbm.at[s], leg.at[s], sem_l.at[s]),
            pltpu.make_async_copy(coef_hbm.at[:, s], coef.at[s], sem_c.at[s]),
        )

    def start(s, carry):
        for copy in fetch(s):
            copy.start()
        return carry

    lax.fori_loop(0, SLOTS, start, 0)
    acc[...] = jnp.zeros_like(acc)
    masks = lane_masks()
    perm = lane_permutation()
    lower = lax.broadcasted_iota(jnp.int32, (24, 128), 1) < 64

    def prepare(s, chunks, weights, values):
        spread_rows(leg.at[s], chunks)
        for g in range(GROUPS):
            weights[g] = block_weights(group_rows(chunks, g), masks)
        rows = jnp.concatenate(
            [coef[s, :, :, g * 256 : (g + 1) * 256].reshape(24, 256) for g in range(GROUPS)], axis=0
        )
        rows = jnp.dot(rows, perm, preferred_element_type=F32)
        for g in range(GROUPS):
            part = rows[g * 24 : (g + 1) * 24]
            values[g * 48 : (g + 1) * 48, :] = jnp.concatenate([part[:, :128], part[:, 128:]], axis=0).astype(BF16)

    def combine(s, weights, values):
        base = own_block(blocks_ref, s) * (GROUPS * 24)
        for g in range(GROUPS):
            term = jnp.dot(values[g * 48 : (g + 1) * 48, :], weights[g], preferred_element_type=F32)
            where = pl.ds(pl.multiple_of(base + g * 24, 8), 24)
            acc[where, :] = acc[where, :] + jnp.where(lower, term[:24], term[24:])

    def arrive(s):
        for copy in fetch(s):
            copy.wait()

    def keep_even(t):
        return pltpu.make_async_copy(weights_even.at[t], weights_hbm.at[2 * t], sem_w.at[2 * t])

    def keep_odd(t):
        return pltpu.make_async_copy(weights_odd.at[t], weights_hbm.at[2 * t + 1], sem_w.at[2 * t + 1])

    arrive(0)
    prepare(0, chunks_even, weights_even.at[0], values_even)

    def pair(t, carry):
        keep_even(t).start()
        arrive(2 * t + 1)
        arrive(2 * t + 2)
        prepare(2 * t + 1, chunks_odd, weights_odd.at[t], values_odd)
        combine(2 * t, weights_even.at[t], values_even)
        prepare(2 * t + 2, chunks_even, weights_even.at[t + 1], values_even)
        combine(2 * t + 1, weights_odd.at[t], values_odd)
        keep_odd(t).start()
        return carry

    lax.fori_loop(0, SLOTS // 2, pair, 0)
    last = SLOTS // 2
    keep_even(last).start()
    combine(SLOTS - 1, weights_even.at[last], values_even)
    for comp in range(3):
        for i in range(2):
            parts = []
            for part in range(2):
                for vm in range(2):
                    row = ((vm * 3 + comp) * 2 + part) * 2 + i
                    parts.append(acc[pl.ds(row, 2 * GROUPS, stride=24), :])
            turned[comp * 2 + i] = jnp.concatenate(parts, axis=0).T
    for d in range(8):
        for j in range(4):
            pieces = [turned[n, pl.ds(j * 32 + d, 4, stride=8), :] for n in range(6)]
            out_ref[d, j] = jnp.concatenate(pieces, axis=0).astype(BF16)

    def finish(t, carry):
        keep_even(t).wait()
        keep_odd(t).wait()
        return carry

    lax.fori_loop(0, last, finish, 0)
    keep_even(last).wait()


def synthesis(m_blocks, coeffs, legendre):
    return pl.pallas_call(
        synth_kernel,
        in_specs=[
            pl.BlockSpec(memory_space=pltpu.SMEM),
            pl.BlockSpec(memory_space=pltpu.HBM),
            pl.BlockSpec(memory_space=pltpu.HBM),
        ],
        out_specs=[pl.BlockSpec(memory_space=pltpu.VMEM), pl.BlockSpec(memory_space=pltpu.HBM)],
        out_shape=[
            jax.ShapeDtypeStruct((8, 4, 24, 128), BF16),
            jax.ShapeDtypeStruct((SLOTS, GROUPS, 128, 128), BF16),
        ],
        scratch_shapes=[
            pltpu.VMEM((SLOTS, 12, 2, 4096), BF16),
            pltpu.VMEM((SLOTS, 64, 2048), BF16),
            pltpu.SemaphoreType.DMA((SLOTS,)),
            pltpu.SemaphoreType.DMA((SLOTS,)),
            pltpu.SemaphoreType.DMA((SLOTS,)),
            pltpu.VMEM((16 * 72, 128), F32),
            pltpu.VMEM((16 * 72, 128), F32),
            pltpu.VMEM((SLOTS // 2 + 1, GROUPS, 128, 128), BF16),
            pltpu.VMEM((SLOTS // 2, GROUPS, 128, 128), BF16),
            pltpu.VMEM((GROUPS * 48, 128), BF16),
            pltpu.VMEM((GROUPS * 48, 128), BF16),
            pltpu.VMEM((2 * GROUPS * 24, 128), F32),
            pltpu.VMEM((6, 128, 128), F32),
        ],
        compiler_params=pltpu.CompilerParams(vmem_limit_bytes=60 * 2**20),
        name="synthesis",
    )(m_blocks, coeffs, legendre)


def azimuth_kernel(blocks_ref, weights_ref, in_ref, table, out_ref, even_c, odd_c, even_s, odd_s, folded):
    starts = [pl.multiple_of(blocks_ref[p] * 16, 16) for p in range(16)]

    def basis(part, j):
        return jnp.concatenate([table[part, j, pl.ds(start, 16), :] for start in starts], axis=0)

    lane_group = lax.broadcasted_iota(jnp.int32, (24, 128), 1) // 32
    left = []
    for j in range(4):
        halves = []
        for h in range(2):
            parts = [in_ref[h * 4 + s, j].astype(F32) * (1.0 / 32.0) for s in range(4)]
            halves.append(swap_lane_groups(parts, lane_group))
        both = [jnp.concatenate([halves[0][n], halves[1][n]], axis=1) for n in range(4)]
        left.append([jnp.concatenate([both[part * 2], both[part * 2 + 1]], axis=0).astype(BF16) for part in range(2)])
    for part, refs in ((0, (even_c, odd_c)), (1, (even_s, odd_s))):
        for parity in range(2):
            refs[parity][...] = jnp.dot(
                left[parity][part], basis(part, parity), preferred_element_type=F32
            ) + jnp.dot(left[parity + 2][part], basis(part, parity + 2), preferred_element_type=F32)
    for x in range(QUARTER // 128):
        cols = slice(x * 128, (x + 1) * 128)
        fields = [[], [], [], []]
        for f in range(6):
            rows = slice(f * 8, (f + 1) * 8)
            ce, co, se, so = even_c[rows, cols], odd_c[rows, cols], even_s[rows, cols], odd_s[rows, cols]
            plus, minus = ce + co, ce - co
            total, other = se + so, se - so
            fields[0].append(plus - total)
            fields[1].append(plus + total)
            fields[2].append(minus + other)
            fields[3].append(minus - other)
        products = []
        for n in range(4):
            u0, u1, u2, b0, b1, b2 = fields[n]
            products.append(
                [
                    u1 * b2 - u2 * b1,
                    u2 * b0 - u0 * b2,
                    u0 * b1 - u1 * b0,
                    0.5 * (b0 * b0 + b1 * b1 + b2 * b2),
                ]
            )
        folds = [[], [], [], []]
        for g in range(4):
            p0, p1, p2, p3 = (products[n][g] for n in range(4))
            front, back = p0 + p1, p2 + p3
            left_odd, right_odd = p1 - p0, p2 - p3
            folds[0].append(front + back)
            folds[1].append(front - back)
            folds[2].append(left_odd + right_odd)
            folds[3].append(left_odd - right_odd)
        for n in range(4):
            folded[n, :, cols] = jnp.concatenate(folds[n], axis=0).astype(BF16)
    row = lax.broadcasted_iota(jnp.int32, (8, 1), 0) % 4
    own = lax.axis_index("ma")
    weight = jnp.zeros((8, 1), F32)
    for t in range(4):
        weight = jnp.where(row == t, weights_ref[t * 8 + own], weight)
    lane_group = lax.broadcasted_iota(jnp.int32, (8, 128), 1) // 32
    for j in range(4):
        terms = [
            lax.dot_general(
                folded[part * 2 + j % 2], basis(part, j), (((1,), (1,)), ((), ())), preferred_element_type=F32
            )
            for part in range(2)
        ]
        for gh in range(2):
            for h in range(2):
                parts = []
                for gl in range(2):
                    for part in range(2):
                        g = gh * 2 + gl
                        piece = terms[part][g * 8 : (g + 1) * 8, h * 128 : (h + 1) * 128]
                        parts.append((piece * (1.0 / math.sqrt(POINTS))) * weight)
                swapped = swap_lane_groups(parts, lane_group)
                for s in range(4):
                    where = (j * 2 + gh) * 8
                    out_ref[h * 4 + s, where : where + 8, :] = swapped[s].astype(BF16)


def azimuth(m_blocks, lat_weights, received, table):
    grid_shape = pltpu.VMEM((48, QUARTER), F32)
    return pl.pallas_call(
        azimuth_kernel,
        in_specs=[
            pl.BlockSpec(memory_space=pltpu.SMEM),
            pl.BlockSpec(memory_space=pltpu.SMEM),
            pl.BlockSpec(memory_space=pltpu.VMEM),
            pl.BlockSpec(memory_space=pltpu.VMEM),
        ],
        out_specs=pl.BlockSpec(memory_space=pltpu.VMEM),
        out_shape=jax.ShapeDtypeStruct((8, 64, 128), BF16),
        scratch_shapes=[
            grid_shape,
            grid_shape,
            grid_shape,
            grid_shape,
            pltpu.VMEM((4, 32, QUARTER), BF16),
        ],
        compiler_params=pltpu.CompilerParams(vmem_limit_bytes=32 * 2**20),
        name="azimuth",
    )(m_blocks, lat_weights, received, table)


def analysis_kernel(
    blocks_ref, own_ref, low_ref, high_ref, weights_hbm, plain_hbm, slope_hbm,
    weights, sem_w, placed, turned, terms, values_even, values_odd, out, sem_o,
):
    def fetch(s):
        return pltpu.make_async_copy(weights_hbm.at[s], weights.at[s], sem_w.at[s])

    def start(s, carry):
        fetch(s).start()
        return carry

    lax.fori_loop(0, SLOTS, start, 0)
    for n, ref in enumerate((own_ref, low_ref, high_ref)):
        for d in range(8):
            for j in range(4):
                for gh in range(2):
                    where = (j * 2 + gh) * 8
                    placed[n, pl.ds((gh * 4 + j) * 64 + d, 8, stride=8), :] = ref[d, where : where + 8, :].astype(F32)

    def pick(n, gh, j, i):
        return placed[n, (gh * 4 + j) * 64 + i * 32 : (gh * 4 + j) * 64 + (i + 1) * 32, :]

    for gh in range(2):
        columns = [[], [], [], []]
        for j in range(4):
            o0, o1 = pick(0, gh, j, 0), pick(0, gh, j, 1)
            l0, l1 = pick(1, gh, j, 0), pick(1, gh, j, 1)
            h0, h1 = pick(2, gh, j, 0), pick(2, gh, j, 1)
            columns[0].append(o0)
            columns[1].append(o1)
            columns[2].append((l0 - 8.0 * l1 + 8.0 * o1 - h0) / 12.0)
            columns[3].append((l1 - 8.0 * o0 + 8.0 * h0 - h1) / 12.0)
        for n in range(2):
            for i in range(2):
                block = jnp.concatenate(columns[n * 2 + i], axis=0)
                block = block.T
                for quad in range(4):
                    row = ((i * 2 + gh) * 4 + quad) * 40
                    turned[n, row : row + 32, :] = block[quad * 32 : (quad + 1) * 32]
    lower = lax.broadcasted_iota(jnp.int32, (32, 128), 1) < 64
    for qg in range(2 * GROUPS):
        pair = [turned[n, pl.ds(qg, 16, stride=40), :] for n in range(2)]
        both = jnp.concatenate(pair, axis=0)
        halves = [jnp.where(lower, both, 0.0), jnp.where(lower, 0.0, both)]
        terms[qg] = jnp.concatenate(halves, axis=0).astype(BF16)
    perm = lane_permutation(back=True)

    def send(s):
        return [
            pltpu.make_async_copy(out.at[s, n, i], ref.at[i, s], sem_o.at[s, n, i])
            for n, ref in enumerate((plain_hbm, slope_hbm))
            for i in range(2)
        ]

    def expand(s, values):
        base = own_block(blocks_ref, s) * GROUPS
        for g in range(GROUPS):
            value = lax.dot_general(
                terms[base + g], weights[s, g], (((1,), (1,)), ((), ())), preferred_element_type=F32
            )
            values[g * 32 : (g + 1) * 32, :] = jnp.concatenate([value[:32], value[32:]], axis=1).astype(BF16)

    def order(s, values):
        natural = jnp.dot(values[...], perm, preferred_element_type=F32).astype(BF16)
        for g in range(GROUPS):
            for n in range(2):
                for i in range(2):
                    row = g * 32 + n * 16 + i * 8
                    out[s, n, i, :, g * 256 : (g + 1) * 256] = natural[row : row + 8]

    def leave(s):
        for copy in send(s):
            copy.start()

    fetch(0).wait()
    expand(0, values_even)

    def pair(t, carry):
        fetch(2 * t + 1).wait()
        fetch(2 * t + 2).wait()
        expand(2 * t + 1, values_odd)
        order(2 * t, values_even)
        expand(2 * t + 2, values_even)
        order(2 * t + 1, values_odd)
        leave(2 * t)
        leave(2 * t + 1)
        return carry

    lax.fori_loop(0, SLOTS // 2, pair, 0)
    order(SLOTS - 1, values_even)
    leave(SLOTS - 1)

    def finish(s, carry):
        for copy in send(s):
            copy.wait()
        return carry

    lax.fori_loop(0, SLOTS, finish, 0)


def analysis(m_blocks, own, low, high, weights):
    shape = jax.ShapeDtypeStruct((2, SLOTS, 8, 4096), BF16)
    vmem = pl.BlockSpec(memory_space=pltpu.VMEM)
    hbm = pl.BlockSpec(memory_space=pltpu.HBM)
    return pl.pallas_call(
        analysis_kernel,
        in_specs=[pl.BlockSpec(memory_space=pltpu.SMEM), vmem, vmem, vmem, hbm],
        out_specs=[hbm, hbm],
        out_shape=[shape, shape],
        scratch_shapes=[
            pltpu.VMEM((SLOTS, GROUPS, 128, 128), BF16),
            pltpu.SemaphoreType.DMA((SLOTS,)),
            pltpu.VMEM((3, 512, 128), F32),
            pltpu.VMEM((2, 16 * 40, 128), F32),
            pltpu.VMEM((2 * GROUPS, 64, 128), BF16),
            pltpu.VMEM((GROUPS * 32, 256), BF16),
            pltpu.VMEM((GROUPS * 32, 256), BF16),
            pltpu.VMEM((SLOTS, 2, 2, 8, 4096), BF16),
            pltpu.SemaphoreType.DMA((SLOTS, 2, 2)),
        ],
        compiler_params=pltpu.CompilerParams(vmem_limit_bytes=60 * 2**20),
        name="analysis",
    )(m_blocks, own, low, high, weights)


def local(coeffs, legendre, lat_weights, m_blocks):
    table = jnp.asarray(quarter_table(), BF16)
    sent, weights = synthesis(m_blocks, coeffs.transpose(1, 2, 0, 3), legendre)
    received = lax.all_to_all(sent, "ma", split_axis=0, concat_axis=0, tiled=True)
    sent_back = azimuth(m_blocks, lat_weights, received, table)
    own = lax.all_to_all(sent_back, "ma", split_axis=0, concat_axis=0, tiled=True)
    count = lax.axis_size("row")
    low = lax.ppermute(own, "row", [(r, r + 1) for r in range(count - 1)])
    high = lax.ppermute(own, "row", [(r + 1, r) for r in range(count - 1)])
    plain, slope = analysis(m_blocks, own, low, high, weights)
    return plain.transpose(0, 2, 1, 3), slope.transpose(0, 2, 1, 3)


def solution(mesh):
    placed = (P("row", None, "ma", None), P("ma", None, None), P(), P())
    return jax.shard_map(
        local,
        mesh=mesh,
        in_specs=placed,
        out_specs=(P("row", None, "ma", None), P("row", None, "ma", None)),
        check_vma=False,
    )
```

```python
import functools
import math

import jax
import jax.numpy as jnp
import numpy as np
from jax import lax
from jax.experimental import pallas as pl
from jax.experimental.pallas import tpu as pltpu
from jax.sharding import PartitionSpec as P

F32, BF16 = jnp.float32, jnp.bfloat16
POINTS = 3072
QUARTER = POINTS // 4
SLOTS = 17
GROUPS = 16
SPAN = 16


def lane_permutation(back=False):
    natural = lax.broadcasted_iota(jnp.int32, (256, 256), 1 if back else 0)
    grouped = lax.broadcasted_iota(jnp.int32, (256, 256), 0 if back else 1)
    target = natural // 64 * 64 + natural % 4 * 16 + natural % 64 // 4
    return (target == grouped).astype(F32).astype(BF16)


def lane_masks():
    group = lax.broadcasted_iota(jnp.int32, (16, 128), 1) // 32
    return [(group == j).astype(F32).astype(BF16) for j in range(4)]


def quarter_table():
    j = np.arange(4)[:, None, None, None]
    b = np.arange(16)[None, :, None, None]
    g = np.arange(16)[None, None, :, None]
    x = np.arange(QUARTER)[None, None, None, :]
    order = b * 64 + g * 4 + j
    turns = (order * (2 * x + 1)) % (2 * POINTS)
    angles = turns * (math.pi / POINTS)
    table = np.stack([np.cos(angles), np.sin(angles)])
    return table.reshape(2, 4, 256, QUARTER)


def own_block(blocks_ref, s):
    lead = blocks_ref[2 * lax.axis_index("ma")]
    return (s >= SPAN - lead).astype(jnp.int32)


def spread_rows(table, chunks):
    for c in range(16):
        chunks[c * 72 : c * 72 + 64, :] = table[:, c * 128 : (c + 1) * 128].astype(F32)


def group_rows(chunks, g):
    pieces = [chunks[pl.ds(g * 4 + j, 16, stride=72), :] for j in range(4)]
    return jnp.concatenate(pieces, axis=0).astype(BF16)


def block_weights(rows, masks):
    rolled = [rows] + [pltpu.roll(rows, 32 * r, 1) for r in (1, 2, 3)]
    pieces = []
    for j in range(2):
        for a in range(4):
            first, second = j, 2 + j
            pieces.append(
                rolled[(first - a) % 4][first * 16 : (first + 1) * 16] * masks[first]
                + rolled[(second - a) % 4][second * 16 : (second + 1) * 16] * masks[second]
            )
    return jnp.concatenate(pieces, axis=0)


def swap_lane_groups(parts, lane_group):
    results = []
    for a in range(4):
        value = None
        for s in range(4):
            shift = (s - a) % 4
            moved = pltpu.roll(parts[s], 32 * shift, 1) if shift else parts[s]
            value = moved if value is None else jnp.where(lane_group == s, moved, value)
        results.append(value)
    return results


def synth_kernel(
    blocks_ref, coef_hbm, leg_hbm, out_ref, weights_hbm,
    coef, leg, sem_c, sem_l, sem_w, chunks_even, chunks_odd, weights_even, weights_odd, values_even, values_odd, acc, turned,
):
    def fetch(s):
        return (
            pltpu.make_async_copy(leg_hbm.at[s], leg.at[s], sem_l.at[s]),
            pltpu.make_async_copy(coef_hbm.at[:, s], coef.at[s], sem_c.at[s]),
        )

    def start(s, carry):
        for copy in fetch(s):
            copy.start()
        return carry

    lax.fori_loop(0, SLOTS, start, 0)
    acc[...] = jnp.zeros_like(acc)
    masks = lane_masks()
    perm = lane_permutation()
    lower = lax.broadcasted_iota(jnp.int32, (24, 128), 1) < 64

    def prepare(s, chunks, weights, values):
        spread_rows(leg.at[s], chunks)
        for g in range(GROUPS):
            weights[g] = block_weights(group_rows(chunks, g), masks)
        rows = jnp.concatenate(
            [coef[s, :, :, g * 256 : (g + 1) * 256].reshape(24, 256) for g in range(GROUPS)], axis=0
        )
        rows = jnp.dot(rows, perm, preferred_element_type=F32)
        for g in range(GROUPS):
            part = rows[g * 24 : (g + 1) * 24]
            values[g * 48 : (g + 1) * 48, :] = jnp.concatenate([part[:, :128], part[:, 128:]], axis=0).astype(BF16)

    def combine(s, weights, values):
        base = own_block(blocks_ref, s) * (GROUPS * 24)
        for g in range(GROUPS):
            term = jnp.dot(values[g * 48 : (g + 1) * 48, :], weights[g], preferred_element_type=F32)
            where = pl.ds(pl.multiple_of(base + g * 24, 8), 24)
            acc[where, :] = acc[where, :] + jnp.where(lower, term[:24], term[24:])

    def arrive(s):
        for copy in fetch(s):
            copy.wait()

    def keep_even(t):
        return pltpu.make_async_copy(weights_even.at[t], weights_hbm.at[2 * t], sem_w.at[2 * t])

    def keep_odd(t):
        return pltpu.make_async_copy(weights_odd.at[t], weights_hbm.at[2 * t + 1], sem_w.at[2 * t + 1])

    arrive(0)
    prepare(0, chunks_even, weights_even.at[0], values_even)

    def pair(t, carry):
        keep_even(t).start()
        arrive(2 * t + 1)
        arrive(2 * t + 2)
        prepare(2 * t + 1, chunks_odd, weights_odd.at[t], values_odd)
        combine(2 * t, weights_even.at[t], values_even)
        prepare(2 * t + 2, chunks_even, weights_even.at[t + 1], values_even)
        combine(2 * t + 1, weights_odd.at[t], values_odd)
        keep_odd(t).start()
        return carry

    lax.fori_loop(0, SLOTS // 2, pair, 0)
    last = SLOTS // 2
    keep_even(last).start()
    combine(SLOTS - 1, weights_even.at[last], values_even)
    for comp in range(3):
        for i in range(2):
            parts = []
            for part in range(2):
                for vm in range(2):
                    row = ((vm * 3 + comp) * 2 + part) * 2 + i
                    parts.append(acc[pl.ds(row, 2 * GROUPS, stride=24), :])
            turned[comp * 2 + i] = jnp.concatenate(parts, axis=0).T
    for d in range(8):
        for j in range(4):
            pieces = [turned[n, pl.ds(j * 32 + d, 4, stride=8), :] for n in range(6)]
            out_ref[d, j] = jnp.concatenate(pieces, axis=0).astype(BF16)

    def finish(t, carry):
        keep_even(t).wait()
        keep_odd(t).wait()
        return carry

    lax.fori_loop(0, last, finish, 0)
    keep_even(last).wait()


def in_hbm(x):
    return pltpu.with_memory_space_constraint(x, pltpu.HBM)


def synthesis(m_blocks, coeffs, legendre):
    return pl.pallas_call(
        synth_kernel,
        in_specs=[
            pl.BlockSpec(memory_space=pltpu.SMEM),
            pl.BlockSpec(memory_space=pltpu.HBM),
            pl.BlockSpec(memory_space=pltpu.HBM),
        ],
        out_specs=[pl.BlockSpec(memory_space=pltpu.VMEM), pl.BlockSpec(memory_space=pltpu.HBM)],
        out_shape=[
            jax.ShapeDtypeStruct((8, 4, 24, 128), BF16),
            pltpu.HBM((SLOTS, GROUPS, 128, 128), BF16),
        ],
        scratch_shapes=[
            pltpu.VMEM((SLOTS, 12, 2, 4096), BF16),
            pltpu.VMEM((SLOTS, 64, 2048), BF16),
            pltpu.SemaphoreType.DMA((SLOTS,)),
            pltpu.SemaphoreType.DMA((SLOTS,)),
            pltpu.SemaphoreType.DMA((SLOTS,)),
            pltpu.VMEM((16 * 72, 128), F32),
            pltpu.VMEM((16 * 72, 128), F32),
            pltpu.VMEM((SLOTS // 2 + 1, GROUPS, 128, 128), BF16),
            pltpu.VMEM((SLOTS // 2, GROUPS, 128, 128), BF16),
            pltpu.VMEM((GROUPS * 48, 128), BF16),
            pltpu.VMEM((GROUPS * 48, 128), BF16),
            pltpu.VMEM((2 * GROUPS * 24, 128), F32),
            pltpu.VMEM((6, 128, 128), F32),
        ],
        compiler_params=pltpu.CompilerParams(vmem_limit_bytes=60 * 2**20),
        name="synthesis",
    )(m_blocks, in_hbm(coeffs), in_hbm(legendre))


def azimuth_kernel(blocks_ref, weights_ref, in_ref, table, out_ref, even_c, odd_c, even_s, odd_s, folded):
    starts = [pl.multiple_of(blocks_ref[p] * 16, 16) for p in range(16)]

    def basis(part, j):
        return jnp.concatenate([table[part, j, pl.ds(start, 16), :] for start in starts], axis=0)

    lane_group = lax.broadcasted_iota(jnp.int32, (24, 128), 1) // 32
    left = []
    for j in range(4):
        halves = []
        for h in range(2):
            parts = [in_ref[h * 4 + s, j].astype(F32) * (1.0 / 32.0) for s in range(4)]
            halves.append(swap_lane_groups(parts, lane_group))
        both = [jnp.concatenate([halves[0][n], halves[1][n]], axis=1) for n in range(4)]
        left.append([jnp.concatenate([both[part * 2], both[part * 2 + 1]], axis=0).astype(BF16) for part in range(2)])
    for part, refs in ((0, (even_c, odd_c)), (1, (even_s, odd_s))):
        for parity in range(2):
            refs[parity][...] = jnp.dot(
                left[parity][part], basis(part, parity), preferred_element_type=F32
            ) + jnp.dot(left[parity + 2][part], basis(part, parity + 2), preferred_element_type=F32)
    for x in range(QUARTER // 128):
        cols = slice(x * 128, (x + 1) * 128)
        fields = [[], [], [], []]
        for f in range(6):
            rows = slice(f * 8, (f + 1) * 8)
            ce, co, se, so = even_c[rows, cols], odd_c[rows, cols], even_s[rows, cols], odd_s[rows, cols]
            plus, minus = ce + co, ce - co
            total, other = se + so, se - so
            fields[0].append(plus - total)
            fields[1].append(plus + total)
            fields[2].append(minus + other)
            fields[3].append(minus - other)
        products = []
        for n in range(4):
            u0, u1, u2, b0, b1, b2 = fields[n]
            products.append(
                [
                    u1 * b2 - u2 * b1,
                    u2 * b0 - u0 * b2,
                    u0 * b1 - u1 * b0,
                    0.5 * (b0 * b0 + b1 * b1 + b2 * b2),
                ]
            )
        folds = [[], [], [], []]
        for g in range(4):
            p0, p1, p2, p3 = (products[n][g] for n in range(4))
            front, back = p0 + p1, p2 + p3
            left_odd, right_odd = p1 - p0, p2 - p3
            folds[0].append(front + back)
            folds[1].append(front - back)
            folds[2].append(left_odd + right_odd)
            folds[3].append(left_odd - right_odd)
        for n in range(4):
            folded[n, :, cols] = jnp.concatenate(folds[n], axis=0).astype(BF16)
    row = lax.broadcasted_iota(jnp.int32, (8, 1), 0) % 4
    own = lax.axis_index("ma")
    weight = jnp.zeros((8, 1), F32)
    for t in range(4):
        weight = jnp.where(row == t, weights_ref[t * 8 + own], weight)
    lane_group = lax.broadcasted_iota(jnp.int32, (8, 128), 1) // 32
    for j in range(4):
        terms = [
            lax.dot_general(
                folded[part * 2 + j % 2], basis(part, j), (((1,), (1,)), ((), ())), preferred_element_type=F32
            )
            for part in range(2)
        ]
        for gh in range(2):
            for h in range(2):
                parts = []
                for gl in range(2):
                    for part in range(2):
                        g = gh * 2 + gl
                        piece = terms[part][g * 8 : (g + 1) * 8, h * 128 : (h + 1) * 128]
                        parts.append((piece * (1.0 / math.sqrt(POINTS))) * weight)
                swapped = swap_lane_groups(parts, lane_group)
                for s in range(4):
                    where = (j * 2 + gh) * 8
                    out_ref[h * 4 + s, where : where + 8, :] = swapped[s].astype(BF16)


def azimuth(m_blocks, lat_weights, received, table):
    grid_shape = pltpu.VMEM((48, QUARTER), F32)
    return pl.pallas_call(
        azimuth_kernel,
        in_specs=[
            pl.BlockSpec(memory_space=pltpu.SMEM),
            pl.BlockSpec(memory_space=pltpu.SMEM),
            pl.BlockSpec(memory_space=pltpu.VMEM),
            pl.BlockSpec(memory_space=pltpu.VMEM),
        ],
        out_specs=pl.BlockSpec(memory_space=pltpu.VMEM),
        out_shape=jax.ShapeDtypeStruct((8, 64, 128), BF16),
        scratch_shapes=[
            grid_shape,
            grid_shape,
            grid_shape,
            grid_shape,
            pltpu.VMEM((4, 32, QUARTER), BF16),
        ],
        compiler_params=pltpu.CompilerParams(vmem_limit_bytes=32 * 2**20),
        name="azimuth",
    )(m_blocks, lat_weights, received, table)


def turn_kernel(first, weights_hbm, out_hbm, weights, turned, sem_in, sem_out):
    count = turned.shape[0]

    def fetch(s):
        return pltpu.make_async_copy(weights_hbm.at[first + s], weights.at[s], sem_in.at[s])

    def leave(s):
        return pltpu.make_async_copy(turned.at[s], out_hbm.at[s], sem_out.at[s])

    def start(s, carry):
        fetch(s).start()
        return carry

    lax.fori_loop(0, count, start, 0)
    perm = lane_permutation(back=True)[:128, :128]

    def slot(s, carry):
        fetch(s).wait()
        for g in range(0, GROUPS, 2):
            one, two = weights[s, g], weights[s, g + 1]
            both = jnp.concatenate(
                [one[:64] + pltpu.roll(two[:64], 32, 1), pltpu.roll(one[64:], 96, 1) + two[64:]], axis=0
            )
            both = lax.dot_general(both, perm, (((0,), (0,)), ((), ())), preferred_element_type=F32)
            for n in range(2):
                rows = [both[(u * 2 + n) * 32 : (u * 2 + n + 1) * 32] for u in range(2)]
                turned[s, g + n] = jnp.concatenate(rows, axis=0).astype(BF16)
        leave(s).start()
        return carry

    lax.fori_loop(0, count, slot, 0)

    def finish(s, carry):
        leave(s).wait()
        return carry

    lax.fori_loop(0, count, finish, 0)


def turn(weights, first, count):
    shape = (count, GROUPS, 64, 128)
    return pl.pallas_call(
        functools.partial(turn_kernel, first),
        in_specs=[pl.BlockSpec(memory_space=pltpu.HBM)],
        out_specs=pl.BlockSpec(memory_space=pltpu.HBM),
        out_shape=pltpu.HBM(shape, BF16),
        scratch_shapes=[
            pltpu.VMEM((count, GROUPS, 128, 128), BF16),
            pltpu.VMEM(shape, BF16),
            pltpu.SemaphoreType.DMA((count,)),
            pltpu.SemaphoreType.DMA((count,)),
        ],
        compiler_params=pltpu.CompilerParams(vmem_limit_bytes=32 * 2**20),
        cost_estimate=pl.CostEstimate(
            flops=2 * count * GROUPS * 128**3, bytes_accessed=4 * count * GROUPS * 128**2, transcendentals=0
        ),
        name="turn",
    )(in_hbm(weights))


def analysis_kernel(
    blocks_ref, *refs, count,
):
    messages = refs[:count]
    first_hbm, second_hbm, out_hbm, weights, sem_w, placed, turned, terms, out, sem_o = refs[count:]
    split = first_hbm.shape[0]

    def fetch(s, source):
        return pltpu.make_async_copy(source, weights.at[s], sem_w.at[s])

    def start_first(s, carry):
        fetch(s, first_hbm.at[s]).start()
        return carry

    def start_second(s, carry):
        fetch(split + s, second_hbm.at[s]).start()
        return carry

    lax.fori_loop(0, split, start_first, 0)
    lax.fori_loop(0, SLOTS - split, start_second, 0)
    for n, ref in enumerate(messages):
        for d in range(8):
            for j in range(4):
                for gh in range(2):
                    where = (j * 2 + gh) * 8
                    placed[n, pl.ds((gh * 4 + j) * 64 + d, 8, stride=8), :] = ref[d, where : where + 8, :].astype(F32)

    def pick(n, gh, j, i):
        return placed[n, (gh * 4 + j) * 64 + i * 32 : (gh * 4 + j) * 64 + (i + 1) * 32, :]

    row = lax.axis_index("row")
    has_low, has_high = row > 0, row < lax.axis_size("row") - 1

    def shells(gh, j):
        own = [pick(0, gh, j, i) for i in range(2)]
        if count == 1:
            return own
        low = [jnp.where(has_low, pick(1, gh, j, i), 0.0) for i in range(2)]
        high = [jnp.where(has_high, pick(2, gh, j, i), 0.0) for i in range(2)]
        return [
            (low[0] - 8.0 * low[1] + 8.0 * own[1] - high[0]) / 12.0,
            (low[1] - 8.0 * own[0] + 8.0 * high[0] - high[1]) / 12.0,
        ]

    for gh in range(2):
        columns = [shells(gh, j) for j in range(4)]
        for i in range(2):
            block = jnp.concatenate([columns[j][i] for j in range(4)], axis=0).T
            for quad in range(4):
                where = ((i * 2 + gh) * 4 + quad) * 40
                turned[where : where + 32, :] = block[quad * 32 : (quad + 1) * 32]
    lower = lax.broadcasted_iota(jnp.int32, (16, 128), 1) < 64
    for qg in range(2 * GROUPS):
        both = turned[pl.ds(qg, 16, stride=40), :]
        halves = [jnp.where(lower, both, 0.0), jnp.where(lower, 0.0, both)]
        terms[qg] = jnp.concatenate(halves, axis=0).astype(BF16)

    def send(s):
        return [pltpu.make_async_copy(out.at[s, i], out_hbm.at[i, s], sem_o.at[s, i]) for i in range(2)]

    group = lax.broadcasted_iota(jnp.int32, (32, 128), 1) // 64
    halves = [(group == j).astype(F32).astype(BF16) for j in range(2)]

    def slot(s):
        base = own_block(blocks_ref, s) * GROUPS
        for g in range(GROUPS):
            narrow = weights[s, g]
            blocks = [narrow[u * 32 : (u + 1) * 32] * halves[j] for u in range(2) for j in range(2)]
            value = jnp.dot(terms[base + g], jnp.concatenate(blocks, axis=0), preferred_element_type=F32)
            value = jnp.concatenate([value[:16], value[16:]], axis=1).astype(BF16)
            for i in range(2):
                out[s, i, :, g * 256 : (g + 1) * 256] = value[i * 8 : (i + 1) * 8]

    def arrive(s):
        fetch(s, first_hbm.at[0]).wait()

    def leave(s):
        for copy in send(s):
            copy.start()

    def pair(t, carry):
        arrive(2 * t)
        arrive(2 * t + 1)
        slot(2 * t)
        slot(2 * t + 1)
        leave(2 * t)
        leave(2 * t + 1)
        return carry

    lax.fori_loop(0, SLOTS // 2, pair, 0)
    arrive(SLOTS - 1)
    slot(SLOTS - 1)
    leave(SLOTS - 1)

    def finish(s, carry):
        for copy in send(s):
            copy.wait()
        return carry

    lax.fori_loop(0, SLOTS, finish, 0)


def analysis(name, m_blocks, messages, first, second):
    vmem = pl.BlockSpec(memory_space=pltpu.VMEM)
    hbm = pl.BlockSpec(memory_space=pltpu.HBM)
    count = len(messages)
    return pl.pallas_call(
        functools.partial(analysis_kernel, count=count),
        in_specs=[pl.BlockSpec(memory_space=pltpu.SMEM)] + [vmem] * count + [hbm, hbm],
        out_specs=hbm,
        out_shape=jax.ShapeDtypeStruct((2, SLOTS, 8, 4096), BF16),
        scratch_shapes=[
            pltpu.VMEM((SLOTS, GROUPS, 64, 128), BF16),
            pltpu.SemaphoreType.DMA((SLOTS,)),
            pltpu.VMEM((count, 512, 128), F32),
            pltpu.VMEM((16 * 40, 128), F32),
            pltpu.VMEM((2 * GROUPS, 32, 128), BF16),
            pltpu.VMEM((SLOTS, 2, 8, 4096), BF16),
            pltpu.SemaphoreType.DMA((SLOTS, 2)),
        ],
        compiler_params=pltpu.CompilerParams(vmem_limit_bytes=24 * 2**20),
        cost_estimate=pl.CostEstimate(
            flops=2 * SLOTS * GROUPS * 32 * 128**2, bytes_accessed=12 * 2**20, transcendentals=0
        ),
        name=name,
    )(m_blocks, *messages, in_hbm(first), in_hbm(second))


def local(coeffs, legendre, lat_weights, m_blocks):
    table = jnp.asarray(quarter_table(), BF16)
    sent, weights = synthesis(m_blocks, coeffs.transpose(1, 2, 0, 3), legendre)
    first = turn(weights, 0, 9)
    received = lax.all_to_all(sent, "ma", split_axis=0, concat_axis=0, tiled=True)
    received, first, weights = lax.optimization_barrier((received, first, weights))
    sent_back = azimuth(m_blocks, lat_weights, received, table)
    sent_back, weights = lax.optimization_barrier((sent_back, weights))
    second = turn(weights, 9, 8)
    own = lax.all_to_all(sent_back, "ma", split_axis=0, concat_axis=0, tiled=True)
    own, second = lax.optimization_barrier((own, second))
    count = lax.axis_size("row")
    low = lax.ppermute(own, "row", [(r, (r + 1) % count) for r in range(count)])
    high = lax.ppermute(own, "row", [((r + 1) % count, r) for r in range(count)])
    plain = analysis("plain", m_blocks, [own], first, second)
    slope = analysis("slope", m_blocks, [own, low, high], first, second)
    return plain.transpose(0, 2, 1, 3), slope.transpose(0, 2, 1, 3)


def solution(mesh):
    placed = (P("row", None, "ma", None), P("ma", None, None), P(), P())
    return jax.shard_map(
        local,
        mesh=mesh,
        in_specs=placed,
        out_specs=(P("row", None, "ma", None), P("row", None, "ma", None)),
        check_vma=False,
    )
```

```python
import functools
import math

import jax
import jax.numpy as jnp
import numpy as np
from jax import lax
from jax.experimental import pallas as pl
from jax.experimental.pallas import tpu as pltpu
from jax.sharding import PartitionSpec as P

F32, BF16 = jnp.float32, jnp.bfloat16
POINTS = 3072
QUARTER = POINTS // 4
SLOTS = 17
GROUPS = 16
SPAN = 16
BATCHES = ((0, 1), (1, 2), (3, 6), (9, 8))


def lane_permutation(back=False):
    natural = lax.broadcasted_iota(jnp.int32, (256, 256), 1 if back else 0)
    grouped = lax.broadcasted_iota(jnp.int32, (256, 256), 0 if back else 1)
    target = natural // 64 * 64 + natural % 4 * 16 + natural % 64 // 4
    return (target == grouped).astype(F32).astype(BF16)


def lane_masks():
    group = lax.broadcasted_iota(jnp.int32, (16, 128), 1) // 32
    return [(group == j).astype(F32).astype(BF16) for j in range(4)]


def quarter_table():
    j = np.arange(4)[:, None, None, None]
    b = np.arange(16)[None, :, None, None]
    g = np.arange(16)[None, None, :, None]
    x = np.arange(QUARTER)[None, None, None, :]
    order = b * 64 + g * 4 + j
    turns = (order * (2 * x + 1)) % (2 * POINTS)
    angles = turns * (math.pi / POINTS)
    table = np.stack([np.cos(angles), np.sin(angles)])
    return table.reshape(2, 4, 256, QUARTER)


def own_block(blocks_ref, s):
    lead = blocks_ref[2 * lax.axis_index("ma")]
    return (s >= SPAN - lead).astype(jnp.int32)


def spread_rows(table, chunks):
    for c in range(16):
        chunks[c * 72 : c * 72 + 64, :] = table[:, c * 128 : (c + 1) * 128].astype(F32)


def group_rows(chunks, g):
    pieces = [chunks[pl.ds(g * 4 + j, 16, stride=72), :] for j in range(4)]
    return jnp.concatenate(pieces, axis=0).astype(BF16)


def block_weights(rows, masks):
    rolled = [rows] + [pltpu.roll(rows, 32 * r, 1) for r in (1, 2, 3)]
    pieces = []
    for j in range(2):
        for a in range(4):
            first, second = j, 2 + j
            pieces.append(
                rolled[(first - a) % 4][first * 16 : (first + 1) * 16] * masks[first]
                + rolled[(second - a) % 4][second * 16 : (second + 1) * 16] * masks[second]
            )
    return jnp.concatenate(pieces, axis=0)


def swap_lane_groups(parts, lane_group):
    results = []
    for a in range(4):
        value = None
        for s in range(4):
            shift = (s - a) % 4
            moved = pltpu.roll(parts[s], 32 * shift, 1) if shift else parts[s]
            value = moved if value is None else jnp.where(lane_group == s, moved, value)
        results.append(value)
    return results


def synth_kernel(
    blocks_hbm, coef_hbm, leg_hbm, out_ref, weights_hbm,
    blocks_ref, sem_b, coef, leg, sem_c, sem_l, sem_w, chunks_even, chunks_odd, weights_even, weights_odd, values_even, values_odd, acc, turned,
):
    def fetch(n):
        first, count = BATCHES[n]
        slots = pl.ds(first, count)
        return (
            pltpu.make_async_copy(leg_hbm.at[slots], leg.at[slots], sem_l.at[n]),
            pltpu.make_async_copy(coef_hbm.at[:, slots], coef.at[:, slots], sem_c.at[n]),
        )

    for n in range(len(BATCHES)):
        for copy in fetch(n):
            copy.start()
    order = pltpu.make_async_copy(blocks_hbm, blocks_ref, sem_b)
    order.start()
    acc[...] = jnp.zeros_like(acc)
    masks = lane_masks()
    perm = lane_permutation()
    lower = lax.broadcasted_iota(jnp.int32, (24, 128), 1) < 64

    def prepare(s, chunks, weights, values):
        spread_rows(leg.at[s], chunks)
        for g in range(GROUPS):
            weights[g] = block_weights(group_rows(chunks, g), masks)
        rows = jnp.concatenate(
            [coef[:, s, :, g * 256 : (g + 1) * 256].reshape(24, 256) for g in range(GROUPS)], axis=0
        )
        rows = jnp.dot(rows, perm, preferred_element_type=F32)
        for g in range(GROUPS):
            part = rows[g * 24 : (g + 1) * 24]
            values[g * 48 : (g + 1) * 48, :] = jnp.concatenate([part[:, :128], part[:, 128:]], axis=0).astype(BF16)

    def combine(s, weights, values):
        base = own_block(blocks_ref, s) * (GROUPS * 24)
        for g in range(GROUPS):
            term = jnp.dot(values[g * 48 : (g + 1) * 48, :], weights[g], preferred_element_type=F32)
            where = pl.ds(pl.multiple_of(base + g * 24, 8), 24)
            acc[where, :] = acc[where, :] + jnp.where(lower, term[:24], term[24:])

    def arrive(n):
        for copy in fetch(n):
            copy.wait()

    def keep_even(t):
        return pltpu.make_async_copy(weights_even.at[t], weights_hbm.at[2 * t], sem_w.at[2 * t])

    def keep_odd(t):
        return pltpu.make_async_copy(weights_odd.at[t], weights_hbm.at[2 * t + 1], sem_w.at[2 * t + 1])

    arrive(0)
    order.wait()
    prepare(0, chunks_even, weights_even.at[0], values_even)

    def pair(t, carry):
        keep_even(t).start()
        for n in range(1, len(BATCHES)):
            pl.when(2 * t + 1 == BATCHES[n][0])(functools.partial(arrive, n))
        prepare(2 * t + 1, chunks_odd, weights_odd.at[t], values_odd)
        combine(2 * t, weights_even.at[t], values_even)
        prepare(2 * t + 2, chunks_even, weights_even.at[t + 1], values_even)
        combine(2 * t + 1, weights_odd.at[t], values_odd)
        keep_odd(t).start()
        return carry

    lax.fori_loop(0, SLOTS // 2, pair, 0)
    last = SLOTS // 2
    keep_even(last).start()
    combine(SLOTS - 1, weights_even.at[last], values_even)
    for comp in range(3):
        for i in range(2):
            parts = []
            for part in range(2):
                for vm in range(2):
                    row = ((vm * 3 + comp) * 2 + part) * 2 + i
                    parts.append(acc[pl.ds(row, 2 * GROUPS, stride=24), :])
            turned[comp * 2 + i] = jnp.concatenate(parts, axis=0).T
    for d in range(8):
        for j in range(4):
            pieces = [turned[n, pl.ds(j * 32 + d, 4, stride=8), :] for n in range(6)]
            out_ref[d, j] = jnp.concatenate(pieces, axis=0).astype(BF16)

    def finish(t, carry):
        keep_even(t).wait()
        keep_odd(t).wait()
        return carry

    lax.fori_loop(0, last, finish, 0)
    keep_even(last).wait()


def in_hbm(x):
    return pltpu.with_memory_space_constraint(x, pltpu.HBM)


def synthesis(m_blocks, coeffs, legendre):
    return pl.pallas_call(
        synth_kernel,
        in_specs=[pl.BlockSpec(memory_space=pltpu.HBM)] * 3,
        out_specs=[pl.BlockSpec(memory_space=pltpu.VMEM), pl.BlockSpec(memory_space=pltpu.HBM)],
        out_shape=[
            jax.ShapeDtypeStruct((8, 4, 24, 128), BF16),
            pltpu.HBM((SLOTS, GROUPS, 128, 128), BF16),
        ],
        scratch_shapes=[
            pltpu.SMEM((16,), jnp.int32),
            pltpu.SemaphoreType.DMA,
            pltpu.VMEM((12, SLOTS, 2, 4096), BF16),
            pltpu.VMEM((SLOTS, 64, 2048), BF16),
            pltpu.SemaphoreType.DMA((len(BATCHES),)),
            pltpu.SemaphoreType.DMA((len(BATCHES),)),
            pltpu.SemaphoreType.DMA((SLOTS,)),
            pltpu.VMEM((16 * 72, 128), F32),
            pltpu.VMEM((16 * 72, 128), F32),
            pltpu.VMEM((SLOTS // 2 + 1, GROUPS, 128, 128), BF16),
            pltpu.VMEM((SLOTS // 2, GROUPS, 128, 128), BF16),
            pltpu.VMEM((GROUPS * 48, 128), BF16),
            pltpu.VMEM((GROUPS * 48, 128), BF16),
            pltpu.VMEM((2 * GROUPS * 24, 128), F32),
            pltpu.VMEM((6, 128, 128), F32),
        ],
        compiler_params=pltpu.CompilerParams(vmem_limit_bytes=60 * 2**20),
        name="synthesis",
    )(in_hbm(m_blocks), in_hbm(coeffs), in_hbm(legendre))


def azimuth_kernel(blocks_ref, weights_ref, in_ref, table, out_ref, even_c, odd_c, even_s, odd_s, folded):
    lane_group = lax.broadcasted_iota(jnp.int32, (24, 128), 1) // 32
    left = []
    for j in range(4):
        halves = []
        for h in range(2):
            parts = [in_ref[h * 4 + s, j].astype(F32) * (1.0 / 32.0) for s in range(4)]
            halves.append(swap_lane_groups(parts, lane_group))
        both = [jnp.concatenate([halves[0][n], halves[1][n]], axis=1) for n in range(4)]
        left.append([jnp.concatenate([both[part * 2], both[part * 2 + 1]], axis=0).astype(BF16) for part in range(2)])
    starts = [pl.multiple_of(blocks_ref[p] * 16, 16) for p in range(16)]

    def basis(part, j):
        return jnp.concatenate([table[part, j, pl.ds(start, 16), :] for start in starts], axis=0)

    for part, refs in ((0, (even_c, odd_c)), (1, (even_s, odd_s))):
        for parity in range(2):
            refs[parity][...] = jnp.dot(
                left[parity][part], basis(part, parity), preferred_element_type=F32
            ) + jnp.dot(left[parity + 2][part], basis(part, parity + 2), preferred_element_type=F32)
    for x in range(QUARTER // 128):
        cols = slice(x * 128, (x + 1) * 128)
        fields = [[], [], [], []]
        for f in range(6):
            rows = slice(f * 8, (f + 1) * 8)
            ce, co, se, so = even_c[rows, cols], odd_c[rows, cols], even_s[rows, cols], odd_s[rows, cols]
            plus, minus = ce + co, ce - co
            total, other = se + so, se - so
            fields[0].append(plus - total)
            fields[1].append(plus + total)
            fields[2].append(minus + other)
            fields[3].append(minus - other)
        products = []
        for n in range(4):
            u0, u1, u2, b0, b1, b2 = fields[n]
            products.append(
                [
                    u1 * b2 - u2 * b1,
                    u2 * b0 - u0 * b2,
                    u0 * b1 - u1 * b0,
                    0.5 * (b0 * b0 + b1 * b1 + b2 * b2),
                ]
            )
        folds = [[], [], [], []]
        for g in range(4):
            p0, p1, p2, p3 = (products[n][g] for n in range(4))
            front, back = p0 + p1, p2 + p3
            left_odd, right_odd = p1 - p0, p2 - p3
            folds[0].append(front + back)
            folds[1].append(front - back)
            folds[2].append(left_odd + right_odd)
            folds[3].append(left_odd - right_odd)
        for n in range(4):
            folded[n, :, cols] = jnp.concatenate(folds[n], axis=0).astype(BF16)
    row = lax.broadcasted_iota(jnp.int32, (8, 1), 0) % 4
    own = lax.axis_index("ma")
    weight = jnp.zeros((8, 1), F32)
    for t in range(4):
        weight = jnp.where(row == t, weights_ref[t * 8 + own], weight)
    lane_group = lax.broadcasted_iota(jnp.int32, (8, 128), 1) // 32
    for j in range(4):
        terms = [
            lax.dot_general(
                folded[part * 2 + j % 2], basis(part, j), (((1,), (1,)), ((), ())), preferred_element_type=F32
            )
            for part in range(2)
        ]
        for gh in range(2):
            for h in range(2):
                parts = []
                for gl in range(2):
                    for part in range(2):
                        g = gh * 2 + gl
                        piece = terms[part][g * 8 : (g + 1) * 8, h * 128 : (h + 1) * 128]
                        parts.append((piece * (1.0 / math.sqrt(POINTS))) * weight)
                swapped = swap_lane_groups(parts, lane_group)
                for s in range(4):
                    where = (j * 2 + gh) * 8
                    out_ref[h * 4 + s, where : where + 8, :] = swapped[s].astype(BF16)


def azimuth(m_blocks, lat_weights, received, table):
    grid_shape = pltpu.VMEM((48, QUARTER), F32)
    return pl.pallas_call(
        azimuth_kernel,
        in_specs=[pl.BlockSpec(memory_space=pltpu.SMEM)] * 2 + [pl.BlockSpec(memory_space=pltpu.VMEM)] * 2,
        out_specs=pl.BlockSpec(memory_space=pltpu.VMEM),
        out_shape=jax.ShapeDtypeStruct((8, 64, 128), BF16),
        scratch_shapes=[
            grid_shape,
            grid_shape,
            grid_shape,
            grid_shape,
            pltpu.VMEM((4, 32, QUARTER), BF16),
        ],
        compiler_params=pltpu.CompilerParams(vmem_limit_bytes=32 * 2**20),
        name="azimuth",
    )(m_blocks, lat_weights, received, table)


def turn_kernel(first, weights_hbm, out_hbm, weights, turned, sem_in, sem_out):
    count = turned.shape[0]

    def fetch(s):
        return pltpu.make_async_copy(weights_hbm.at[first + s], weights.at[s], sem_in.at[s])

    def leave(s):
        return pltpu.make_async_copy(turned.at[s], out_hbm.at[s], sem_out.at[s])

    def start(s, carry):
        fetch(s).start()
        return carry

    lax.fori_loop(0, count, start, 0)
    perm = lane_permutation(back=True)[:128, :128]

    def slot(s, carry):
        fetch(s).wait()
        for g in range(0, GROUPS, 2):
            one, two = weights[s, g], weights[s, g + 1]
            both = jnp.concatenate(
                [one[:64] + pltpu.roll(two[:64], 32, 1), pltpu.roll(one[64:], 96, 1) + two[64:]], axis=0
            )
            both = lax.dot_general(both, perm, (((0,), (0,)), ((), ())), preferred_element_type=F32)
            for n in range(2):
                rows = [both[(u * 2 + n) * 32 : (u * 2 + n + 1) * 32] for u in range(2)]
                turned[s, g + n] = jnp.concatenate(rows, axis=0).astype(BF16)
        leave(s).start()
        return carry

    lax.fori_loop(0, count, slot, 0)

    def finish(s, carry):
        leave(s).wait()
        return carry

    lax.fori_loop(0, count, finish, 0)


def turn(weights, first, count):
    shape = (count, GROUPS, 64, 128)
    return pl.pallas_call(
        functools.partial(turn_kernel, first),
        in_specs=[pl.BlockSpec(memory_space=pltpu.HBM)],
        out_specs=pl.BlockSpec(memory_space=pltpu.HBM),
        out_shape=pltpu.HBM(shape, BF16),
        scratch_shapes=[
            pltpu.VMEM((count, GROUPS, 128, 128), BF16),
            pltpu.VMEM(shape, BF16),
            pltpu.SemaphoreType.DMA((count,)),
            pltpu.SemaphoreType.DMA((count,)),
        ],
        compiler_params=pltpu.CompilerParams(vmem_limit_bytes=32 * 2**20),
        cost_estimate=pl.CostEstimate(
            flops=2 * count * GROUPS * 128**3, bytes_accessed=4 * count * GROUPS * 128**2, transcendentals=0
        ),
        name="turn",
    )(in_hbm(weights))


def analysis_kernel(blocks_hbm, *refs, count):
    messages = refs[:count]
    if count == 1:
        first_hbm, second_hbm, out_hbm, weights, blocks_ref, sem_b, sem_w, placed, turned, terms, out, sem_o = refs[1:]
    else:
        weights, out_hbm, blocks_ref, sem_b, placed, turned, terms, out, sem_o = refs[count:]
    order = pltpu.make_async_copy(blocks_hbm, blocks_ref, sem_b)
    order.start()
    if count == 1:
        split = first_hbm.shape[0]
        batches = ((first_hbm, 0, 0, 2), (first_hbm, 2, 2, split - 2), (second_hbm, 0, split, SLOTS - split))
    else:
        batches = ()

    def fetch(n):
        source, at, first, number = batches[n]
        return pltpu.make_async_copy(source.at[pl.ds(at, number)], weights.at[pl.ds(first, number)], sem_w.at[n])

    for n in range(len(batches)):
        fetch(n).start()
    for n, ref in enumerate(messages):
        for d in range(8):
            for j in range(4):
                for gh in range(2):
                    where = (j * 2 + gh) * 8
                    placed[n, pl.ds((gh * 4 + j) * 64 + d, 8, stride=8), :] = ref[d, where : where + 8, :].astype(F32)

    def pick(n, gh, j, i):
        return placed[n, (gh * 4 + j) * 64 + i * 32 : (gh * 4 + j) * 64 + (i + 1) * 32, :]

    row = lax.axis_index("row")
    has_low, has_high = row > 0, row < lax.axis_size("row") - 1

    def shells(gh, j):
        own = [pick(0, gh, j, i) for i in range(2)]
        if count == 1:
            return own
        low = [jnp.where(has_low, pick(1, gh, j, i), 0.0) for i in range(2)]
        high = [jnp.where(has_high, pick(2, gh, j, i), 0.0) for i in range(2)]
        return [
            (low[0] - 8.0 * low[1] + 8.0 * own[1] - high[0]) / 12.0,
            (low[1] - 8.0 * own[0] + 8.0 * high[0] - high[1]) / 12.0,
        ]

    for gh in range(2):
        columns = [shells(gh, j) for j in range(4)]
        for i in range(2):
            block = jnp.concatenate([columns[j][i] for j in range(4)], axis=0).T
            for quad in range(4):
                where = ((i * 2 + gh) * 4 + quad) * 40
                turned[where : where + 32, :] = block[quad * 32 : (quad + 1) * 32]
    lower = lax.broadcasted_iota(jnp.int32, (16, 128), 1) < 64
    terms[...] = jnp.zeros_like(terms)
    for qg in range(2 * GROUPS):
        both = turned[pl.ds(qg, 16, stride=40), :]
        halves = [jnp.where(lower, both, 0.0), jnp.where(lower, 0.0, both)]
        n = qg % 2
        terms[qg // 2, n * 32 : (n + 1) * 32, n * 128 : (n + 1) * 128] = jnp.concatenate(halves, axis=0).astype(BF16)

    def send(first, count):
        slots = pl.ds(first, count)
        return [pltpu.make_async_copy(out.at[i, slots], out_hbm.at[i, slots], sem_o.at[i]) for i in range(2)]

    def leave(first, count):
        for copy in send(first, count):
            copy.start()

    group = lax.broadcasted_iota(jnp.int32, (32, 128), 1) // 64
    halves = [(group == j).astype(F32).astype(BF16) for j in range(2)]

    def slot(s):
        base = own_block(blocks_ref, s) * (GROUPS // 2)
        for g in range(0, GROUPS, 2):
            blocks = [
                weights[s, g + n, u * 32 : (u + 1) * 32] * halves[j]
                for n in range(2) for u in range(2) for j in range(2)
            ]
            value = jnp.dot(terms[base + g // 2], jnp.concatenate(blocks, axis=0), preferred_element_type=F32)
            for n in range(2):
                part = [value[(n * 2 + u) * 16 : (n * 2 + u + 1) * 16] for u in range(2)]
                part = jnp.concatenate(part, axis=1).astype(BF16)
                for i in range(2):
                    out[i, s, :, (g + n) * 256 : (g + n + 1) * 256] = part[i * 8 : (i + 1) * 8]

    order.wait()

    def pair(t, carry):
        for n in range(len(batches)):
            need = batches[n][2] // 2
            pl.when(t == need)(lambda n=n: fetch(n).wait())
        slot(2 * t)
        slot(2 * t + 1)
        leave(2 * t, 2)
        return carry

    lax.fori_loop(0, SLOTS // 2, pair, 0)
    slot(SLOTS - 1)
    leave(SLOTS - 1, 1)
    for copy in send(0, SLOTS):
        copy.wait()


def analysis(name, m_blocks, messages, weights):
    vmem = pl.BlockSpec(memory_space=pltpu.VMEM)
    hbm = pl.BlockSpec(memory_space=pltpu.HBM)
    count = len(messages)
    plain = count == 1
    out_shape = pltpu.HBM((2, SLOTS, 8, 4096), BF16)
    shape = (SLOTS, GROUPS, 64, 128)
    return pl.pallas_call(
        functools.partial(analysis_kernel, count=count),
        in_specs=[hbm] + [vmem] * count + ([hbm, hbm] if plain else [vmem]),
        out_specs=[hbm, vmem] if plain else hbm,
        out_shape=[out_shape, pltpu.VMEM(shape, BF16)] if plain else out_shape,
        scratch_shapes=[
            pltpu.SMEM((16,), jnp.int32),
            pltpu.SemaphoreType.DMA,
            *([pltpu.SemaphoreType.DMA((3,))] if plain else []),
            pltpu.VMEM((count, 512, 128), F32),
            pltpu.VMEM((16 * 40, 128), F32),
            pltpu.VMEM((GROUPS, 64, 256), BF16),
            pltpu.VMEM((2, SLOTS, 8, 4096), BF16),
            pltpu.SemaphoreType.DMA((2,)),
        ],
        compiler_params=pltpu.CompilerParams(vmem_limit_bytes=24 * 2**20),
        cost_estimate=pl.CostEstimate(
            flops=2 * SLOTS * GROUPS * 32 * 128**2, bytes_accessed=12 * 2**20, transcendentals=0
        ),
        name=name,
    )(in_hbm(m_blocks), *messages, *(in_hbm(w) if plain else pltpu.with_memory_space_constraint(w, pltpu.VMEM) for w in weights))


def local(coeffs, legendre, lat_weights, m_blocks):
    table = jnp.asarray(quarter_table(), BF16)
    sent, weights = synthesis(m_blocks, coeffs.transpose(1, 2, 0, 3), legendre)
    first = turn(weights, 0, 9)
    received = lax.all_to_all(sent, "ma", split_axis=0, concat_axis=0, tiled=True)
    received, first, weights = lax.optimization_barrier((received, first, weights))
    sent_back = azimuth(m_blocks, lat_weights, received, table)
    sent_back, weights = lax.optimization_barrier((sent_back, weights))
    second = turn(weights, 9, 8)
    own = lax.all_to_all(sent_back, "ma", split_axis=0, concat_axis=0, tiled=True)
    own, second = lax.optimization_barrier((own, second))
    count = lax.axis_size("row")
    low = lax.ppermute(own, "row", [(r, (r + 1) % count) for r in range(count)])
    high = lax.ppermute(own, "row", [((r + 1) % count, r) for r in range(count)])
    plain, kept = analysis("plain", m_blocks, [own], [first, second])
    slope = analysis("slope", m_blocks, [own, low, high], [kept])
    return plain.transpose(0, 2, 1, 3), slope.transpose(0, 2, 1, 3)


def solution(mesh):
    placed = (P("row", None, "ma", None), P("ma", None, None), P(), P())
    return jax.shard_map(
        local,
        mesh=mesh,
        in_specs=placed,
        out_specs=(P("row", None, "ma", None), P("row", None, "ma", None)),
        check_vma=False,
    )
```

```python
import functools
import math

import jax
import jax.numpy as jnp
import numpy as np
from jax import lax
from jax.experimental import pallas as pl
from jax.experimental.pallas import tpu as pltpu
from jax.sharding import PartitionSpec as P

F32, BF16 = jnp.float32, jnp.bfloat16
POINTS = 3072
QUARTER = POINTS // 4
SLOTS = 17
GROUPS = 16
SPAN = 16
PITCH = 132
BATCHES = ((0, 1), (1, 2), (3, 6), (9, 8))


def lane_permutation(back=False):
    natural = lax.broadcasted_iota(jnp.int32, (128, 128), 1 if back else 0)
    grouped = lax.broadcasted_iota(jnp.int32, (128, 128), 0 if back else 1)
    c = natural % 64 // 4
    matrices = []
    for u in range(2):
        target = natural // 64 * 64 + (natural + 2 * u) % 4 * 16 + c % 2 * 8 + c // 2
        matrices.append((target == grouped).astype(F32).astype(BF16))
    return jnp.concatenate(matrices, axis=1)


def lane_masks():
    group = lax.broadcasted_iota(jnp.int32, (16, 128), 1) // 32
    return [(group == j).astype(F32).astype(BF16) for j in range(4)]


def quarter_table():
    j = np.arange(4)[:, None, None, None]
    b = np.arange(16)[None, :, None, None]
    g = np.arange(16)[None, None, :, None]
    x = np.arange(QUARTER)[None, None, None, :]
    order = b * 64 + g * 4 + j
    turns = (order * (2 * x + 1)) % (2 * POINTS)
    angles = turns * (math.pi / POINTS)
    table = np.stack([np.cos(angles), np.sin(angles)])
    return table.reshape(2, 4, 256, QUARTER)


def own_block(blocks_ref, s):
    lead = blocks_ref[2 * lax.axis_index("ma")]
    return (s >= SPAN - lead).astype(jnp.int32)


def spread(rows, n, scattered):
    scattered[pl.ds(n // 2 * PITCH + n % 2, 64, stride=2), :] = rows


def gather(scattered, row):
    return [scattered[pl.ds(2 * row + odd, 8, stride=PITCH), :] for odd in range(2)]


def group_rows(chunks, g):
    pieces = [piece for j in range(4) for piece in gather(chunks, g * 4 + j)]
    return jnp.concatenate(pieces, axis=0).astype(BF16)


def order_weights(rows, masks):
    rolled = [rows] + [pltpu.roll(rows, 32 * r, 1) for r in (1, 2, 3)]
    pieces = []
    for j in range(2):
        for a in range(4):
            pieces.append(
                rolled[(j - a) % 4][j * 16 : (j + 1) * 16] * masks[j]
                + rolled[(j + 2 - a) % 4][(j + 2) * 16 : (j + 3) * 16] * masks[j + 2]
            )
    return jnp.concatenate(pieces, axis=0)


def block_weights(rows, masks, place):
    blocks = []
    for j in range(2):
        for a in range(4):
            block = rows[j * 16 : (j + 1) * 16] * masks[a] + rows[(j + 2) * 16 : (j + 3) * 16] * masks[(a + 2) % 4]
            shift = (place - a) % 4
            blocks.append(pltpu.roll(block, 32 * shift, 1) if shift else block)
    return blocks


def swap_lane_groups(parts, lane_group):
    results = []
    for a in range(4):
        value = None
        for s in range(4):
            shift = (s - a) % 4
            moved = pltpu.roll(parts[s], 32 * shift, 1) if shift else parts[s]
            value = moved if value is None else jnp.where(lane_group == s, moved, value)
        results.append(value)
    return results


def synth_kernel(
    blocks_hbm, coef_hbm, leg_hbm, out_ref,
    blocks_ref, sem_b, coef, leg, sem_c, sem_l, chunks_even, chunks_odd, parts_even, parts_odd, weights_even, weights_odd, values_even, values_odd, acc, turned,
):
    def fetch(n):
        first, count = BATCHES[n]
        slots = pl.ds(first, count)
        return (
            pltpu.make_async_copy(leg_hbm.at[slots], leg.at[slots], sem_l.at[n]),
            pltpu.make_async_copy(coef_hbm.at[:, slots], coef.at[:, slots], sem_c.at[n]),
        )

    for n in range(len(BATCHES)):
        for copy in fetch(n):
            copy.start()
    order = pltpu.make_async_copy(blocks_hbm, blocks_ref, sem_b)
    order.start()
    acc[...] = jnp.zeros_like(acc)
    masks = lane_masks()
    perm = lane_permutation()[:, :128]
    lower = lax.broadcasted_iota(jnp.int32, (32, 128), 1) < 64
    parts_even[...] = jnp.zeros_like(parts_even)
    parts_odd[...] = jnp.zeros_like(parts_odd)

    def prepare(s, chunks, parts, weights, values):
        for c in range(16):
            spread(leg[s, :, c * 128 : (c + 1) * 128].astype(F32), c, chunks)
        for g in range(GROUPS):
            weights[g] = order_weights(group_rows(chunks, g), masks)
        rows = jnp.dot(coef[:, s].reshape(12 * 64, 128), perm, preferred_element_type=F32)
        for k in range(12):
            spread(rows[k * 64 : (k + 1) * 64], k, parts)
        for g in range(GROUPS):
            pieces = [piece for n in range(4) for piece in gather(parts, g * 4 + n)]
            values[g * 64 : (g + 1) * 64, :] = jnp.concatenate(pieces, axis=0).astype(BF16)

    def combine(s, weights, values):
        base = own_block(blocks_ref, s) * (GROUPS * 40)
        for g in range(GROUPS):
            term = jnp.dot(values[g * 64 : (g + 1) * 64, :], weights[g], preferred_element_type=F32)
            where = pl.ds(pl.multiple_of(base + g * 40, 8), 32)
            acc[where, :] = acc[where, :] + jnp.where(lower, term[:32], term[32:])

    def arrive(n):
        for copy in fetch(n):
            copy.wait()

    arrive(0)
    order.wait()
    prepare(0, chunks_even, parts_even, weights_even, values_even)

    def pair(t, carry):
        for n in range(1, len(BATCHES)):
            pl.when(2 * t + 1 == BATCHES[n][0])(functools.partial(arrive, n))
        prepare(2 * t + 1, chunks_odd, parts_odd, weights_odd, values_odd)
        combine(2 * t, weights_even, values_even)
        prepare(2 * t + 2, chunks_even, parts_even, weights_even, values_even)
        combine(2 * t + 1, weights_odd, values_odd)
        return carry

    lax.fori_loop(0, SLOTS // 2, pair, 0)
    combine(SLOTS - 1, weights_even, values_even)
    for comp in range(3):
        for i in range(2):
            parts = []
            for part in range(2):
                for vm in range(2):
                    row = i * 16 + part * 8 + vm * 3 + comp
                    parts.append(acc[pl.ds(row, 2 * GROUPS, stride=40), :])
            turned[comp * 2 + i] = jnp.concatenate(parts, axis=0).T
    for d in range(8):
        for j in range(4):
            pieces = [turned[n, pl.ds(j * 32 + d, 4, stride=8), :] for n in range(6)]
            out_ref[d, j] = jnp.concatenate(pieces, axis=0).astype(BF16)


def in_hbm(x):
    return pltpu.with_memory_space_constraint(x, pltpu.HBM)


def synthesis(m_blocks, coeffs, legendre):
    return pl.pallas_call(
        synth_kernel,
        in_specs=[pl.BlockSpec(memory_space=pltpu.HBM)] * 3,
        out_specs=pl.BlockSpec(memory_space=pltpu.VMEM),
        out_shape=jax.ShapeDtypeStruct((8, 4, 24, 128), BF16),
        scratch_shapes=[
            pltpu.SMEM((16,), jnp.int32),
            pltpu.SemaphoreType.DMA,
            pltpu.VMEM((12, SLOTS, 64, 128), BF16),
            pltpu.VMEM((SLOTS, 64, 2048), BF16),
            pltpu.SemaphoreType.DMA((len(BATCHES),)),
            pltpu.SemaphoreType.DMA((len(BATCHES),)),
            pltpu.VMEM((8 * PITCH, 128), F32),
            pltpu.VMEM((8 * PITCH, 128), F32),
            pltpu.VMEM((8 * PITCH, 128), F32),
            pltpu.VMEM((8 * PITCH, 128), F32),
            pltpu.VMEM((GROUPS, 128, 128), BF16),
            pltpu.VMEM((GROUPS, 128, 128), BF16),
            pltpu.VMEM((GROUPS * 64, 128), BF16),
            pltpu.VMEM((GROUPS * 64, 128), BF16),
            pltpu.VMEM((2 * GROUPS * 40, 128), F32),
            pltpu.VMEM((6, 128, 128), F32),
        ],
        compiler_params=pltpu.CompilerParams(vmem_limit_bytes=60 * 2**20),
        name="synthesis",
    )(in_hbm(m_blocks), in_hbm(coeffs), in_hbm(legendre))


def azimuth_kernel(blocks_ref, weights_ref, in_ref, table, out_ref, even_c, odd_c, even_s, odd_s, folded):
    lane_group = lax.broadcasted_iota(jnp.int32, (24, 128), 1) // 32
    left = []
    for j in range(4):
        halves = []
        for h in range(2):
            parts = [in_ref[h * 4 + s, j].astype(F32) * (1.0 / 32.0) for s in range(4)]
            halves.append(swap_lane_groups(parts, lane_group))
        both = [jnp.concatenate([halves[0][n], halves[1][n]], axis=1) for n in range(4)]
        left.append([jnp.concatenate([both[part * 2], both[part * 2 + 1]], axis=0).astype(BF16) for part in range(2)])
    starts = [pl.multiple_of(blocks_ref[p] * 16, 16) for p in range(16)]

    def basis(part, j):
        return jnp.concatenate([table[part, j, pl.ds(start, 16), :] for start in starts], axis=0)

    for part, refs in ((0, (even_c, odd_c)), (1, (even_s, odd_s))):
        for parity in range(2):
            refs[parity][...] = jnp.dot(
                left[parity][part], basis(part, parity), preferred_element_type=F32
            ) + jnp.dot(left[parity + 2][part], basis(part, parity + 2), preferred_element_type=F32)
    for x in range(QUARTER // 128):
        cols = slice(x * 128, (x + 1) * 128)
        fields = [[], [], [], []]
        for f in range(6):
            rows = slice(f * 8, (f + 1) * 8)
            ce, co, se, so = even_c[rows, cols], odd_c[rows, cols], even_s[rows, cols], odd_s[rows, cols]
            plus, minus = ce + co, ce - co
            total, other = se + so, se - so
            fields[0].append(plus - total)
            fields[1].append(plus + total)
            fields[2].append(minus + other)
            fields[3].append(minus - other)
        products = []
        for n in range(4):
            u0, u1, u2, b0, b1, b2 = fields[n]
            products.append(
                [
                    u1 * b2 - u2 * b1,
                    u2 * b0 - u0 * b2,
                    u0 * b1 - u1 * b0,
                    0.5 * (b0 * b0 + b1 * b1 + b2 * b2),
                ]
            )
        folds = [[], [], [], []]
        for g in range(4):
            p0, p1, p2, p3 = (products[n][g] for n in range(4))
            front, back = p0 + p1, p2 + p3
            left_odd, right_odd = p1 - p0, p2 - p3
            folds[0].append(front + back)
            folds[1].append(front - back)
            folds[2].append(left_odd + right_odd)
            folds[3].append(left_odd - right_odd)
        for n in range(4):
            folded[n, :, cols] = jnp.concatenate(folds[n], axis=0).astype(BF16)
    row = lax.broadcasted_iota(jnp.int32, (8, 1), 0) % 4
    own = lax.axis_index("ma")
    weight = jnp.zeros((8, 1), F32)
    for t in range(4):
        weight = jnp.where(row == t, weights_ref[t * 8 + own], weight)
    lane_group = lax.broadcasted_iota(jnp.int32, (8, 128), 1) // 32
    for j in range(4):
        terms = [
            lax.dot_general(
                folded[part * 2 + j % 2], basis(part, j), (((1,), (1,)), ((), ())), preferred_element_type=F32
            )
            for part in range(2)
        ]
        for gh in range(2):
            for h in range(2):
                parts = []
                for gl in range(2):
                    for part in range(2):
                        g = gh * 2 + gl
                        piece = terms[part][g * 8 : (g + 1) * 8, h * 128 : (h + 1) * 128]
                        parts.append((piece * (1.0 / math.sqrt(POINTS))) * weight)
                swapped = swap_lane_groups(parts, lane_group)
                for s in range(4):
                    where = (j * 2 + gh) * 8
                    out_ref[h * 4 + s, where : where + 8, :] = swapped[s].astype(BF16)


def azimuth(m_blocks, lat_weights, received, table):
    grid_shape = pltpu.VMEM((48, QUARTER), F32)
    return pl.pallas_call(
        azimuth_kernel,
        in_specs=[pl.BlockSpec(memory_space=pltpu.SMEM)] * 2 + [pl.BlockSpec(memory_space=pltpu.VMEM)] * 2,
        out_specs=pl.BlockSpec(memory_space=pltpu.VMEM),
        out_shape=jax.ShapeDtypeStruct((8, 64, 128), BF16),
        scratch_shapes=[
            grid_shape,
            grid_shape,
            grid_shape,
            grid_shape,
            pltpu.VMEM((4, 32, QUARTER), BF16),
        ],
        compiler_params=pltpu.CompilerParams(vmem_limit_bytes=32 * 2**20),
        name="azimuth",
    )(m_blocks, lat_weights, received, table)


def turn_kernel(first, leg_hbm, out_hbm, leg, chunks, turned, sem_in, sem_out):
    count = turned.shape[0]

    def fetch(s):
        return pltpu.make_async_copy(leg_hbm.at[first + s], leg.at[s], sem_in.at[s])

    def leave(s):
        return pltpu.make_async_copy(turned.at[s], out_hbm.at[s], sem_out.at[s])

    def start(s, carry):
        fetch(s).start()
        return carry

    lax.fori_loop(0, count, start, 0)
    perm = lane_permutation(back=True)
    masks = lane_masks()

    def slot(s, carry):
        fetch(s).wait()
        for c in range(16):
            spread(leg[s, :, c * 128 : (c + 1) * 128].astype(F32), c, chunks)
        for g in range(0, GROUPS, 2):
            blocks = [block_weights(group_rows(chunks, g + n), masks, n) for n in range(2)]
            both = jnp.concatenate([one + two for one, two in zip(*blocks)], axis=0)
            both = lax.dot_general(both, perm, (((0,), (0,)), ((), ())), preferred_element_type=F32)
            for n in range(2):
                rows = [both[(u * 2 + n) * 32 : (u * 2 + n + 1) * 32, u * 128 : (u + 1) * 128] for u in range(2)]
                turned[s, g + n] = jnp.concatenate(rows, axis=0).astype(BF16)
        leave(s).start()
        return carry

    lax.fori_loop(0, count, slot, 0)

    def finish(s, carry):
        leave(s).wait()
        return carry

    lax.fori_loop(0, count, finish, 0)


def turn(legendre, first, count):
    shape = (count, GROUPS, 64, 128)
    return pl.pallas_call(
        functools.partial(turn_kernel, first),
        in_specs=[pl.BlockSpec(memory_space=pltpu.HBM)],
        out_specs=pl.BlockSpec(memory_space=pltpu.HBM),
        out_shape=pltpu.HBM(shape, BF16),
        scratch_shapes=[
            pltpu.VMEM((count, 64, 2048), BF16),
            pltpu.VMEM((8 * PITCH, 128), F32),
            pltpu.VMEM(shape, BF16),
            pltpu.SemaphoreType.DMA((count,)),
            pltpu.SemaphoreType.DMA((count,)),
        ],
        compiler_params=pltpu.CompilerParams(vmem_limit_bytes=60 * 2**20),
        cost_estimate=pl.CostEstimate(
            flops=2 * count * GROUPS * 128**3, bytes_accessed=4 * count * GROUPS * 128**2, transcendentals=0
        ),
        name="turn",
    )(in_hbm(legendre))


def analysis_kernel(blocks_hbm, *refs, count):
    messages = refs[:count]
    if count == 1:
        first_hbm, second_hbm, out_hbm, weights, blocks_ref, sem_b, sem_w, placed, turned, terms, out, sem_o = refs[1:]
    else:
        weights, out_hbm, blocks_ref, sem_b, placed, turned, terms, out, sem_o = refs[count:]
    order = pltpu.make_async_copy(blocks_hbm, blocks_ref, sem_b)
    order.start()
    if count == 1:
        split = first_hbm.shape[0]
        batches = ((first_hbm, 0, 0, 2), (first_hbm, 2, 2, split - 2), (second_hbm, 0, split, SLOTS - split))
    else:
        batches = ()

    def fetch(n):
        source, at, first, number = batches[n]
        return pltpu.make_async_copy(source.at[pl.ds(at, number)], weights.at[pl.ds(first, number)], sem_w.at[n])

    for n in range(len(batches)):
        fetch(n).start()
    for n, ref in enumerate(messages):
        for d in range(8):
            for j in range(4):
                for gh in range(2):
                    where = (j * 2 + gh) * 8
                    placed[n, pl.ds((gh * 4 + j) * 64 + d, 8, stride=8), :] = ref[d, where : where + 8, :].astype(F32)

    def pick(n, gh, j, i):
        return placed[n, (gh * 4 + j) * 64 + i * 32 : (gh * 4 + j) * 64 + (i + 1) * 32, :]

    row = lax.axis_index("row")
    has_low, has_high = row > 0, row < lax.axis_size("row") - 1

    def shells(gh, j):
        own = [pick(0, gh, j, i) for i in range(2)]
        if count == 1:
            return own
        low = [jnp.where(has_low, pick(1, gh, j, i), 0.0) for i in range(2)]
        high = [jnp.where(has_high, pick(2, gh, j, i), 0.0) for i in range(2)]
        return [
            (low[0] - 8.0 * low[1] + 8.0 * own[1] - high[0]) / 12.0,
            (low[1] - 8.0 * own[0] + 8.0 * high[0] - high[1]) / 12.0,
        ]

    for gh in range(2):
        columns = [shells(gh, j) for j in range(4)]
        for i in range(2):
            block = jnp.concatenate([columns[j][i] for j in range(4)], axis=0).T
            for quad in range(4):
                where = ((i * 2 + gh) * 4 + quad) * 40
                turned[where : where + 32, :] = block[quad * 32 : (quad + 1) * 32]
    lower = lax.broadcasted_iota(jnp.int32, (16, 128), 1) < 64
    terms[...] = jnp.zeros_like(terms)
    for qg in range(2 * GROUPS):
        both = turned[pl.ds(qg, 16, stride=40), :]
        halves = [jnp.where(lower, both, 0.0), jnp.where(lower, 0.0, both)]
        n = qg % 2
        terms[qg // 2, n * 32 : (n + 1) * 32, n * 128 : (n + 1) * 128] = jnp.concatenate(halves, axis=0).astype(BF16)

    def send(first, count):
        slots = pl.ds(first, count)
        return [pltpu.make_async_copy(out.at[i, slots], out_hbm.at[i, slots], sem_o.at[i]) for i in range(2)]

    def leave(first, count):
        for copy in send(first, count):
            copy.start()

    group = lax.broadcasted_iota(jnp.int32, (32, 128), 1) // 64
    halves = [(group == j).astype(F32).astype(BF16) for j in range(2)]

    def slot(s):
        base = own_block(blocks_ref, s) * (GROUPS // 2)
        for g in range(0, GROUPS, 2):
            blocks = [
                weights[s, g + n, u * 32 : (u + 1) * 32] * halves[j]
                for n in range(2) for u in range(2) for j in range(2)
            ]
            value = jnp.dot(terms[base + g // 2], jnp.concatenate(blocks, axis=0), preferred_element_type=F32)
            for n in range(2):
                part = [value[(n * 2 + u) * 16 : (n * 2 + u + 1) * 16] for u in range(2)]
                part = jnp.concatenate(part, axis=1).astype(BF16)
                for i in range(2):
                    out[i, s, :, (g + n) * 256 : (g + n + 1) * 256] = part[i * 8 : (i + 1) * 8]

    order.wait()

    def pair(t, carry):
        for n in range(len(batches)):
            need = batches[n][2] // 2
            pl.when(t == need)(lambda n=n: fetch(n).wait())
        slot(2 * t)
        slot(2 * t + 1)
        leave(2 * t, 2)
        return carry

    lax.fori_loop(0, SLOTS // 2, pair, 0)
    slot(SLOTS - 1)
    leave(SLOTS - 1, 1)
    for copy in send(0, SLOTS):
        copy.wait()


def analysis(name, m_blocks, messages, weights):
    vmem = pl.BlockSpec(memory_space=pltpu.VMEM)
    hbm = pl.BlockSpec(memory_space=pltpu.HBM)
    count = len(messages)
    plain = count == 1
    out_shape = pltpu.HBM((2, SLOTS, 8, 4096), BF16)
    shape = (SLOTS, GROUPS, 64, 128)
    return pl.pallas_call(
        functools.partial(analysis_kernel, count=count),
        in_specs=[hbm] + [vmem] * count + ([hbm, hbm] if plain else [vmem]),
        out_specs=[hbm, vmem] if plain else hbm,
        out_shape=[out_shape, pltpu.VMEM(shape, BF16)] if plain else out_shape,
        scratch_shapes=[
            pltpu.SMEM((16,), jnp.int32),
            pltpu.SemaphoreType.DMA,
            *([pltpu.SemaphoreType.DMA((3,))] if plain else []),
            pltpu.VMEM((count, 512, 128), F32),
            pltpu.VMEM((16 * 40, 128), F32),
            pltpu.VMEM((GROUPS, 64, 256), BF16),
            pltpu.VMEM((2, SLOTS, 8, 4096), BF16),
            pltpu.SemaphoreType.DMA((2,)),
        ],
        compiler_params=pltpu.CompilerParams(vmem_limit_bytes=24 * 2**20),
        cost_estimate=pl.CostEstimate(
            flops=2 * SLOTS * GROUPS * 32 * 128**2, bytes_accessed=12 * 2**20, transcendentals=0
        ),
        name=name,
    )(in_hbm(m_blocks), *messages, *(in_hbm(w) if plain else pltpu.with_memory_space_constraint(w, pltpu.VMEM) for w in weights))


def rows_of(coeffs):
    split = coeffs.reshape(2, 12, SLOTS, 32, 128)
    return split.transpose(1, 2, 3, 0, 4).reshape(12, SLOTS, 64, 128)


def local(coeffs, legendre, lat_weights, m_blocks):
    table = jnp.asarray(quarter_table(), BF16)
    sent = synthesis(m_blocks, rows_of(coeffs), legendre)
    sent, legendre = lax.optimization_barrier((sent, legendre))
    first = turn(legendre, 0, 9)
    received = lax.all_to_all(sent, "ma", split_axis=0, concat_axis=0, tiled=True)
    received, first, legendre = lax.optimization_barrier((received, first, legendre))
    sent_back = azimuth(m_blocks, lat_weights, received, table)
    sent_back, legendre = lax.optimization_barrier((sent_back, legendre))
    second = turn(legendre, 9, 8)
    own = lax.all_to_all(sent_back, "ma", split_axis=0, concat_axis=0, tiled=True)
    own, second = lax.optimization_barrier((own, second))
    count = lax.axis_size("row")
    low = lax.ppermute(own, "row", [(r, (r + 1) % count) for r in range(count)])
    high = lax.ppermute(own, "row", [((r + 1) % count, r) for r in range(count)])
    plain, kept = analysis("plain", m_blocks, [own], [first, second])
    slope = analysis("slope", m_blocks, [own, low, high], [kept])
    return plain.transpose(0, 2, 1, 3), slope.transpose(0, 2, 1, 3)


def solution(mesh):
    placed = (P("row", None, "ma", None), P("ma", None, None), P(), P())
    return jax.shard_map(
        local,
        mesh=mesh,
        in_specs=placed,
        out_specs=(P("row", None, "ma", None), P("row", None, "ma", None)),
        check_vma=False,
    )
```

```python
import functools
import math

import jax
import jax.numpy as jnp
import numpy as np
from jax import lax
from jax.experimental import pallas as pl
from jax.experimental.pallas import tpu as pltpu
from jax.sharding import PartitionSpec as P

F32, BF16 = jnp.float32, jnp.bfloat16
POINTS = 3072
QUARTER = POINTS // 4
EIGHTH = POINTS // 8
SLOTS = 17
GROUPS = 16
SPAN = 16
PITCH = 132
BATCHES = ((0, 1), (1, 2), (3, 2), (5, 4), (9, 8))


def lane_permutation(back=False):
    natural = lax.broadcasted_iota(jnp.int32, (128, 128), 1 if back else 0)
    grouped = lax.broadcasted_iota(jnp.int32, (128, 128), 0 if back else 1)
    c = natural % 64 // 4
    matrices = []
    for u in range(2):
        target = natural // 64 * 64 + (natural + 2 * u) % 4 * 16 + c % 2 * 8 + c // 2
        matrices.append((target == grouped).astype(F32).astype(BF16))
    return jnp.concatenate(matrices, axis=1)


def lane_masks():
    group = lax.broadcasted_iota(jnp.int32, (16, 128), 1) // 32
    return [(group == j).astype(F32).astype(BF16) for j in range(4)]


def eighth_table():
    j = np.arange(4)[:, None, None, None]
    b = np.arange(16)[None, :, None, None]
    g = np.arange(16)[None, None, :, None]
    x = np.arange(EIGHTH)[None, None, None, :]
    order = b * 64 + g * 4 + j
    turns = (order * (2 * x + 1)) % (2 * POINTS)
    angles = turns * (math.pi / POINTS)
    table = np.stack([np.cos(angles), np.sin(angles)])
    return table.reshape(2, 4, 256, EIGHTH)


def own_block(blocks_ref, s):
    lead = blocks_ref[2 * lax.axis_index("ma")]
    return (s >= SPAN - lead).astype(jnp.int32)


def spread(rows, n, scattered):
    scattered[pl.ds(n // 2 * PITCH + n % 2, 64, stride=2), :] = rows


def gather(scattered, row):
    return [scattered[pl.ds(2 * row + odd, 8, stride=PITCH), :] for odd in range(2)]


def group_rows(chunks, g):
    pieces = [piece for j in range(4) for piece in gather(chunks, g * 4 + j)]
    return jnp.concatenate(pieces, axis=0).astype(BF16)


def order_weights(rows, masks):
    rolled = [rows] + [pltpu.roll(rows, 32 * r, 1) for r in (1, 2, 3)]
    pieces = []
    for j in range(2):
        for a in range(4):
            pieces.append(
                rolled[(j - a) % 4][j * 16 : (j + 1) * 16] * masks[j]
                + rolled[(j + 2 - a) % 4][(j + 2) * 16 : (j + 3) * 16] * masks[j + 2]
            )
    return jnp.concatenate(pieces, axis=0)


def block_weights(rows, masks, place):
    blocks = []
    for j in range(2):
        for a in range(4):
            block = rows[j * 16 : (j + 1) * 16] * masks[a] + rows[(j + 2) * 16 : (j + 3) * 16] * masks[(a + 2) % 4]
            shift = (place - a) % 4
            blocks.append(pltpu.roll(block, 32 * shift, 1) if shift else block)
    return blocks


def swap_lane_groups(parts, lane_group):
    results = []
    for a in range(4):
        value = None
        for s in range(4):
            shift = (s - a) % 4
            moved = pltpu.roll(parts[s], 32 * shift, 1) if shift else parts[s]
            value = moved if value is None else jnp.where(lane_group == s, moved, value)
        results.append(value)
    return results


def synth_kernel(
    blocks_hbm, coef_hbm, leg_hbm, out_ref,
    blocks_ref, sem_b, coef, leg, sem_c, sem_l, chunks_even, chunks_odd, parts_even, parts_odd, weights_even, weights_odd, values_even, values_odd, acc, turned,
):
    def fetch(n):
        first, count = BATCHES[n]
        slots = pl.ds(first, count)
        return (
            pltpu.make_async_copy(leg_hbm.at[slots], leg.at[slots], sem_l.at[n]),
            pltpu.make_async_copy(coef_hbm.at[:, slots], coef.at[:, slots], sem_c.at[n]),
        )

    for n in range(len(BATCHES)):
        for copy in fetch(n):
            copy.start()
    order = pltpu.make_async_copy(blocks_hbm, blocks_ref, sem_b)
    order.start()
    acc[...] = jnp.zeros_like(acc)
    masks = lane_masks()
    perm = lane_permutation()[:, :128]
    lower = lax.broadcasted_iota(jnp.int32, (32, 128), 1) < 64
    parts_even[...] = jnp.zeros_like(parts_even)
    parts_odd[...] = jnp.zeros_like(parts_odd)

    def prepare(s, chunks, parts, weights, values):
        for c in range(16):
            spread(leg[s, :, c * 128 : (c + 1) * 128].astype(F32), c, chunks)
        for g in range(GROUPS):
            weights[g] = order_weights(group_rows(chunks, g), masks)
        rows = jnp.dot(coef[:, s].reshape(12 * 64, 128), perm, preferred_element_type=F32)
        for k in range(12):
            spread(rows[k * 64 : (k + 1) * 64], k, parts)
        for g in range(GROUPS):
            pieces = [piece for n in range(4) for piece in gather(parts, g * 4 + n)]
            values[g * 64 : (g + 1) * 64, :] = jnp.concatenate(pieces, axis=0).astype(BF16)

    def combine(s, weights, values):
        base = own_block(blocks_ref, s) * (GROUPS * 40)
        for g in range(GROUPS):
            term = jnp.dot(values[g * 64 : (g + 1) * 64, :], weights[g], preferred_element_type=F32)
            where = pl.ds(pl.multiple_of(base + g * 40, 8), 32)
            acc[where, :] = acc[where, :] + jnp.where(lower, term[:32], term[32:])

    def arrive(n):
        for copy in fetch(n):
            copy.wait()

    arrive(0)
    order.wait()
    prepare(0, chunks_even, parts_even, weights_even, values_even)

    def pair(t, carry):
        for n in range(1, len(BATCHES)):
            pl.when(2 * t + 1 == BATCHES[n][0])(functools.partial(arrive, n))
        prepare(2 * t + 1, chunks_odd, parts_odd, weights_odd, values_odd)
        combine(2 * t, weights_even, values_even)
        prepare(2 * t + 2, chunks_even, parts_even, weights_even, values_even)
        combine(2 * t + 1, weights_odd, values_odd)
        return carry

    lax.fori_loop(0, SLOTS // 2, pair, 0)
    combine(SLOTS - 1, weights_even, values_even)
    for comp in range(3):
        for i in range(2):
            parts = []
            for part in range(2):
                for vm in range(2):
                    row = i * 16 + part * 8 + vm * 3 + comp
                    parts.append(acc[pl.ds(row, 2 * GROUPS, stride=40), :])
            turned[comp * 2 + i] = jnp.concatenate(parts, axis=0).T
    for d in range(8):
        for j in range(4):
            pieces = [turned[n, pl.ds(j * 32 + d, 4, stride=8), :] for n in range(6)]
            out_ref[d, j] = jnp.concatenate(pieces, axis=0).astype(BF16)


def in_hbm(x):
    return pltpu.with_memory_space_constraint(x, pltpu.HBM)


def synthesis(m_blocks, coeffs, legendre):
    return pl.pallas_call(
        synth_kernel,
        in_specs=[pl.BlockSpec(memory_space=pltpu.HBM)] * 3,
        out_specs=pl.BlockSpec(memory_space=pltpu.VMEM),
        out_shape=jax.ShapeDtypeStruct((8, 4, 24, 128), BF16),
        scratch_shapes=[
            pltpu.SMEM((16,), jnp.int32),
            pltpu.SemaphoreType.DMA,
            pltpu.VMEM((12, SLOTS, 64, 128), BF16),
            pltpu.VMEM((SLOTS, 64, 2048), BF16),
            pltpu.SemaphoreType.DMA((len(BATCHES),)),
            pltpu.SemaphoreType.DMA((len(BATCHES),)),
            pltpu.VMEM((8 * PITCH, 128), F32),
            pltpu.VMEM((8 * PITCH, 128), F32),
            pltpu.VMEM((8 * PITCH, 128), F32),
            pltpu.VMEM((8 * PITCH, 128), F32),
            pltpu.VMEM((GROUPS, 128, 128), BF16),
            pltpu.VMEM((GROUPS, 128, 128), BF16),
            pltpu.VMEM((GROUPS * 64, 128), BF16),
            pltpu.VMEM((GROUPS * 64, 128), BF16),
            pltpu.VMEM((2 * GROUPS * 40, 128), F32),
            pltpu.VMEM((6, 128, 128), F32),
        ],
        compiler_params=pltpu.CompilerParams(vmem_limit_bytes=60 * 2**20),
        name="synthesis",
    )(in_hbm(m_blocks), in_hbm(coeffs), in_hbm(legendre))


def azimuth_kernel(blocks_ref, weights_ref, in_ref, table, out_ref, even_c, odd_c, even_s, odd_s, folded):
    lane_group = lax.broadcasted_iota(jnp.int32, (24, 128), 1) // 32
    left = []
    for j in range(4):
        halves = []
        for h in range(2):
            parts = [in_ref[h * 4 + s, j].astype(F32) * (1.0 / 32.0) for s in range(4)]
            halves.append(swap_lane_groups(parts, lane_group))
        both = [jnp.concatenate([halves[0][n], halves[1][n]], axis=1) for n in range(4)]
        left.append([jnp.concatenate([both[part * 2], both[part * 2 + 1]], axis=0).astype(BF16) for part in range(2)])
    starts = [pl.multiple_of(blocks_ref[p] * 16, 16) for p in range(16)]

    def basis(part, j):
        return jnp.concatenate([table[part, j, pl.ds(start, 16), :] for start in starts], axis=0)

    near, far = slice(0, EIGHTH), slice(EIGHTH, QUARTER)
    for part, ref in ((0, even_c), (1, even_s)):
        zero, two = (jnp.dot(left[j][part], basis(part, j), preferred_element_type=F32) for j in (0, 2))
        ref[:, near] = zero + two
        ref[:, far] = zero - two if part == 0 else two - zero
    both = [jnp.concatenate(left[j], axis=0) for j in (1, 3)]
    for part, here, there in ((0, odd_c, odd_s), (1, odd_s, odd_c)):
        one, three = (jnp.dot(both[n], basis(part, 2 * n + 1), preferred_element_type=F32) for n in range(2))
        here[:, near] = (one + three)[part * 48 : (part + 1) * 48]
        there[:, far] = (one - three)[(1 - part) * 48 : (2 - part) * 48]
    for x in range(QUARTER // 128):
        cols = slice(x * 128, (x + 1) * 128)
        fields = [[], [], [], []]
        for f in range(6):
            rows = slice(f * 8, (f + 1) * 8)
            ce, co, se, so = even_c[rows, cols], odd_c[rows, cols], even_s[rows, cols], odd_s[rows, cols]
            plus, minus = ce + co, ce - co
            total, other = se + so, se - so
            fields[0].append(plus - total)
            fields[1].append(plus + total)
            fields[2].append(minus + other)
            fields[3].append(minus - other)
        products = []
        for n in range(4):
            u0, u1, u2, b0, b1, b2 = fields[n]
            products.append(
                [
                    u1 * b2 - u2 * b1,
                    u2 * b0 - u0 * b2,
                    u0 * b1 - u1 * b0,
                    0.5 * (b0 * b0 + b1 * b1 + b2 * b2),
                ]
            )
        folds = [[], [], [], []]
        for g in range(4):
            p0, p1, p2, p3 = (products[n][g] for n in range(4))
            front, back = p0 + p1, p2 + p3
            left_odd, right_odd = p1 - p0, p2 - p3
            folds[0].append(front + back)
            folds[1].append(front - back)
            folds[2].append(left_odd + right_odd)
            folds[3].append(left_odd - right_odd)
        for n in range(4):
            folded[n, :, cols] = jnp.concatenate(folds[n], axis=0)
    row = lax.broadcasted_iota(jnp.int32, (8, 1), 0) % 4
    own = lax.axis_index("ma")
    weight = jnp.zeros((8, 1), F32)
    for t in range(4):
        weight = jnp.where(row == t, weights_ref[t * 8 + own], weight)
    lane_group = lax.broadcasted_iota(jnp.int32, (8, 128), 1) // 32
    def back(rows, part, j):
        return lax.dot_general(
            rows.astype(BF16), basis(part, j), (((1,), (1,)), ((), ())), preferred_element_type=F32
        )

    for j in range(4):
        c_near, c_far = folded[j % 2, :, near], folded[j % 2, :, far]
        s_near, s_far = folded[2 + j % 2, :, near], folded[2 + j % 2, :, far]
        if j == 0:
            terms = [back(c_near + c_far, 0, j), back(s_near - s_far, 1, j)]
        elif j == 2:
            terms = [back(c_near - c_far, 0, j), back(s_near + s_far, 1, j)]
        else:
            sign = 1.0 if j == 1 else -1.0
            total = back(jnp.concatenate([c_near, sign * s_far], axis=0), 0, j)
            total = total + back(jnp.concatenate([sign * c_far, s_near], axis=0), 1, j)
            terms = [total[:32], total[32:]]
        for gh in range(2):
            for h in range(2):
                parts = []
                for gl in range(2):
                    for part in range(2):
                        g = gh * 2 + gl
                        piece = terms[part][g * 8 : (g + 1) * 8, h * 128 : (h + 1) * 128]
                        parts.append((piece * (1.0 / math.sqrt(POINTS))) * weight)
                swapped = swap_lane_groups(parts, lane_group)
                for s in range(4):
                    where = (j * 2 + gh) * 8
                    out_ref[h * 4 + s, where : where + 8, :] = swapped[s].astype(BF16)


def azimuth(m_blocks, lat_weights, received, table):
    grid_shape = pltpu.VMEM((48, QUARTER), F32)
    return pl.pallas_call(
        azimuth_kernel,
        in_specs=[pl.BlockSpec(memory_space=pltpu.SMEM)] * 2 + [pl.BlockSpec(memory_space=pltpu.VMEM)] * 2,
        out_specs=pl.BlockSpec(memory_space=pltpu.VMEM),
        out_shape=jax.ShapeDtypeStruct((8, 64, 128), BF16),
        scratch_shapes=[
            grid_shape,
            grid_shape,
            grid_shape,
            grid_shape,
            pltpu.VMEM((4, 32, QUARTER), F32),
        ],
        compiler_params=pltpu.CompilerParams(vmem_limit_bytes=32 * 2**20),
        name="azimuth",
    )(m_blocks, lat_weights, received, table)


def turn_kernel(first, leg_hbm, out_hbm, leg, chunks, turned, sem_in, sem_out):
    count = turned.shape[0]

    def fetch(s):
        return pltpu.make_async_copy(leg_hbm.at[first + s], leg.at[s], sem_in.at[s])

    def leave(s):
        return pltpu.make_async_copy(turned.at[s], out_hbm.at[s], sem_out.at[s])

    def start(s, carry):
        fetch(s).start()
        return carry

    lax.fori_loop(0, count, start, 0)
    perm = lane_permutation(back=True)
    masks = lane_masks()

    def slot(s, carry):
        fetch(s).wait()
        for c in range(16):
            spread(leg[s, :, c * 128 : (c + 1) * 128].astype(F32), c, chunks)
        for g in range(0, GROUPS, 2):
            blocks = [block_weights(group_rows(chunks, g + n), masks, n) for n in range(2)]
            both = jnp.concatenate([one + two for one, two in zip(*blocks)], axis=0)
            both = lax.dot_general(both, perm, (((0,), (0,)), ((), ())), preferred_element_type=F32)
            for n in range(2):
                rows = [both[(u * 2 + n) * 32 : (u * 2 + n + 1) * 32, u * 128 : (u + 1) * 128] for u in range(2)]
                turned[s, g + n] = jnp.concatenate(rows, axis=0).astype(BF16)
        leave(s).start()
        return carry

    lax.fori_loop(0, count, slot, 0)

    def finish(s, carry):
        leave(s).wait()
        return carry

    lax.fori_loop(0, count, finish, 0)


def turn(legendre, first, count):
    shape = (count, GROUPS, 64, 128)
    return pl.pallas_call(
        functools.partial(turn_kernel, first),
        in_specs=[pl.BlockSpec(memory_space=pltpu.HBM)],
        out_specs=pl.BlockSpec(memory_space=pltpu.HBM),
        out_shape=pltpu.HBM(shape, BF16),
        scratch_shapes=[
            pltpu.VMEM((count, 64, 2048), BF16),
            pltpu.VMEM((8 * PITCH, 128), F32),
            pltpu.VMEM(shape, BF16),
            pltpu.SemaphoreType.DMA((count,)),
            pltpu.SemaphoreType.DMA((count,)),
        ],
        compiler_params=pltpu.CompilerParams(vmem_limit_bytes=60 * 2**20),
        cost_estimate=pl.CostEstimate(
            flops=2 * count * GROUPS * 128**3, bytes_accessed=4 * count * GROUPS * 128**2, transcendentals=0
        ),
        name="turn",
    )(in_hbm(legendre))


def analysis_kernel(blocks_hbm, *refs, count):
    messages = refs[:count]
    if count == 1:
        first_hbm, second_hbm, out_hbm, weights, blocks_ref, sem_b, sem_w, placed, turned, terms, out, sem_o = refs[1:]
    else:
        weights, out_hbm, blocks_ref, sem_b, placed, turned, terms, out, sem_o = refs[count:]
    order = pltpu.make_async_copy(blocks_hbm, blocks_ref, sem_b)
    order.start()
    if count == 1:
        split = first_hbm.shape[0]
        batches = ((first_hbm, 0, 0, 2), (first_hbm, 2, 2, split - 2), (second_hbm, 0, split, SLOTS - split))
    else:
        batches = ()

    def fetch(n):
        source, at, first, number = batches[n]
        return pltpu.make_async_copy(source.at[pl.ds(at, number)], weights.at[pl.ds(first, number)], sem_w.at[n])

    for n in range(len(batches)):
        fetch(n).start()
    for n, ref in enumerate(messages):
        for d in range(8):
            for j in range(4):
                for gh in range(2):
                    where = (j * 2 + gh) * 8
                    placed[n, pl.ds((gh * 4 + j) * 64 + d, 8, stride=8), :] = ref[d, where : where + 8, :].astype(F32)

    def pick(n, gh, j, i):
        return placed[n, (gh * 4 + j) * 64 + i * 32 : (gh * 4 + j) * 64 + (i + 1) * 32, :]

    row = lax.axis_index("row")
    has_low, has_high = row > 0, row < lax.axis_size("row") - 1

    def shells(gh, j):
        own = [pick(0, gh, j, i) for i in range(2)]
        if count == 1:
            return own
        low = [jnp.where(has_low, pick(1, gh, j, i), 0.0) for i in range(2)]
        high = [jnp.where(has_high, pick(2, gh, j, i), 0.0) for i in range(2)]
        return [
            (low[0] - 8.0 * low[1] + 8.0 * own[1] - high[0]) / 12.0,
            (low[1] - 8.0 * own[0] + 8.0 * high[0] - high[1]) / 12.0,
        ]

    for gh in range(2):
        columns = [shells(gh, j) for j in range(4)]
        for i in range(2):
            block = jnp.concatenate([columns[j][i] for j in range(4)], axis=0).T
            for quad in range(4):
                where = ((i * 2 + gh) * 4 + quad) * 40
                turned[where : where + 32, :] = block[quad * 32 : (quad + 1) * 32]
    lower = lax.broadcasted_iota(jnp.int32, (16, 128), 1) < 64
    terms[...] = jnp.zeros_like(terms)
    for qg in range(2 * GROUPS):
        both = turned[pl.ds(qg, 16, stride=40), :]
        halves = [jnp.where(lower, both, 0.0), jnp.where(lower, 0.0, both)]
        n = qg % 2
        terms[qg // 2, n * 32 : (n + 1) * 32, n * 128 : (n + 1) * 128] = jnp.concatenate(halves, axis=0).astype(BF16)

    def send(first, count):
        slots = pl.ds(first, count)
        return [pltpu.make_async_copy(out.at[i, slots], out_hbm.at[i, slots], sem_o.at[i]) for i in range(2)]

    def leave(first, count):
        for copy in send(first, count):
            copy.start()

    group = lax.broadcasted_iota(jnp.int32, (32, 128), 1) // 64
    halves = [(group == j).astype(F32).astype(BF16) for j in range(2)]

    def slot(s):
        base = own_block(blocks_ref, s) * (GROUPS // 2)
        for g in range(0, GROUPS, 2):
            blocks = [
                weights[s, g + n, u * 32 : (u + 1) * 32] * halves[j]
                for n in range(2) for u in range(2) for j in range(2)
            ]
            value = jnp.dot(terms[base + g // 2], jnp.concatenate(blocks, axis=0), preferred_element_type=F32)
            for n in range(2):
                part = [value[(n * 2 + u) * 16 : (n * 2 + u + 1) * 16] for u in range(2)]
                part = jnp.concatenate(part, axis=1).astype(BF16)
                for i in range(2):
                    out[i, s, :, (g + n) * 256 : (g + n + 1) * 256] = part[i * 8 : (i + 1) * 8]

    order.wait()

    def pair(t, carry):
        for n in range(len(batches)):
            need = batches[n][2] // 2
            pl.when(t == need)(lambda n=n: fetch(n).wait())
        slot(2 * t)
        slot(2 * t + 1)
        leave(2 * t, 2)
        return carry

    lax.fori_loop(0, SLOTS // 2, pair, 0)
    slot(SLOTS - 1)
    leave(SLOTS - 1, 1)
    for copy in send(0, SLOTS):
        copy.wait()


def analysis(name, m_blocks, messages, weights):
    vmem = pl.BlockSpec(memory_space=pltpu.VMEM)
    hbm = pl.BlockSpec(memory_space=pltpu.HBM)
    count = len(messages)
    plain = count == 1
    out_shape = pltpu.HBM((2, SLOTS, 8, 4096), BF16)
    shape = (SLOTS, GROUPS, 64, 128)
    return pl.pallas_call(
        functools.partial(analysis_kernel, count=count),
        in_specs=[hbm] + [vmem] * count + ([hbm, hbm] if plain else [vmem]),
        out_specs=[hbm, vmem] if plain else hbm,
        out_shape=[out_shape, pltpu.VMEM(shape, BF16)] if plain else out_shape,
        scratch_shapes=[
            pltpu.SMEM((16,), jnp.int32),
            pltpu.SemaphoreType.DMA,
            *([pltpu.SemaphoreType.DMA((3,))] if plain else []),
            pltpu.VMEM((count, 512, 128), F32),
            pltpu.VMEM((16 * 40, 128), F32),
            pltpu.VMEM((GROUPS, 64, 256), BF16),
            pltpu.VMEM((2, SLOTS, 8, 4096), BF16),
            pltpu.SemaphoreType.DMA((2,)),
        ],
        compiler_params=pltpu.CompilerParams(vmem_limit_bytes=24 * 2**20),
        cost_estimate=pl.CostEstimate(
            flops=2 * SLOTS * GROUPS * 32 * 128**2, bytes_accessed=12 * 2**20, transcendentals=0
        ),
        name=name,
    )(in_hbm(m_blocks), *messages, *(in_hbm(w) if plain else pltpu.with_memory_space_constraint(w, pltpu.VMEM) for w in weights))


def rows_of(coeffs):
    split = coeffs.reshape(2, 12, SLOTS, 32, 128)
    return split.transpose(1, 2, 3, 0, 4).reshape(12, SLOTS, 64, 128)


def local(coeffs, legendre, lat_weights, m_blocks):
    table = jnp.asarray(eighth_table(), BF16)
    sent = synthesis(m_blocks, rows_of(coeffs), legendre)
    sent, legendre = lax.optimization_barrier((sent, legendre))
    first = turn(legendre, 0, 9)
    received = lax.all_to_all(sent, "ma", split_axis=0, concat_axis=0, tiled=True)
    received, first, legendre = lax.optimization_barrier((received, first, legendre))
    sent_back = azimuth(m_blocks, lat_weights, received, table)
    sent_back, legendre = lax.optimization_barrier((sent_back, legendre))
    second = turn(legendre, 9, 8)
    own = lax.all_to_all(sent_back, "ma", split_axis=0, concat_axis=0, tiled=True)
    own, second = lax.optimization_barrier((own, second))
    count = lax.axis_size("row")
    low = lax.ppermute(own, "row", [(r, (r + 1) % count) for r in range(count)])
    high = lax.ppermute(own, "row", [((r + 1) % count, r) for r in range(count)])
    plain, kept = analysis("plain", m_blocks, [own], [first, second])
    slope = analysis("slope", m_blocks, [own, low, high], [kept])
    return plain.transpose(0, 2, 1, 3), slope.transpose(0, 2, 1, 3)


def solution(mesh):
    placed = (P("row", None, "ma", None), P("ma", None, None), P(), P())
    return jax.shard_map(
        local,
        mesh=mesh,
        in_specs=placed,
        out_specs=(P("row", None, "ma", None), P("row", None, "ma", None)),
        check_vma=False,
    )
```

```python
import functools
import math

import jax
import jax.numpy as jnp
import numpy as np
from jax import lax
from jax.experimental import pallas as pl
from jax.experimental.pallas import tpu as pltpu
from jax.sharding import PartitionSpec as P

F32, BF16 = jnp.float32, jnp.bfloat16
POINTS = 3072
QUARTER = POINTS // 4
EIGHTH = POINTS // 8
SLOTS = 17
GROUPS = 16
SPAN = 16
PITCH = 132
BATCHES = ((0, 1), (1, 2), (3, 2), (5, 4), (9, 8))


def lane_permutation(back=False):
    natural = lax.broadcasted_iota(jnp.int32, (128, 128), 1 if back else 0)
    grouped = lax.broadcasted_iota(jnp.int32, (128, 128), 0 if back else 1)
    c = natural % 64 // 4
    matrices = []
    for u in range(2):
        target = natural // 64 * 64 + (natural + 2 * u) % 4 * 16 + c % 2 * 8 + c // 2
        matrices.append((target == grouped).astype(F32).astype(BF16))
    return jnp.concatenate(matrices, axis=1)


def lane_masks():
    group = lax.broadcasted_iota(jnp.int32, (16, 128), 1) // 32
    return [(group == j).astype(F32).astype(BF16) for j in range(4)]


def eighth_table():
    j = np.arange(4)[:, None, None, None]
    b = np.arange(16)[None, :, None, None]
    g = np.arange(16)[None, None, :, None]
    x = np.arange(EIGHTH)[None, None, None, :]
    order = b * 64 + g * 4 + j
    turns = (order * (2 * x + 1)) % (2 * POINTS)
    angles = turns * (math.pi / POINTS)
    table = np.stack([np.cos(angles), np.sin(angles)])
    return table.reshape(2, 4, 256, EIGHTH)


def own_block(blocks_ref, s):
    lead = blocks_ref[2 * lax.axis_index("ma")]
    return (s >= SPAN - lead).astype(jnp.int32)


def spread(rows, n, scattered):
    scattered[pl.ds(n // 2 * PITCH + n % 2, 64, stride=2), :] = rows


def gather(scattered, row):
    return [scattered[pl.ds(2 * row + odd, 8, stride=PITCH), :] for odd in range(2)]


def group_rows(chunks, g):
    pieces = [piece for j in range(4) for piece in gather(chunks, g * 4 + j)]
    return jnp.concatenate(pieces, axis=0).astype(BF16)


def order_weights(rows, masks):
    rolled = [rows] + [pltpu.roll(rows, 32 * r, 1) for r in (1, 2, 3)]
    pieces = []
    for j in range(2):
        for a in range(4):
            pieces.append(
                rolled[(j - a) % 4][j * 16 : (j + 1) * 16] * masks[j]
                + rolled[(j + 2 - a) % 4][(j + 2) * 16 : (j + 3) * 16] * masks[j + 2]
            )
    return jnp.concatenate(pieces, axis=0)


def block_weights(rows, masks, place):
    blocks = []
    for j in range(2):
        for a in range(4):
            block = rows[j * 16 : (j + 1) * 16] * masks[a] + rows[(j + 2) * 16 : (j + 3) * 16] * masks[(a + 2) % 4]
            shift = (place - a) % 4
            blocks.append(pltpu.roll(block, 32 * shift, 1) if shift else block)
    return blocks


def swap_lane_groups(parts, lane_group):
    results = []
    for a in range(4):
        value = None
        for s in range(4):
            shift = (s - a) % 4
            moved = pltpu.roll(parts[s], 32 * shift, 1) if shift else parts[s]
            value = moved if value is None else jnp.where(lane_group == s, moved, value)
        results.append(value)
    return results


def synth_kernel(
    blocks_hbm, coef_hbm, leg_hbm, out_ref,
    blocks_ref, sem_b, coef, leg, sem_c, sem_l, chunks_even, chunks_odd, parts_even, parts_odd, weights_even, weights_odd, values_even, values_odd, acc, turned,
):
    def fetch(n):
        first, count = BATCHES[n]
        slots = pl.ds(first, count)
        return (
            pltpu.make_async_copy(leg_hbm.at[slots], leg.at[slots], sem_l.at[n]),
            pltpu.make_async_copy(coef_hbm.at[:, slots], coef.at[:, slots], sem_c.at[n]),
        )

    for n in range(len(BATCHES)):
        for copy in fetch(n):
            copy.start()
    order = pltpu.make_async_copy(blocks_hbm, blocks_ref, sem_b)
    order.start()
    acc[...] = jnp.zeros_like(acc)
    masks = lane_masks()
    perm = lane_permutation()[:, :128]
    lower = lax.broadcasted_iota(jnp.int32, (32, 128), 1) < 64
    parts_even[...] = jnp.zeros_like(parts_even)
    parts_odd[...] = jnp.zeros_like(parts_odd)

    def prepare(s, chunks, parts, weights, values):
        for c in range(16):
            spread(leg[s, :, c * 128 : (c + 1) * 128].astype(F32), c, chunks)
        for g in range(GROUPS):
            weights[g] = order_weights(group_rows(chunks, g), masks)
        rows = jnp.dot(coef[:, s].reshape(12 * 64, 128), perm, preferred_element_type=F32)
        for k in range(12):
            spread(rows[k * 64 : (k + 1) * 64], k, parts)
        for g in range(GROUPS):
            pieces = [piece for n in range(4) for piece in gather(parts, g * 4 + n)]
            values[g * 64 : (g + 1) * 64, :] = jnp.concatenate(pieces, axis=0).astype(BF16)

    def combine(s, weights, values):
        base = own_block(blocks_ref, s) * (GROUPS * 40)
        for g in range(GROUPS):
            term = jnp.dot(values[g * 64 : (g + 1) * 64, :], weights[g], preferred_element_type=F32)
            where = pl.ds(pl.multiple_of(base + g * 40, 8), 32)
            acc[where, :] = acc[where, :] + jnp.where(lower, term[:32], term[32:])

    def arrive(n):
        for copy in fetch(n):
            copy.wait()

    arrive(0)
    order.wait()
    prepare(0, chunks_even, parts_even, weights_even, values_even)

    def pair(t, carry):
        for n in range(1, len(BATCHES)):
            pl.when(2 * t + 1 == BATCHES[n][0])(functools.partial(arrive, n))
        prepare(2 * t + 1, chunks_odd, parts_odd, weights_odd, values_odd)
        combine(2 * t, weights_even, values_even)
        prepare(2 * t + 2, chunks_even, parts_even, weights_even, values_even)
        combine(2 * t + 1, weights_odd, values_odd)
        return carry

    lax.fori_loop(0, SLOTS // 2, pair, 0)
    combine(SLOTS - 1, weights_even, values_even)
    for comp in range(3):
        for i in range(2):
            parts = []
            for part in range(2):
                for vm in range(2):
                    row = i * 16 + part * 8 + vm * 3 + comp
                    parts.append(acc[pl.ds(row, 2 * GROUPS, stride=40), :])
            turned[comp * 2 + i] = jnp.concatenate(parts, axis=0).T
    for d in range(8):
        for j in range(4):
            pieces = [turned[n, pl.ds(j * 32 + d, 4, stride=8), :] for n in range(6)]
            out_ref[d, j] = jnp.concatenate(pieces, axis=0).astype(BF16)


def in_hbm(x):
    return pltpu.with_memory_space_constraint(x, pltpu.HBM)


def synthesis(m_blocks, coeffs, legendre):
    return pl.pallas_call(
        synth_kernel,
        in_specs=[pl.BlockSpec(memory_space=pltpu.HBM)] * 3,
        out_specs=pl.BlockSpec(memory_space=pltpu.VMEM),
        out_shape=jax.ShapeDtypeStruct((8, 4, 24, 128), BF16),
        scratch_shapes=[
            pltpu.SMEM((16,), jnp.int32),
            pltpu.SemaphoreType.DMA,
            pltpu.VMEM((12, SLOTS, 64, 128), BF16),
            pltpu.VMEM((SLOTS, 64, 2048), BF16),
            pltpu.SemaphoreType.DMA((len(BATCHES),)),
            pltpu.SemaphoreType.DMA((len(BATCHES),)),
            pltpu.VMEM((8 * PITCH, 128), F32),
            pltpu.VMEM((8 * PITCH, 128), F32),
            pltpu.VMEM((8 * PITCH, 128), F32),
            pltpu.VMEM((8 * PITCH, 128), F32),
            pltpu.VMEM((GROUPS, 128, 128), BF16),
            pltpu.VMEM((GROUPS, 128, 128), BF16),
            pltpu.VMEM((GROUPS * 64, 128), BF16),
            pltpu.VMEM((GROUPS * 64, 128), BF16),
            pltpu.VMEM((2 * GROUPS * 40, 128), F32),
            pltpu.VMEM((6, 128, 128), F32),
        ],
        compiler_params=pltpu.CompilerParams(vmem_limit_bytes=60 * 2**20),
        name="synthesis",
    )(in_hbm(m_blocks), in_hbm(coeffs), in_hbm(legendre))


def azimuth_kernel(blocks_ref, weights_ref, in_ref, table, out_ref, even_c, odd_c, even_s, odd_s, folded):
    lane_group = lax.broadcasted_iota(jnp.int32, (24, 128), 1) // 32
    left = []
    for j in range(4):
        halves = []
        for h in range(2):
            parts = [in_ref[h * 4 + s, j].astype(F32) * (1.0 / 32.0) for s in range(4)]
            halves.append(swap_lane_groups(parts, lane_group))
        both = [jnp.concatenate([halves[0][n], halves[1][n]], axis=1) for n in range(4)]
        left.append([jnp.concatenate([both[part * 2], both[part * 2 + 1]], axis=0).astype(BF16) for part in range(2)])
    starts = [pl.multiple_of(blocks_ref[p] * 16, 16) for p in range(16)]

    def basis(part, j):
        return jnp.concatenate([table[part, j, pl.ds(start, 16), :] for start in starts], axis=0)

    near, far = slice(0, EIGHTH), slice(EIGHTH, QUARTER)
    for part, ref in ((0, even_c), (1, even_s)):
        zero, two = (jnp.dot(left[j][part], basis(part, j), preferred_element_type=F32) for j in (0, 2))
        ref[:, near] = zero + two
        ref[:, far] = zero - two if part == 0 else two - zero
    both = [jnp.concatenate(left[j], axis=0) for j in (1, 3)]
    for part, here, there in ((0, odd_c, odd_s), (1, odd_s, odd_c)):
        one, three = (jnp.dot(both[n], basis(part, 2 * n + 1), preferred_element_type=F32) for n in range(2))
        here[:, near] = (one + three)[part * 48 : (part + 1) * 48]
        there[:, far] = (one - three)[(1 - part) * 48 : (2 - part) * 48]
    for x in range(QUARTER // 128):
        cols = slice(x * 128, (x + 1) * 128)
        fields = [[], [], [], []]
        for f in range(6):
            rows = slice(f * 8, (f + 1) * 8)
            ce, co, se, so = even_c[rows, cols], odd_c[rows, cols], even_s[rows, cols], odd_s[rows, cols]
            plus, minus = ce + co, ce - co
            total, other = se + so, se - so
            fields[0].append(plus - total)
            fields[1].append(plus + total)
            fields[2].append(minus + other)
            fields[3].append(minus - other)
        products = []
        for n in range(4):
            u0, u1, u2, b0, b1, b2 = fields[n]
            products.append(
                [
                    u1 * b2 - u2 * b1,
                    u2 * b0 - u0 * b2,
                    u0 * b1 - u1 * b0,
                    0.5 * (b0 * b0 + b1 * b1 + b2 * b2),
                ]
            )
        folds = [[], [], [], []]
        for g in range(4):
            p0, p1, p2, p3 = (products[n][g] for n in range(4))
            front, back = p0 + p1, p2 + p3
            left_odd, right_odd = p1 - p0, p2 - p3
            folds[0].append(front + back)
            folds[1].append(front - back)
            folds[2].append(left_odd + right_odd)
            folds[3].append(left_odd - right_odd)
        for n in range(4):
            folded[n, :, cols] = jnp.concatenate(folds[n], axis=0)
    row = lax.broadcasted_iota(jnp.int32, (8, 1), 0) % 4
    own = lax.axis_index("ma")
    weight = jnp.zeros((8, 1), F32)
    for t in range(4):
        weight = jnp.where(row == t, weights_ref[t * 8 + own], weight)
    lane_group = lax.broadcasted_iota(jnp.int32, (8, 128), 1) // 32
    def back(rows, part, j):
        return lax.dot_general(
            rows.astype(BF16), basis(part, j), (((1,), (1,)), ((), ())), preferred_element_type=F32
        )

    for j in range(4):
        c_near, c_far = folded[j % 2, :, near], folded[j % 2, :, far]
        s_near, s_far = folded[2 + j % 2, :, near], folded[2 + j % 2, :, far]
        if j == 0:
            terms = [back(c_near + c_far, 0, j), back(s_near - s_far, 1, j)]
        elif j == 2:
            terms = [back(c_near - c_far, 0, j), back(s_near + s_far, 1, j)]
        else:
            sign = 1.0 if j == 1 else -1.0
            total = back(jnp.concatenate([c_near, sign * s_far], axis=0), 0, j)
            total = total + back(jnp.concatenate([sign * c_far, s_near], axis=0), 1, j)
            terms = [total[:32], total[32:]]
        for gh in range(2):
            for h in range(2):
                parts = []
                for gl in range(2):
                    for part in range(2):
                        g = gh * 2 + gl
                        piece = terms[part][g * 8 : (g + 1) * 8, h * 128 : (h + 1) * 128]
                        parts.append((piece * (1.0 / math.sqrt(POINTS))) * weight)
                swapped = swap_lane_groups(parts, lane_group)
                for s in range(4):
                    where = (j * 2 + gh) * 8
                    out_ref[h * 4 + s, where : where + 8, :] = swapped[s].astype(BF16)


def azimuth(m_blocks, lat_weights, received, table):
    grid_shape = pltpu.VMEM((48, QUARTER), F32)
    return pl.pallas_call(
        azimuth_kernel,
        in_specs=[pl.BlockSpec(memory_space=pltpu.SMEM)] * 2 + [pl.BlockSpec(memory_space=pltpu.VMEM)] * 2,
        out_specs=pl.BlockSpec(memory_space=pltpu.VMEM),
        out_shape=jax.ShapeDtypeStruct((8, 64, 128), BF16),
        scratch_shapes=[
            grid_shape,
            grid_shape,
            grid_shape,
            grid_shape,
            pltpu.VMEM((4, 32, QUARTER), F32),
        ],
        compiler_params=pltpu.CompilerParams(vmem_limit_bytes=32 * 2**20),
        name="azimuth",
    )(m_blocks, lat_weights, received, table)


def turn_kernel(first, leg_hbm, out_hbm, leg, chunks, turned, sem_in, sem_out):
    count = turned.shape[0]

    def fetch(s):
        return pltpu.make_async_copy(leg_hbm.at[first + s], leg.at[s], sem_in.at[s])

    def leave(s):
        return pltpu.make_async_copy(turned.at[s], out_hbm.at[s], sem_out.at[s])

    def start(s, carry):
        fetch(s).start()
        return carry

    lax.fori_loop(0, count, start, 0)
    perm = lane_permutation(back=True)
    masks = lane_masks()

    def slot(s, carry):
        fetch(s).wait()
        for c in range(16):
            spread(leg[s, :, c * 128 : (c + 1) * 128].astype(F32), c, chunks)
        for g in range(0, GROUPS, 2):
            blocks = [block_weights(group_rows(chunks, g + n), masks, n) for n in range(2)]
            both = jnp.concatenate([one + two for one, two in zip(*blocks)], axis=0)
            both = lax.dot_general(both, perm, (((0,), (0,)), ((), ())), preferred_element_type=F32)
            for n in range(2):
                rows = [both[(u * 2 + n) * 32 : (u * 2 + n + 1) * 32, u * 128 : (u + 1) * 128] for u in range(2)]
                turned[s, g + n] = jnp.concatenate(rows, axis=0).astype(BF16)
        leave(s).start()
        return carry

    lax.fori_loop(0, count, slot, 0)

    def finish(s, carry):
        leave(s).wait()
        return carry

    lax.fori_loop(0, count, finish, 0)


def turn(legendre, first, count):
    shape = (count, GROUPS, 64, 128)
    return pl.pallas_call(
        functools.partial(turn_kernel, first),
        in_specs=[pl.BlockSpec(memory_space=pltpu.HBM)],
        out_specs=pl.BlockSpec(memory_space=pltpu.HBM),
        out_shape=pltpu.HBM(shape, BF16),
        scratch_shapes=[
            pltpu.VMEM((count, 64, 2048), BF16),
            pltpu.VMEM((8 * PITCH, 128), F32),
            pltpu.VMEM(shape, BF16),
            pltpu.SemaphoreType.DMA((count,)),
            pltpu.SemaphoreType.DMA((count,)),
        ],
        compiler_params=pltpu.CompilerParams(vmem_limit_bytes=60 * 2**20),
        cost_estimate=pl.CostEstimate(
            flops=2 * count * GROUPS * 128**3, bytes_accessed=4 * count * GROUPS * 128**2, transcendentals=0
        ),
        name="turn",
    )(in_hbm(legendre))


def analysis_kernel(blocks_hbm, *refs, count):
    messages = refs[:count]
    if count == 1:
        first_hbm, second_hbm, out_hbm, weights, blocks_ref, sem_b, sem_w, placed, turned, terms, out, sem_o = refs[1:]
    else:
        weights, out_hbm, blocks_ref, sem_b, placed, turned, terms, out, sem_o = refs[count:]
    order = pltpu.make_async_copy(blocks_hbm, blocks_ref, sem_b)
    order.start()
    if count == 1:
        split = first_hbm.shape[0]
        batches = ((first_hbm, 0, 0, 4), (first_hbm, 4, 4, split - 4), (second_hbm, 0, split, SLOTS - split))
    else:
        batches = ()

    def fetch(n):
        source, at, first, number = batches[n]
        return pltpu.make_async_copy(source.at[pl.ds(at, number)], weights.at[pl.ds(first, number)], sem_w.at[n])

    for n in range(len(batches)):
        fetch(n).start()
    for n, ref in enumerate(messages):
        for d in range(8):
            for j in range(4):
                for gh in range(2):
                    where = (j * 2 + gh) * 8
                    placed[n, pl.ds((gh * 4 + j) * 64 + d, 8, stride=8), :] = ref[d, where : where + 8, :].astype(F32)

    def pick(n, gh, j, i):
        return placed[n, (gh * 4 + j) * 64 + i * 32 : (gh * 4 + j) * 64 + (i + 1) * 32, :]

    row = lax.axis_index("row")
    has_low, has_high = row > 0, row < lax.axis_size("row") - 1

    def shells(gh, j):
        own = [pick(0, gh, j, i) for i in range(2)]
        if count == 1:
            return own
        low = [jnp.where(has_low, pick(1, gh, j, i), 0.0) for i in range(2)]
        high = [jnp.where(has_high, pick(2, gh, j, i), 0.0) for i in range(2)]
        return [
            (low[0] - 8.0 * low[1] + 8.0 * own[1] - high[0]) / 12.0,
            (low[1] - 8.0 * own[0] + 8.0 * high[0] - high[1]) / 12.0,
        ]

    for gh in range(2):
        columns = [shells(gh, j) for j in range(4)]
        for i in range(2):
            block = jnp.concatenate([columns[j][i] for j in range(4)], axis=0).T
            for quad in range(4):
                where = ((i * 2 + gh) * 4 + quad) * 40
                turned[where : where + 32, :] = block[quad * 32 : (quad + 1) * 32]
    lower = lax.broadcasted_iota(jnp.int32, (16, 128), 1) < 64
    terms[...] = jnp.zeros_like(terms)
    for qg in range(2 * GROUPS):
        both = turned[pl.ds(qg, 16, stride=40), :]
        halves = [jnp.where(lower, both, 0.0), jnp.where(lower, 0.0, both)]
        n = qg % 2
        terms[qg // 2, n * 32 : (n + 1) * 32, n * 128 : (n + 1) * 128] = jnp.concatenate(halves, axis=0).astype(BF16)

    def send(first, count):
        slots = pl.ds(first, count)
        return [pltpu.make_async_copy(out.at[i, slots], out_hbm.at[i, slots], sem_o.at[i]) for i in range(2)]

    def leave(first, count):
        for copy in send(first, count):
            copy.start()

    group = lax.broadcasted_iota(jnp.int32, (32, 128), 1) // 64
    halves = [(group == j).astype(F32).astype(BF16) for j in range(2)]

    def slot(s):
        base = own_block(blocks_ref, s) * (GROUPS // 2)
        for g in range(0, GROUPS, 2):
            blocks = [
                weights[s, g + n, u * 32 : (u + 1) * 32] * halves[j]
                for n in range(2) for u in range(2) for j in range(2)
            ]
            value = jnp.dot(terms[base + g // 2], jnp.concatenate(blocks, axis=0), preferred_element_type=F32)
            for n in range(2):
                part = [value[(n * 2 + u) * 16 : (n * 2 + u + 1) * 16] for u in range(2)]
                part = jnp.concatenate(part, axis=1).astype(BF16)
                for i in range(2):
                    out[i, s, :, (g + n) * 256 : (g + n + 1) * 256] = part[i * 8 : (i + 1) * 8]

    order.wait()

    def pair(t, carry):
        for n in range(len(batches)):
            need = batches[n][2] // 4
            pl.when(t == need)(lambda n=n: fetch(n).wait())
        slot(4 * t)
        slot(4 * t + 1)
        slot(4 * t + 2)
        slot(4 * t + 3)
        leave(4 * t, 4)
        return carry

    lax.fori_loop(0, SLOTS // 4, pair, 0)
    slot(SLOTS - 1)
    leave(SLOTS - 1, 1)
    for copy in send(0, SLOTS):
        copy.wait()


def analysis(name, m_blocks, messages, weights):
    vmem = pl.BlockSpec(memory_space=pltpu.VMEM)
    hbm = pl.BlockSpec(memory_space=pltpu.HBM)
    count = len(messages)
    plain = count == 1
    out_shape = pltpu.HBM((2, SLOTS, 8, 4096), BF16)
    shape = (SLOTS, GROUPS, 64, 128)
    return pl.pallas_call(
        functools.partial(analysis_kernel, count=count),
        in_specs=[hbm] + [vmem] * count + ([hbm, hbm] if plain else [vmem]),
        out_specs=[hbm, vmem] if plain else hbm,
        out_shape=[out_shape, pltpu.VMEM(shape, BF16)] if plain else out_shape,
        scratch_shapes=[
            pltpu.SMEM((16,), jnp.int32),
            pltpu.SemaphoreType.DMA,
            *([pltpu.SemaphoreType.DMA((3,))] if plain else []),
            pltpu.VMEM((count, 512, 128), F32),
            pltpu.VMEM((16 * 40, 128), F32),
            pltpu.VMEM((GROUPS, 64, 256), BF16),
            pltpu.VMEM((2, SLOTS, 8, 4096), BF16),
            pltpu.SemaphoreType.DMA((2,)),
        ],
        compiler_params=pltpu.CompilerParams(vmem_limit_bytes=24 * 2**20),
        cost_estimate=pl.CostEstimate(
            flops=2 * SLOTS * GROUPS * 32 * 128**2, bytes_accessed=12 * 2**20, transcendentals=0
        ),
        name=name,
    )(in_hbm(m_blocks), *messages, *(in_hbm(w) if plain else pltpu.with_memory_space_constraint(w, pltpu.VMEM) for w in weights))


def rows_of(coeffs):
    split = coeffs.reshape(2, 12, SLOTS, 32, 128)
    return split.transpose(1, 2, 3, 0, 4).reshape(12, SLOTS, 64, 128)


def local(coeffs, legendre, lat_weights, m_blocks):
    table = jnp.asarray(eighth_table(), BF16)
    sent = synthesis(m_blocks, rows_of(coeffs), legendre)
    sent, legendre = lax.optimization_barrier((sent, legendre))
    first = turn(legendre, 0, 9)
    received = lax.all_to_all(sent, "ma", split_axis=0, concat_axis=0, tiled=True)
    received, first, legendre = lax.optimization_barrier((received, first, legendre))
    sent_back = azimuth(m_blocks, lat_weights, received, table)
    sent_back, legendre = lax.optimization_barrier((sent_back, legendre))
    second = turn(legendre, 9, 8)
    own = lax.all_to_all(sent_back, "ma", split_axis=0, concat_axis=0, tiled=True)
    own, second = lax.optimization_barrier((own, second))
    count = lax.axis_size("row")
    low = lax.ppermute(own, "row", [(r, (r + 1) % count) for r in range(count)])
    high = lax.ppermute(own, "row", [((r + 1) % count, r) for r in range(count)])
    plain, kept = analysis("plain", m_blocks, [own], [first, second])
    slope = analysis("slope", m_blocks, [own, low, high], [kept])
    return plain.transpose(0, 2, 1, 3), slope.transpose(0, 2, 1, 3)


def solution(mesh):
    placed = (P("row", None, "ma", None), P("ma", None, None), P(), P())
    return jax.shard_map(
        local,
        mesh=mesh,
        in_specs=placed,
        out_specs=(P("row", None, "ma", None), P("row", None, "ma", None)),
        check_vma=False,
    )
```

```python
import functools
import math

import jax
import jax.numpy as jnp
import numpy as np
from jax import lax
from jax.experimental import pallas as pl
from jax.experimental.pallas import tpu as pltpu
from jax.sharding import PartitionSpec as P

F32, BF16 = jnp.float32, jnp.bfloat16
POINTS = 3072
QUARTER = POINTS // 4
EIGHTH = POINTS // 8
SLOTS = 17
GROUPS = 16
SPAN = 16
PITCH = 132
BATCHES = ((0, 1), (1, 2), (3, 2), (5, 4), (9, 8))


def lane_permutation(back=False):
    natural = lax.broadcasted_iota(jnp.int32, (128, 128), 1 if back else 0)
    grouped = lax.broadcasted_iota(jnp.int32, (128, 128), 0 if back else 1)
    c = natural % 64 // 4
    matrices = []
    for u in range(2):
        target = natural // 64 * 64 + (natural + 2 * u) % 4 * 16 + c % 2 * 8 + c // 2
        matrices.append((target == grouped).astype(F32).astype(BF16))
    return jnp.concatenate(matrices, axis=1)


def lane_masks():
    group = lax.broadcasted_iota(jnp.int32, (16, 128), 1) // 32
    return [(group == j).astype(F32).astype(BF16) for j in range(4)]


def eighth_table():
    j = np.arange(4)[:, None, None, None]
    b = np.arange(16)[None, :, None, None]
    g = np.arange(16)[None, None, :, None]
    x = np.arange(EIGHTH)[None, None, None, :]
    order = b * 64 + g * 4 + j
    turns = (order * (2 * x + 1)) % (2 * POINTS)
    angles = turns * (math.pi / POINTS)
    table = np.stack([np.cos(angles), np.sin(angles)])
    return table.reshape(2, 4, 256, EIGHTH)


def own_block(blocks_ref, s):
    lead = blocks_ref[2 * lax.axis_index("ma")]
    return (s >= SPAN - lead).astype(jnp.int32)


def spread(rows, n, scattered):
    scattered[pl.ds(n // 2 * PITCH + n % 2, 64, stride=2), :] = rows


def gather(scattered, row):
    return [scattered[pl.ds(2 * row + odd, 8, stride=PITCH), :] for odd in range(2)]


def group_rows(chunks, g):
    pieces = [piece for j in range(4) for piece in gather(chunks, g * 4 + j)]
    return jnp.concatenate(pieces, axis=0).astype(BF16)


def order_weights(rows, masks):
    rolled = [rows] + [pltpu.roll(rows, 32 * r, 1) for r in (1, 2, 3)]
    pieces = []
    for j in range(2):
        for a in range(4):
            pieces.append(
                rolled[(j - a) % 4][j * 16 : (j + 1) * 16] * masks[j]
                + rolled[(j + 2 - a) % 4][(j + 2) * 16 : (j + 3) * 16] * masks[j + 2]
            )
    return jnp.concatenate(pieces, axis=0)


def block_weights(rows, masks, place):
    blocks = []
    for j in range(2):
        for a in range(4):
            block = rows[j * 16 : (j + 1) * 16] * masks[a] + rows[(j + 2) * 16 : (j + 3) * 16] * masks[(a + 2) % 4]
            shift = (place - a) % 4
            blocks.append(pltpu.roll(block, 32 * shift, 1) if shift else block)
    return blocks


def swap_lane_groups(parts, lane_group):
    results = []
    for a in range(4):
        value = None
        for s in range(4):
            shift = (s - a) % 4
            moved = pltpu.roll(parts[s], 32 * shift, 1) if shift else parts[s]
            value = moved if value is None else jnp.where(lane_group == s, moved, value)
        results.append(value)
    return results


def synth_kernel(
    blocks_hbm, coef_hbm, leg_hbm, out_ref,
    blocks_ref, sem_b, coef, leg, sem_c, sem_l, chunks_even, chunks_odd, parts_even, parts_odd, weights_even, weights_odd, values_even, values_odd, acc, turned,
):
    def fetch(n):
        first, count = BATCHES[n]
        slots = pl.ds(first, count)
        return (
            pltpu.make_async_copy(leg_hbm.at[slots], leg.at[slots], sem_l.at[n]),
            pltpu.make_async_copy(coef_hbm.at[:, slots], coef.at[:, slots], sem_c.at[n]),
        )

    for n in range(len(BATCHES)):
        for copy in fetch(n):
            copy.start()
    order = pltpu.make_async_copy(blocks_hbm, blocks_ref, sem_b)
    order.start()
    acc[...] = jnp.zeros_like(acc)
    masks = lane_masks()
    perm = lane_permutation()[:, :128]
    lower = lax.broadcasted_iota(jnp.int32, (32, 128), 1) < 64
    parts_even[...] = jnp.zeros_like(parts_even)
    parts_odd[...] = jnp.zeros_like(parts_odd)

    def prepare(s, chunks, parts, weights, values):
        for c in range(16):
            spread(leg[s, :, c * 128 : (c + 1) * 128].astype(F32), c, chunks)
        for g in range(GROUPS):
            weights[g] = order_weights(group_rows(chunks, g), masks)
        rows = jnp.dot(coef[:, s].reshape(12 * 64, 128), perm, preferred_element_type=F32)
        for k in range(12):
            spread(rows[k * 64 : (k + 1) * 64], k, parts)
        for g in range(GROUPS):
            pieces = [piece for n in range(4) for piece in gather(parts, g * 4 + n)]
            values[g * 64 : (g + 1) * 64, :] = jnp.concatenate(pieces, axis=0).astype(BF16)

    def combine(s, weights, values):
        base = own_block(blocks_ref, s) * (GROUPS * 40)
        for g in range(GROUPS):
            term = jnp.dot(values[g * 64 : (g + 1) * 64, :], weights[g], preferred_element_type=F32)
            where = pl.ds(pl.multiple_of(base + g * 40, 8), 32)
            acc[where, :] = acc[where, :] + jnp.where(lower, term[:32], term[32:])

    def arrive(n):
        for copy in fetch(n):
            copy.wait()

    arrive(0)
    order.wait()
    prepare(0, chunks_even, parts_even, weights_even, values_even)

    def pair(t, carry):
        for n in range(1, len(BATCHES)):
            pl.when(2 * t + 1 == BATCHES[n][0])(functools.partial(arrive, n))
        prepare(2 * t + 1, chunks_odd, parts_odd, weights_odd, values_odd)
        combine(2 * t, weights_even, values_even)
        prepare(2 * t + 2, chunks_even, parts_even, weights_even, values_even)
        combine(2 * t + 1, weights_odd, values_odd)
        return carry

    lax.fori_loop(0, SLOTS // 2, pair, 0)
    combine(SLOTS - 1, weights_even, values_even)
    for comp in range(3):
        for i in range(2):
            parts = []
            for part in range(2):
                for vm in range(2):
                    row = i * 16 + part * 8 + vm * 3 + comp
                    parts.append(acc[pl.ds(row, 2 * GROUPS, stride=40), :])
            turned[comp * 2 + i] = jnp.concatenate(parts, axis=0).T
    for d in range(8):
        for j in range(4):
            pieces = [turned[n, pl.ds(j * 32 + d, 4, stride=8), :] for n in range(6)]
            out_ref[d, j] = jnp.concatenate(pieces, axis=0).astype(BF16)


def in_hbm(x):
    return pltpu.with_memory_space_constraint(x, pltpu.HBM)


def synthesis(m_blocks, coeffs, legendre):
    return pl.pallas_call(
        synth_kernel,
        in_specs=[pl.BlockSpec(memory_space=pltpu.HBM)] * 3,
        out_specs=pl.BlockSpec(memory_space=pltpu.VMEM),
        out_shape=jax.ShapeDtypeStruct((8, 4, 24, 128), BF16),
        scratch_shapes=[
            pltpu.SMEM((16,), jnp.int32),
            pltpu.SemaphoreType.DMA,
            pltpu.VMEM((12, SLOTS, 64, 128), BF16),
            pltpu.VMEM((SLOTS, 64, 2048), BF16),
            pltpu.SemaphoreType.DMA((len(BATCHES),)),
            pltpu.SemaphoreType.DMA((len(BATCHES),)),
            pltpu.VMEM((8 * PITCH, 128), F32),
            pltpu.VMEM((8 * PITCH, 128), F32),
            pltpu.VMEM((8 * PITCH, 128), F32),
            pltpu.VMEM((8 * PITCH, 128), F32),
            pltpu.VMEM((GROUPS, 128, 128), BF16),
            pltpu.VMEM((GROUPS, 128, 128), BF16),
            pltpu.VMEM((GROUPS * 64, 128), BF16),
            pltpu.VMEM((GROUPS * 64, 128), BF16),
            pltpu.VMEM((2 * GROUPS * 40, 128), F32),
            pltpu.VMEM((6, 128, 128), F32),
        ],
        compiler_params=pltpu.CompilerParams(vmem_limit_bytes=60 * 2**20),
        name="synthesis",
    )(in_hbm(m_blocks), in_hbm(coeffs), in_hbm(legendre))


def azimuth_kernel(blocks_ref, weights_ref, in_ref, table, out_ref, even_c, odd_c, even_s, odd_s, folded):
    lane_group = lax.broadcasted_iota(jnp.int32, (24, 128), 1) // 32
    left = []
    for j in range(4):
        halves = []
        for h in range(2):
            parts = [in_ref[h * 4 + s, j].astype(F32) * (1.0 / 32.0) for s in range(4)]
            halves.append(swap_lane_groups(parts, lane_group))
        both = [jnp.concatenate([halves[0][n], halves[1][n]], axis=1) for n in range(4)]
        left.append([jnp.concatenate([both[part * 2], both[part * 2 + 1]], axis=0).astype(BF16) for part in range(2)])
    starts = [pl.multiple_of(blocks_ref[p] * 16, 16) for p in range(16)]

    def basis(part, j):
        return jnp.concatenate([table[part, j, pl.ds(start, 16), :] for start in starts], axis=0)

    near, far = slice(0, EIGHTH), slice(EIGHTH, QUARTER)
    for part, ref in ((0, even_c), (1, even_s)):
        zero, two = (jnp.dot(left[j][part], basis(part, j), preferred_element_type=F32) for j in (0, 2))
        ref[:, near] = zero + two
        ref[:, far] = zero - two if part == 0 else two - zero
    both = [jnp.concatenate(left[j], axis=0) for j in (1, 3)]
    for part, here, there in ((0, odd_c, odd_s), (1, odd_s, odd_c)):
        one, three = (jnp.dot(both[n], basis(part, 2 * n + 1), preferred_element_type=F32) for n in range(2))
        here[:, near] = (one + three)[part * 48 : (part + 1) * 48]
        there[:, far] = (one - three)[(1 - part) * 48 : (2 - part) * 48]
    for x in range(QUARTER // 128):
        cols = slice(x * 128, (x + 1) * 128)
        fields = [[], [], [], []]
        for f in range(6):
            rows = slice(f * 8, (f + 1) * 8)
            ce, co, se, so = even_c[rows, cols], odd_c[rows, cols], even_s[rows, cols], odd_s[rows, cols]
            plus, minus = ce + co, ce - co
            total, other = se + so, se - so
            fields[0].append(plus - total)
            fields[1].append(plus + total)
            fields[2].append(minus + other)
            fields[3].append(minus - other)
        products = []
        for n in range(4):
            u0, u1, u2, b0, b1, b2 = fields[n]
            products.append(
                [
                    u1 * b2 - u2 * b1,
                    u2 * b0 - u0 * b2,
                    u0 * b1 - u1 * b0,
                    0.5 * (b0 * b0 + b1 * b1 + b2 * b2),
                ]
            )
        folds = [[], [], [], []]
        for g in range(4):
            p0, p1, p2, p3 = (products[n][g] for n in range(4))
            front, back = p0 + p1, p2 + p3
            left_odd, right_odd = p1 - p0, p2 - p3
            folds[0].append(front + back)
            folds[1].append(front - back)
            folds[2].append(left_odd + right_odd)
            folds[3].append(left_odd - right_odd)
        for n in range(4):
            folded[n, :, cols] = jnp.concatenate(folds[n], axis=0)
    row = lax.broadcasted_iota(jnp.int32, (8, 1), 0) % 4
    own = lax.axis_index("ma")
    weight = jnp.zeros((8, 1), F32)
    for t in range(4):
        weight = jnp.where(row == t, weights_ref[t * 8 + own], weight)
    lane_group = lax.broadcasted_iota(jnp.int32, (8, 128), 1) // 32
    def back(rows, part, j):
        return lax.dot_general(
            rows.astype(BF16), basis(part, j), (((1,), (1,)), ((), ())), preferred_element_type=F32
        )

    for j in range(4):
        c_near, c_far = folded[j % 2, :, near], folded[j % 2, :, far]
        s_near, s_far = folded[2 + j % 2, :, near], folded[2 + j % 2, :, far]
        if j == 0:
            terms = [back(c_near + c_far, 0, j), back(s_near - s_far, 1, j)]
        elif j == 2:
            terms = [back(c_near - c_far, 0, j), back(s_near + s_far, 1, j)]
        else:
            sign = 1.0 if j == 1 else -1.0
            total = back(jnp.concatenate([c_near, sign * s_far], axis=0), 0, j)
            total = total + back(jnp.concatenate([sign * c_far, s_near], axis=0), 1, j)
            terms = [total[:32], total[32:]]
        for gh in range(2):
            for h in range(2):
                parts = []
                for gl in range(2):
                    for part in range(2):
                        g = gh * 2 + gl
                        piece = terms[part][g * 8 : (g + 1) * 8, h * 128 : (h + 1) * 128]
                        parts.append((piece * (1.0 / math.sqrt(POINTS))) * weight)
                swapped = swap_lane_groups(parts, lane_group)
                for s in range(4):
                    where = (j * 2 + gh) * 8
                    out_ref[h * 4 + s, where : where + 8, :] = swapped[s].astype(BF16)


def azimuth(m_blocks, lat_weights, received, table):
    grid_shape = pltpu.VMEM((48, QUARTER), F32)
    return pl.pallas_call(
        azimuth_kernel,
        in_specs=[pl.BlockSpec(memory_space=pltpu.SMEM)] * 2 + [pl.BlockSpec(memory_space=pltpu.VMEM)] * 2,
        out_specs=pl.BlockSpec(memory_space=pltpu.VMEM),
        out_shape=jax.ShapeDtypeStruct((8, 64, 128), BF16),
        scratch_shapes=[
            grid_shape,
            grid_shape,
            grid_shape,
            grid_shape,
            pltpu.VMEM((4, 32, QUARTER), F32),
        ],
        compiler_params=pltpu.CompilerParams(vmem_limit_bytes=32 * 2**20),
        name="azimuth",
    )(m_blocks, lat_weights, received, table)


def turn_kernel(first, leg_hbm, out_hbm, leg, chunks, turned, sem_in, sem_out):
    count = turned.shape[0]

    def fetch(s):
        return pltpu.make_async_copy(leg_hbm.at[first + s], leg.at[s], sem_in.at[s])

    def leave(s):
        return pltpu.make_async_copy(turned.at[s], out_hbm.at[s], sem_out.at[s])

    def start(s, carry):
        fetch(s).start()
        return carry

    lax.fori_loop(0, count, start, 0)
    perm = lane_permutation(back=True)
    masks = lane_masks()

    def slot(s, carry):
        fetch(s).wait()
        for c in range(16):
            spread(leg[s, :, c * 128 : (c + 1) * 128].astype(F32), c, chunks)
        for g in range(0, GROUPS, 2):
            blocks = [block_weights(group_rows(chunks, g + n), masks, n) for n in range(2)]
            both = jnp.concatenate([one + two for one, two in zip(*blocks)], axis=0)
            both = lax.dot_general(both, perm, (((0,), (0,)), ((), ())), preferred_element_type=F32)
            for n in range(2):
                rows = [both[(u * 2 + n) * 32 : (u * 2 + n + 1) * 32, u * 128 : (u + 1) * 128] for u in range(2)]
                turned[s, g + n] = jnp.concatenate(rows, axis=0).astype(BF16)
        leave(s).start()
        return carry

    lax.fori_loop(0, count, slot, 0)

    def finish(s, carry):
        leave(s).wait()
        return carry

    lax.fori_loop(0, count, finish, 0)


def turn(legendre, first, count):
    shape = (count, GROUPS, 64, 128)
    return pl.pallas_call(
        functools.partial(turn_kernel, first),
        in_specs=[pl.BlockSpec(memory_space=pltpu.HBM)],
        out_specs=pl.BlockSpec(memory_space=pltpu.HBM),
        out_shape=pltpu.HBM(shape, BF16),
        scratch_shapes=[
            pltpu.VMEM((count, 64, 2048), BF16),
            pltpu.VMEM((8 * PITCH, 128), F32),
            pltpu.VMEM(shape, BF16),
            pltpu.SemaphoreType.DMA((count,)),
            pltpu.SemaphoreType.DMA((count,)),
        ],
        compiler_params=pltpu.CompilerParams(vmem_limit_bytes=60 * 2**20),
        cost_estimate=pl.CostEstimate(
            flops=2 * count * GROUPS * 128**3, bytes_accessed=4 * count * GROUPS * 128**2, transcendentals=0
        ),
        name="turn",
    )(in_hbm(legendre))


def analysis_kernel(blocks_hbm, *refs, count):
    messages = refs[:count]
    if count == 1:
        first_hbm, second_hbm, out_hbm, weights, blocks_ref, sem_b, sem_w, placed, turned, terms, out, sem_o = refs[1:]
    else:
        weights, out_hbm, blocks_ref, sem_b, placed, turned, terms, out, sem_o = refs[count:]
    order = pltpu.make_async_copy(blocks_hbm, blocks_ref, sem_b)
    order.start()
    if count == 1:
        split = first_hbm.shape[0]
        batches = ((first_hbm, 0, 0, 4), (first_hbm, 4, 4, split - 4), (second_hbm, 0, split, SLOTS - split))
    else:
        batches = ()

    def fetch(n):
        source, at, first, number = batches[n]
        return pltpu.make_async_copy(source.at[pl.ds(at, number)], weights.at[pl.ds(first, number)], sem_w.at[n])

    for n in range(len(batches)):
        fetch(n).start()
    for n, ref in enumerate(messages):
        for d in range(8):
            for j in range(4):
                for gh in range(2):
                    where = (j * 2 + gh) * 8
                    placed[n, pl.ds((gh * 4 + j) * 64 + d, 8, stride=8), :] = ref[d, where : where + 8, :].astype(F32)

    def pick(n, gh, j, i):
        return placed[n, (gh * 4 + j) * 64 + i * 32 : (gh * 4 + j) * 64 + (i + 1) * 32, :]

    row = lax.axis_index("row")
    has_low, has_high = row > 0, row < lax.axis_size("row") - 1

    def shells(gh, j):
        own = [pick(0, gh, j, i) for i in range(2)]
        if count == 1:
            return own
        low = [jnp.where(has_low, pick(1, gh, j, i), 0.0) for i in range(2)]
        high = [jnp.where(has_high, pick(2, gh, j, i), 0.0) for i in range(2)]
        return [
            (low[0] - 8.0 * low[1] + 8.0 * own[1] - high[0]) / 12.0,
            (low[1] - 8.0 * own[0] + 8.0 * high[0] - high[1]) / 12.0,
        ]

    for gh in range(2):
        columns = [shells(gh, j) for j in range(4)]
        for i in range(2):
            block = jnp.concatenate([columns[j][i] for j in range(4)], axis=0).T
            for quad in range(4):
                where = ((i * 2 + gh) * 4 + quad) * 40
                turned[where : where + 32, :] = block[quad * 32 : (quad + 1) * 32]
    lower = lax.broadcasted_iota(jnp.int32, (16, 128), 1) < 64
    terms[...] = jnp.zeros_like(terms)
    for qg in range(2 * GROUPS):
        both = turned[pl.ds(qg, 16, stride=40), :]
        halves = [jnp.where(lower, both, 0.0), jnp.where(lower, 0.0, both)]
        n = qg % 2
        terms[qg // 2, n * 32 : (n + 1) * 32, n * 128 : (n + 1) * 128] = jnp.concatenate(halves, axis=0).astype(BF16)

    def send(first, count):
        slots = pl.ds(first, count)
        return [pltpu.make_async_copy(out.at[i, slots], out_hbm.at[i, slots], sem_o.at[i]) for i in range(2)]

    def leave(first, count):
        for copy in send(first, count):
            copy.start()

    group = lax.broadcasted_iota(jnp.int32, (32, 128), 1) // 64
    halves = [(group == j).astype(F32).astype(BF16) for j in range(2)]

    def slot(s):
        base = own_block(blocks_ref, s) * (GROUPS // 2)
        for g in range(0, GROUPS, 2):
            blocks = [
                weights[s, g + n, u * 32 : (u + 1) * 32] * halves[j]
                for n in range(2) for u in range(2) for j in range(2)
            ]
            value = jnp.dot(terms[base + g // 2], jnp.concatenate(blocks, axis=0), preferred_element_type=F32)
            for n in range(2):
                part = [value[(n * 2 + u) * 16 : (n * 2 + u + 1) * 16] for u in range(2)]
                part = jnp.concatenate(part, axis=1).astype(BF16)
                for i in range(2):
                    out[i, s, :, (g + n) * 256 : (g + n + 1) * 256] = part[i * 8 : (i + 1) * 8]

    order.wait()

    def pair(t, carry):
        for n in range(len(batches)):
            need = batches[n][2] // 8
            pl.when(t == need)(lambda n=n: fetch(n).wait())
        for n in range(8):
            slot(8 * t + n)
            if n % 4 == 3:
                leave(8 * t + n - 3, 4)
        return carry

    lax.fori_loop(0, SLOTS // 8, pair, 0)
    slot(SLOTS - 1)
    leave(SLOTS - 1, 1)
    for copy in send(0, SLOTS):
        copy.wait()


def analysis(name, m_blocks, messages, weights):
    vmem = pl.BlockSpec(memory_space=pltpu.VMEM)
    hbm = pl.BlockSpec(memory_space=pltpu.HBM)
    count = len(messages)
    plain = count == 1
    out_shape = pltpu.HBM((2, SLOTS, 8, 4096), BF16)
    shape = (SLOTS, GROUPS, 64, 128)
    return pl.pallas_call(
        functools.partial(analysis_kernel, count=count),
        in_specs=[hbm] + [vmem] * count + ([hbm, hbm] if plain else [vmem]),
        out_specs=[hbm, vmem] if plain else hbm,
        out_shape=[out_shape, pltpu.VMEM(shape, BF16)] if plain else out_shape,
        scratch_shapes=[
            pltpu.SMEM((16,), jnp.int32),
            pltpu.SemaphoreType.DMA,
            *([pltpu.SemaphoreType.DMA((3,))] if plain else []),
            pltpu.VMEM((count, 512, 128), F32),
            pltpu.VMEM((16 * 40, 128), F32),
            pltpu.VMEM((GROUPS, 64, 256), BF16),
            pltpu.VMEM((2, SLOTS, 8, 4096), BF16),
            pltpu.SemaphoreType.DMA((2,)),
        ],
        compiler_params=pltpu.CompilerParams(vmem_limit_bytes=24 * 2**20),
        cost_estimate=pl.CostEstimate(
            flops=2 * SLOTS * GROUPS * 32 * 128**2, bytes_accessed=12 * 2**20, transcendentals=0
        ),
        name=name,
    )(in_hbm(m_blocks), *messages, *(in_hbm(w) if plain else pltpu.with_memory_space_constraint(w, pltpu.VMEM) for w in weights))


def rows_of(coeffs):
    split = coeffs.reshape(2, 12, SLOTS, 32, 128)
    return split.transpose(1, 2, 3, 0, 4).reshape(12, SLOTS, 64, 128)


def local(coeffs, legendre, lat_weights, m_blocks):
    table = jnp.asarray(eighth_table(), BF16)
    sent = synthesis(m_blocks, rows_of(coeffs), legendre)
    sent, legendre = lax.optimization_barrier((sent, legendre))
    first = turn(legendre, 0, 9)
    received = lax.all_to_all(sent, "ma", split_axis=0, concat_axis=0, tiled=True)
    received, first, legendre = lax.optimization_barrier((received, first, legendre))
    sent_back = azimuth(m_blocks, lat_weights, received, table)
    sent_back, legendre = lax.optimization_barrier((sent_back, legendre))
    second = turn(legendre, 9, 8)
    own = lax.all_to_all(sent_back, "ma", split_axis=0, concat_axis=0, tiled=True)
    own, second = lax.optimization_barrier((own, second))
    count = lax.axis_size("row")
    low = lax.ppermute(own, "row", [(r, (r + 1) % count) for r in range(count)])
    high = lax.ppermute(own, "row", [((r + 1) % count, r) for r in range(count)])
    plain, kept = analysis("plain", m_blocks, [own], [first, second])
    slope = analysis("slope", m_blocks, [own, low, high], [kept])
    return plain.transpose(0, 2, 1, 3), slope.transpose(0, 2, 1, 3)


def solution(mesh):
    placed = (P("row", None, "ma", None), P("ma", None, None), P(), P())
    return jax.shard_map(
        local,
        mesh=mesh,
        in_specs=placed,
        out_specs=(P("row", None, "ma", None), P("row", None, "ma", None)),
        check_vma=False,
    )
```
